256 devices in a mesh: pair: 64 (over z, x, core), occ: 4 (over y).
Axes of the slice: x: 4, y: 4, z: 8, core: 2. Of those that a mesh axis runs over, the one named last changes fastest.
Arguments:
- amplitudes: bfloat16 [256, 256, 128], P('pair', 'occ'), may hold values from -6 to 6
- vectors: bfloat16 [256, 5120, 128], P('pair', 'occ'), may hold values from -0.078125 to 0.078125
- pair_count: int32 [256], P('pair'), may hold values from 64 to 128
- tile_map: int32 [256, 32], replicated, may hold values from 0 to 255, as said below
Outputs:
- residual: bfloat16 [256, 256, 128], P('pair', 'occ')
The draws below stay inside these ranges and needn't reach their ends.
Inputs may be any that keep to these rules, and one draw needn't show every extreme that they name: `tile_map`: entries of a row are distinct. The rows of one index of pair (blocks d * 4 to (d + 1) * 4 - 1) name every block of that index and exactly one block of every other index of pair.
All inputs are finite; a program needn't handle non-finite values.
Results may differ from the reference program's by a relative error of at most 0.001.
Values may be sent and summed in bfloat16 or wider, within the bound.
A program may use at most 128 MiB of HBM per device.

```python
import jax
import jax.numpy as jnp
from jax import lax

TILE = 128
K = 5120
PB_DEV = 4
NPB = 256
NIJ = 256
NBR = 32


def draw_pair_count(key, part):
    key = jax.random.fold_in(key, 5)
    counts = jax.random.randint(key, (NPB,), TILE // 2, TILE + 1)
    first = jnp.arange(NPB) % PB_DEV == 0
    return jnp.where(first, TILE, counts).astype(jnp.int32)


def draw_tile_map(key, part):
    key = jax.random.fold_in(key, 11)
    npair = NPB // PB_DEV
    width = PB_DEV + npair - 1
    key_pick, key_perm = jax.random.split(key)
    device = jnp.arange(npair)[:, None]
    peers = (device + jnp.arange(1, npair)[None, :]) % npair
    picked = jax.random.randint(key_pick, (npair, npair - 1), 0, PB_DEV)
    remote = peers * PB_DEV + picked
    own = device * PB_DEV + jnp.arange(PB_DEV)[None, :]
    pool = jnp.concatenate([own, remote], axis=1)
    keys = jax.random.split(key_perm, npair)
    orders = jax.vmap(lambda single: jax.random.permutation(single, width))(keys)
    pool = jnp.take_along_axis(pool, orders, axis=1)
    place = (jnp.arange(PB_DEV)[:, None] * NBR + jnp.arange(NBR)[None, :]) % width
    rows = pool[:, place]
    return rows.reshape(NPB, NBR).astype(jnp.int32)


def steps_of(rng, dims, shards, smallest, largest):
    level = 1.0
    for dim, shards_of in shards:
        draws = jax.random.uniform(jax.random.fold_in(jax.random.fold_in(rng, 6), dim), (shards_of,), jnp.float32, smallest / len(shards), largest / len(shards))
        level = level * jnp.repeat(jnp.exp(draws), dims[dim] // shards_of).reshape((-1,) + (1,) * (len(dims) - 1 - dim))
    return level


def centred(stream_key, extent, spread, bound, shards=(), kind=jnp.bfloat16):
    entries = spread * jax.random.normal(stream_key, extent, jnp.float32)
    if shards:
        entries = entries * steps_of(stream_key, extent, shards, -0.22, 0.18)
    return jnp.clip(entries, -bound, bound).astype(kind)


def setup_inputs(seed: int = 0) -> dict:
    streams_of = jax.random.split(jax.random.key(seed), 5)
    return {
        "amplitudes": centred(streams_of[0], (NPB, NIJ, TILE), 1.0, 6.0, ((0, 64), (1, 4))),
        "vectors": centred(streams_of[1], (NPB, K, TILE), K ** -0.5, 0.078125, ((0, 64), (1, 4))),
        "pair_count": draw_pair_count(jax.random.fold_in(streams_of[4], 71), 0),
        "tile_map": draw_tile_map(jax.random.fold_in(streams_of[4], 71), 0),
    }


def reference(amplitudes, vectors, pair_count, tile_map):
    slots = lax.broadcasted_iota(jnp.int32, (NPB, 1, TILE), 2)
    live = slots < pair_count.astype(jnp.int32)[:, None, None]
    masked = jnp.where(live, vectors, jnp.zeros_like(vectors)).astype(jnp.bfloat16)

    def one_row(item):
        left, index = item
        partner_vec = jnp.take(masked, index, axis=0).astype(jnp.float32)
        tiles = jnp.einsum("ks,jkt->jst", left.astype(jnp.float32), partner_vec, precision=lax.Precision.HIGHEST)
        partner_amp = jnp.take(amplitudes, index, axis=0).astype(jnp.float32)
        total = jnp.einsum("jit,jst->is", partner_amp, tiles, precision=lax.Precision.HIGHEST)
        return total.astype(jnp.bfloat16)

    return lax.map(one_row, (masked, tile_map.astype(jnp.int32)))
```

```python
import jax
import jax.numpy as jnp
from jax import lax
from jax.sharding import Mesh, PartitionSpec as P

NZ, NX, NC, NY = 8, 4, 2, 4
ROWS = 16


def split(x):
    hi = lax.reduce_precision(x, 8, 7)
    return hi.astype(jnp.bfloat16), (x - hi).astype(jnp.bfloat16)


def body(amplitudes, vectors, pair_count, tile_map):
    blocks, occ, slots = amplitudes.shape
    total = tile_map.shape[0]
    live = lax.broadcasted_iota(jnp.int32, (blocks, 1, slots), 2) < pair_count[:, None, None]

    vec = lax.all_to_all(vectors, ("z", "c"), split_axis=1, concat_axis=0, tiled=True)
    rows = vec.shape[1]
    vec = vec.reshape(NZ, NC * blocks, rows, slots)
    vec = lax.all_gather(vec, "x", axis=1).reshape(total, rows, slots)

    amp = jnp.where(live, amplitudes, jnp.zeros_like(amplitudes))
    amp = lax.all_to_all(amp, "x", split_axis=1, concat_axis=0, tiled=True)
    amp = lax.all_gather(amp.reshape(NX, blocks, ROWS, slots), "y", axis=2)
    amp = lax.all_gather(amp, ("z", "c"), axis=0)
    amp = amp.reshape(NZ, NC, NX, blocks, NY * ROWS, slots)
    amp = amp.transpose(0, 2, 1, 3, 4, 5).reshape(total, NY * ROWS, slots)

    near = jnp.sum(tile_map[:, :, None] == jnp.arange(total)[None, None, :], axis=1).astype(jnp.bfloat16)
    w = jnp.einsum("qit,qkt->qik", amp, vec, preferred_element_type=jnp.float32)
    hi, lo = split(w)
    u = jnp.einsum("pq,qik->pik", near, hi, preferred_element_type=jnp.float32)
    u = u + jnp.einsum("pq,qik->pik", near, lo, preferred_element_type=jnp.float32)
    hi, lo = split(u)
    out = jnp.einsum("pik,pks->pis", hi, vec, preferred_element_type=jnp.float32)
    out = out + jnp.einsum("pik,pks->pis", lo, vec, preferred_element_type=jnp.float32)

    out = out.reshape(NZ, NX, NC, blocks, NY, ROWS, slots).transpose(4, 0, 2, 1, 3, 5, 6)
    out = lax.psum_scatter(out, "y", scatter_dimension=0)
    out = lax.psum_scatter(out.reshape((NZ * NC, NX) + out.shape[3:]), ("z", "c"), scatter_dimension=0)
    out = lax.all_to_all(out, "x", split_axis=0, concat_axis=0)
    out = out.transpose(1, 0, 2, 3).reshape(blocks, occ, slots)
    return jnp.where(live, out, 0.0).astype(jnp.bfloat16)


def solution(mesh):
    fine = Mesh(mesh.devices.reshape(NZ, NX, NC, NY), ("z", "x", "c", "y"))
    pair = ("z", "x", "c")
    return jax.shard_map(
        body,
        mesh=fine,
        in_specs=(P(pair, "y", None), P(pair, "y", None), P(pair), P()),
        out_specs=P(pair, "y", None),
        check_vma=False,
    )
```

```python
import jax
import jax.numpy as jnp
from jax import lax
from jax.experimental import pallas as pl
from jax.experimental.pallas import tpu as pltpu
from jax.sharding import Mesh, PartitionSpec as P

NZ, NX, NC, NY = 8, 4, 2, 4
BLOCKS = 4
GROUP = NX * NC * BLOCKS
TOTAL = NZ * GROUP
SLOTS = 128
DEPTH = 160
ROWS = 16
PITCH = TOTAL + 8
FIRST = 20
REST = GROUP - FIRST


def split(x):
    hi = x.astype(jnp.bfloat16)
    return hi, (x - hi.astype(jnp.float32)).astype(jnp.bfloat16)


def wait(view, sem):
    pltpu.make_async_copy(view, view, sem).wait()


def kernel(
    amp, vec, near, out,
    vb, ab, w, o, gzb, fzb, yhf, yff, yhg, yfg, fb, fr,
    vzs, vzr, xs, xr, ss, sr, axs, axr, azs, azr, ays, ayr,
    gzs, gzr, fzs, fzr, yhs, yhr, yfs, yfr, es, er,
):
    z, x, c, y = (lax.axis_index(a) for a in ("z", "x", "c", "y"))

    def mod(a, n):
        return lax.rem(a + 4 * n, n)

    def send(src, dst, ssem, rsem, z1=z, x1=x, c1=c, y1=y):
        pltpu.make_async_remote_copy(
            src_ref=src, dst_ref=dst, send_sem=ssem, recv_sem=rsem,
            device_id=(z1, x1, c1, y1), device_id_type=pl.DeviceIdType.MESH,
        ).start()

    zp, zm = mod(z + 1, NZ), mod(z - 1, NZ)
    xp, xm, xo = mod(x + 1, NX), mod(x - 1, NX), mod(x + 2, NX)
    yp, ym = mod(y + 1, NY), mod(y - 1, NY)
    mate = 1 - c
    home, edge = lax.div(y, 2), lax.rem(y, 2)
    active = c == home

    def mine(x0, c0):
        return pl.ds(pl.multiple_of(x0 * (NC * BLOCKS) + c0 * BLOCKS, BLOCKS), BLOCKS)

    def part(x0, c0, h):
        return pl.ds(x0 * (NC * BLOCKS) + c0 * BLOCKS + 2 * h, 2)

    def rows(z1):
        return pl.ds(pl.multiple_of(z1 * DEPTH, DEPTH), DEPTH)

    own = pltpu.make_async_copy(vec.at[:, rows(z), :], vb.at[z, mine(x, c)], vzr.at[z])
    own.start()
    barrier = pltpu.get_barrier_semaphore()

    def greet(z1=z, x1=x, c1=c, y1=y):
        pl.semaphore_signal(barrier, inc=1, device_id=(z1, x1, c1, y1), device_id_type=pl.DeviceIdType.MESH)

    for d in range(1, NZ):
        greet(z1=mod(z + d, NZ))
    for d in range(NX):
        for e in range(NC):
            if d or e:
                greet(x1=mod(x + d, NX), c1=mod(c + e, NC))
    for d in range(1, NY):
        greet(y1=mod(y + d, NY))
    pl.semaphore_wait(barrier, NZ - 1 + NX * NC - 1 + NY - 1)

    for d in range(NX):
        x1 = mod(x + d, NX)
        src = amp.at[:, pl.ds(pl.multiple_of(x1 * ROWS, ROWS), ROWS), :]
        dst = ab.at[edge, z, mine(x, c)]
        if d:
            send(src, dst, axs.at[d], axr.at[x, c], x1=x1, c1=home)
        else:

            @pl.when(active)
            def _():
                pltpu.make_async_copy(src, dst, axr.at[x, c]).start()

            @pl.when(c != home)
            def _():
                send(src, dst, axs.at[0], axr.at[x, c], c1=home)

    for d in (1, -1, 2, -2, 3, -3, 4):
        z1 = mod(z + d, NZ)
        send(vec.at[:, rows(z1), :], vb.at[z, mine(x, c)], vzs.at[z1], vzr.at[z], z1=z1)

    def source(s):
        return mod(z - jnp.where(lax.rem(s, 2) == 1, lax.div(s + 1, 2), -lax.div(s, 2)), NZ)

    def spread_amp(z0):
        for d in range(1, NY):
            send(ab.at[edge, z0], ab.at[edge, z0], ays.at[d - 1, z0], ayr.at[edge, z0], y1=mod(y + d, NY))

    def products(z0):
        for e in range(2):

            @pl.when(y != 2 * c + e)
            def _():
                wait(ab.at[e, z0], ayr.at[e, z0])

        def some(n, carry):
            for u in range(4):
                q = n * 4 + u
                a = jnp.concatenate([ab[0, z0, q], ab[1, z0, q]], axis=0)
                r = lax.dot_general(a, vb[z0, q], (((1,), (1,)), ((), ())), preferred_element_type=jnp.float32)
                w[0, pl.ds(z0 * GROUP + q, 2 * ROWS, stride=PITCH), :] = r[:, :SLOTS]
                w[1, pl.ds(z0 * GROUP + q, 2 * ROWS, stride=PITCH), : DEPTH - SLOTS] = r[:, SLOTS:]
            return carry

        lax.fori_loop(0, GROUP // 4, some, 0)

    def step(s, carry):
        @pl.when(s < NZ)
        def _():
            z0 = source(s)
            block = vb.at[z0, mine(x, c)]
            wait(block, vzr.at[z0])
            send(block, block, xs.at[0, z0], xr.at[0, z0], x1=xp)
            send(block, block, xs.at[1, z0], xr.at[1, z0], x1=xm)
            send(block, block, ss.at[0, z0], sr.at[0, z0], c1=mate)

        @pl.when(jnp.logical_and(s >= 1, s < NZ + 1))
        def _():
            z0 = source(s - 1)
            left, right = vb.at[z0, mine(xm, c)], vb.at[z0, mine(xp, c)]
            wait(left, xr.at[0, z0])
            half = vb.at[z0, part(xm, c, 0)]
            send(half, half, xs.at[2, z0], xr.at[2, z0], x1=xp)
            send(left, left, ss.at[1, z0], sr.at[1, z0], c1=mate)
            wait(right, xr.at[1, z0])
            half = vb.at[z0, part(xp, c, 1)]
            send(half, half, xs.at[3, z0], xr.at[3, z0], x1=xm)
            send(right, right, ss.at[2, z0], sr.at[2, z0], c1=mate)

        @pl.when(jnp.logical_and(s == 0, active))
        def _():
            for x0 in range(NX):
                for c0 in range(NC):
                    wait(ab.at[edge, z, mine(x0, c0)], axr.at[x0, c0])
            spread_amp(z)
            for d in (1, -1, 2, -2, 3, -3, 4):
                z1 = mod(z + d, NZ)
                send(ab.at[edge, z], ab.at[edge, z], azs.at[z1], azr.at[z], z1=z1)

        @pl.when(jnp.logical_and(jnp.logical_and(s >= 1, s < NZ), active))
        def _():
            z0 = source(s)
            wait(ab.at[edge, z0], azr.at[z0])
            spread_amp(z0)

        @pl.when(jnp.logical_and(s >= 2, s < NZ + 2))
        def _():
            z0 = source(s - 2)
            wait(vb.at[z0, part(xo, c, 0)], xr.at[2, z0])
            wait(vb.at[z0, part(xo, c, 1)], xr.at[3, z0])
            block = vb.at[z0, mine(xo, c)]
            send(block, block, ss.at[3, z0], sr.at[3, z0], c1=mate)

        @pl.when(s >= 3)
        def _():
            z0 = source(s - 3)
            for k, x0 in enumerate((x, xm, xp, xo)):
                wait(vb.at[z0, mine(x0, mate)], sr.at[k, z0])
            products(z0)

        return carry

    lax.fori_loop(0, NZ + 3, step, 0)

    def mix(i, carry):
        at = pl.ds(pl.multiple_of(i * PITCH, 8), TOTAL)
        for h in range(2):
            hi, lo = split(w[h, at, :])
            u = jnp.dot(near[...], hi, preferred_element_type=jnp.float32)
            w[h, at, :] = u + jnp.dot(near[...], lo, preferred_element_type=jnp.float32)
        return carry

    lax.fori_loop(0, 2 * ROWS, mix, 0)

    def residuals(zt):
        def some(n, carry):
            for u in range(4):
                p = n * 4 + u
                at = pl.ds(zt * GROUP + p, 2 * ROWS, stride=PITCH)
                hi0, lo0 = split(w[0, at, :])
                hi1, lo1 = split(w[1, at, :])
                left = jnp.concatenate([hi0, lo0], axis=0)
                right = jnp.concatenate([hi1, lo1], axis=0)[:, : DEPTH - SLOTS]
                r = jnp.dot(left, vb[zt, p, :SLOTS, :], preferred_element_type=jnp.float32)
                r = r + jnp.dot(right, vb[zt, p, SLOTS:, :], preferred_element_type=jnp.float32)
                r = r[: 2 * ROWS] + r[2 * ROWS :]
                o[0, zt, p] = r[:ROWS]
                o[1, zt, p] = r[ROWS:]
            return carry

        lax.fori_loop(0, GROUP // 4, some, 0)

    around = mod(y - 2 * c, NY)
    near_e, other_e = 1 - lax.rem(around, 2), lax.rem(around, 2)
    behind = jnp.logical_or(around == 0, around == 3)
    side = jnp.where(behind, 1, 0)
    onward = jnp.where(behind, yp, ym)

    def span(n):
        return (0, FIRST, yhf.at[n], yff.at[:, n]) if n < NZ else (FIRST, REST, yhg, yfg)

    def y1(n, zt):
        lo, size, hb, _ = span(n)

        @pl.when(jnp.logical_not(active))
        def _():
            send(o.at[other_e, zt, pl.ds(lo, size // 2)], hb, yhs.at[0, n], yhr.at[n], y1=ym)
            send(o.at[other_e, zt, pl.ds(lo + size // 2, size // 2)], hb, yhs.at[1, n], yhr.at[n], y1=yp)

    def y2(n, zt):
        lo, size, hb, fb_ = span(n)
        wait(hb, yhr.at[n])
        at = pl.ds(lo + side * (size // 2), size // 2)
        o[near_e, zt, at] = o[near_e, zt, at] + hb[...]
        send(o.at[near_e, zt, pl.ds(lo, size)], fb_.at[side], yfs.at[n], yfr.at[side, n], y1=onward)

    def y3(n, zt):
        lo, size, _, fb_ = span(n)

        @pl.when(active)
        def _():
            for k in range(2):
                wait(fb_.at[k], yfr.at[k, n])
            at = pl.ds(lo, size)
            o[other_e, zt, at] = o[other_e, zt, at] + (fb_[0] + fb_[1])

    def gview(zt, t, k):
        return o.at[pl.ds(k, 1), zt, pl.ds(FIRST, REST)] if t == 0 else o.at[:, zt, pl.ds(FIRST, REST)]

    def fview(zt, t, k):
        return o.at[other_e, zt, pl.ds(k * (FIRST // 2), FIRST // 2)] if t == 0 else o.at[other_e, zt, pl.ds(0, FIRST)]

    def gland(t, k):
        return gzb.at[k, t, pl.ds(0, 1)] if t == 0 else gzb.at[k, t]

    def fland(t, k):
        return fzb.at[k, t, pl.ds(0, FIRST // 2)] if t == 0 else fzb.at[k, t]

    def zsend(view, land, ssem, rsem, k, t):
        zt = mod(z + (4 - t), NZ) if k == 0 else mod(z - (4 - t), NZ)
        send(view(zt, t, k), land(t, k), ssem.at[k, t], rsem.at[k, t], z1=zp if k == 0 else zm)

    def zrecv(view, land, rsem, k, t):
        zt = mod(z + (3 - t), NZ) if k == 0 else mod(z - (3 - t), NZ)
        wait(land(t, k), rsem.at[k, t])
        into = view(zt, t, k)
        into[...] = into[...] + land(t, k)[...]

    def zwork(m, view, land, ssem, rsem):
        if m == 0:
            for k in range(2):
                zsend(view, land, ssem, rsem, k, 0)
        elif m < 7:
            k, t = (0, (m - 1) // 2) if m % 2 else (1, m // 2 - 1)
            zrecv(view, land, rsem, k, t)
            zsend(view, land, ssem, rsem, k, t + 1)
        else:
            for k in range(2):
                zrecv(view, land, rsem, k, 3)

    def g(m):
        zwork(m, gview, gland, gzs, gzr)

    def f(m):
        @pl.when(active)
        def _():
            zwork(m, fview, fland, fzs, fzr)

    order = [mod(z + d, NZ) for d in (4, 3, -3, 2, -2, 1, -1, 0)]
    for n in range(NZ):
        residuals(order[n])
        y1(n, order[n])
        if n >= 1:
            y2(n - 1, order[n - 1])
        if n < 7:
            g(n)
        if n >= 2:
            y3(n - 2, order[n - 2])
            f(n - 2)
    y2(7, z)
    y3(6, order[6])
    f(6)
    g(7)
    y1(8, z)
    y3(7, z)
    y2(8, z)
    f(7)
    y3(8, z)

    @pl.when(active)
    def _():
        fb[...] = o[other_e, z].astype(jnp.bfloat16)
        for d in range(NX):
            for e in range(NC):
                x1, c1 = mod(x + d, NX), mod(c + e, NC)
                src = fb.at[mine(x1, c1)]
                dst = fr.at[:, pl.ds(pl.multiple_of(x * ROWS, ROWS), ROWS), :]
                if d or e:
                    send(src, dst, es.at[2 * d + e], er.at[x], x1=x1, c1=c1)
                else:
                    pltpu.make_async_copy(src, dst, er.at[x]).start()

    for x0 in range(NX):
        wait(fr.at[:, pl.ds(x0 * ROWS, ROWS), :], er.at[x0])
    out[...] = fr[...]

    piece = amp.at[:, pl.ds(0, ROWS), :]
    for d in range(1, NX):
        wait(piece, axs.at[d])

    @pl.when(c != home)
    def _():
        wait(piece, axs.at[0])

    def sent(n, carry):
        z0 = mod(z + n, NZ)
        block, half = vb.at[z0, mine(x, c)], vb.at[z0, part(x, c, 0)]
        for k in range(2):
            wait(block, xs.at[k, z0])
            wait(half, xs.at[2 + k, z0])
        for k in range(4):
            wait(block, ss.at[k, z0])

        @pl.when(n > 0)
        def _():
            wait(block, vzs.at[z0])

        @pl.when(active)
        def _():
            for k in range(NY - 1):
                wait(ab.at[edge, z0], ays.at[k, z0])

            @pl.when(n > 0)
            def _():
                wait(ab.at[edge, z0], azs.at[z0])

        return carry

    lax.fori_loop(0, NZ, sent, 0)
    for n in range(NZ + 1):
        lo, size, hb, fb_ = span(n)

        @pl.when(jnp.logical_not(active))
        def _():
            wait(hb, yhs.at[0, n])
            wait(hb, yhs.at[1, n])

        wait(fb_.at[0], yfs.at[n])
    for k in range(2):
        for t in range(4):
            wait(gland(t, k), gzs.at[k, t])

    @pl.when(active)
    def _():
        for k in range(2):
            for t in range(4):
                wait(fland(t, k), fzs.at[k, t])
        for n in range(1, NX * NC):
            wait(fb.at[pl.ds(0, BLOCKS)], es.at[n])


def body(amplitudes, vectors, pair_count, tile_map):
    live = lax.broadcasted_iota(jnp.int32, (BLOCKS, 1, SLOTS), 2) < pair_count[:, None, None]
    amp = jnp.where(live, amplitudes, jnp.zeros_like(amplitudes))
    near = jnp.sum(tile_map[:, :, None] == jnp.arange(TOTAL)[None, None, :], axis=1).astype(jnp.bfloat16)
    f32, bf16 = jnp.float32, jnp.bfloat16
    dma = pltpu.SemaphoreType.DMA
    out = pl.pallas_call(
        kernel,
        out_shape=jax.ShapeDtypeStruct(amplitudes.shape, bf16),
        in_specs=[
            pl.BlockSpec(memory_space=pltpu.VMEM),
            pl.BlockSpec(memory_space=pl.ANY),
            pl.BlockSpec(memory_space=pltpu.VMEM),
        ],
        out_specs=pl.BlockSpec(memory_space=pltpu.VMEM),
        scratch_shapes=[
            pltpu.VMEM((NZ, GROUP, DEPTH, SLOTS), bf16),
            pltpu.VMEM((2, NZ, GROUP, ROWS, SLOTS), bf16),
            pltpu.VMEM((2, 2 * ROWS * PITCH, SLOTS), f32),
            pltpu.VMEM((2, NZ, GROUP, ROWS, SLOTS), f32),
            pltpu.VMEM((2, 4, 2, REST, ROWS, SLOTS), f32),
            pltpu.VMEM((2, 4, FIRST, ROWS, SLOTS), f32),
            pltpu.VMEM((NZ, FIRST // 2, ROWS, SLOTS), f32),
            pltpu.VMEM((2, NZ, FIRST, ROWS, SLOTS), f32),
            pltpu.VMEM((REST // 2, ROWS, SLOTS), f32),
            pltpu.VMEM((2, REST, ROWS, SLOTS), f32),
            pltpu.VMEM((GROUP, ROWS, SLOTS), bf16),
            pltpu.VMEM((BLOCKS, NX * ROWS, SLOTS), bf16),
            dma((NZ,)), dma((NZ,)),
            dma((4, NZ)), dma((4, NZ)),
            dma((4, NZ)), dma((4, NZ)),
            dma((NX,)), dma((NX, NC)),
            dma((NZ,)), dma((NZ,)),
            dma((NY - 1, NZ)), dma((2, NZ)),
            dma((2, 4)), dma((2, 4)),
            dma((2, 4)), dma((2, 4)),
            dma((2, NZ + 1)), dma((NZ + 1,)),
            dma((NZ + 1,)), dma((2, NZ + 1)),
            dma((NX * NC,)), dma((NX,)),
        ],
        compiler_params=pltpu.CompilerParams(
            collective_id=0, has_side_effects=True, vmem_limit_bytes=60 * 2**20
        ),
        cost_estimate=pl.CostEstimate(flops=12 * 10**9, bytes_accessed=4 * 10**6, transcendentals=0),
    )(amp, vectors, near)
    return jnp.where(live, out, jnp.zeros_like(out))


def solution(mesh):
    fine = Mesh(mesh.devices.reshape(NZ, NX, NC, NY), ("z", "x", "c", "y"))
    pair = ("z", "x", "c")
    return jax.shard_map(
        body,
        mesh=fine,
        in_specs=(P(pair, "y", None), P(pair, "y", None), P(pair), P()),
        out_specs=P(pair, "y", None),
        check_vma=False,
    )
```

```python
import jax
import jax.numpy as jnp
from jax import lax
from jax.experimental import pallas as pl
from jax.experimental.pallas import tpu as pltpu
from jax.sharding import Mesh, PartitionSpec as P

NZ, NX, NC, NY = 8, 4, 2, 4
BLOCKS = 4
GROUP = NX * NC * BLOCKS
TOTAL = NZ * GROUP
SLOTS = 128
DEPTH = 160
ROWS = 16
PITCH = TOTAL + 8
FOLD = SLOTS // (DEPTH - SLOTS)
FIRST = 20
REST = GROUP - FIRST


def split(x):
    hi = x.astype(jnp.bfloat16)
    return hi, (x - hi.astype(jnp.float32)).astype(jnp.bfloat16)


def wait(view, sem):
    pltpu.make_async_copy(view, view, sem).wait()


def kernel(
    amp_in, vec, counts, tiles, out,
    amp, near, vb, ab, w, wt, o, gzb, fzb, yhf, yff, yhg, yfg, fb, fr,
    vzs, vzr, xs, xr, ss, sr, axs, axr, azs, azr, ays, ayf, ayr,
    gzs, gzr, fzs, fzr, yhs, yhr, yfs, yfr, es, er,
):
    z, x, c, y = (lax.axis_index(a) for a in ("z", "x", "c", "y"))

    def mod(a, n):
        return lax.rem(a + 4 * n, n)

    def send(src, dst, ssem, rsem, z1=z, x1=x, c1=c, y1=y):
        pltpu.make_async_remote_copy(
            src_ref=src, dst_ref=dst, send_sem=ssem, recv_sem=rsem,
            device_id=(z1, x1, c1, y1), device_id_type=pl.DeviceIdType.MESH,
        ).start()

    zp, zm = mod(z + 1, NZ), mod(z - 1, NZ)
    xp, xm, xo = mod(x + 1, NX), mod(x - 1, NX), mod(x + 2, NX)
    yp, ym = mod(y + 1, NY), mod(y - 1, NY)
    mate = 1 - c
    home, edge = lax.div(y, 2), lax.rem(y, 2)
    active = c == home

    def mine(x0, c0):
        return pl.ds(pl.multiple_of(x0 * (NC * BLOCKS) + c0 * BLOCKS, BLOCKS), BLOCKS)

    def part(x0, c0, h):
        return pl.ds(x0 * (NC * BLOCKS) + c0 * BLOCKS + 2 * h, 2)

    def rows(z1):
        return pl.ds(pl.multiple_of(z1 * DEPTH, DEPTH), DEPTH)

    own = pltpu.make_async_copy(vec.at[:, rows(z), :], vb.at[z, mine(x, c)], vzr.at[z])
    own.start()
    barrier = pltpu.get_barrier_semaphore()
    slot = lax.broadcasted_iota(jnp.int32, (NX * ROWS, SLOTS), 1)

    def greet(z1=z, x1=x, c1=c, y1=y):
        pl.semaphore_signal(barrier, inc=1, device_id=(z1, x1, c1, y1), device_id_type=pl.DeviceIdType.MESH)

    for d in range(1, NZ):
        greet(z1=mod(z + d, NZ))
    for d in range(NX):
        for e in range(NC):
            if d or e:
                greet(x1=mod(x + d, NX), c1=mod(c + e, NC))
    for d in range(1, NY):
        greet(y1=mod(y + d, NY))
    for b in range(BLOCKS):
        amp[b] = jnp.where(slot < counts[b], amp_in[b], jnp.zeros_like(amp_in[b]))
    pl.semaphore_wait(barrier, NZ - 1 + NX * NC - 1 + NY - 1)

    for d in range(NX):
        x1 = mod(x + d, NX)
        src = amp.at[:, pl.ds(pl.multiple_of(x1 * ROWS, ROWS), ROWS), :]
        dst = ab.at[edge, z, mine(x, c)]
        if d:
            send(src, dst, axs.at[d], axr.at[x, c], x1=x1, c1=home)
        else:

            @pl.when(active)
            def _():
                pltpu.make_async_copy(src, dst, axr.at[x, c]).start()

            @pl.when(c != home)
            def _():
                send(src, dst, axs.at[0], axr.at[x, c], c1=home)

    for d in (1, -1, 2, -2, 3, -3, 4):
        z1 = mod(z + d, NZ)
        send(vec.at[:, rows(z1), :], vb.at[z, mine(x, c)], vzs.at[z1], vzr.at[z], z1=z1)

    def source(s):
        return mod(z - jnp.where(lax.rem(s, 2) == 1, lax.div(s + 1, 2), -lax.div(s, 2)), NZ)

    around = mod(y - 2 * c, NY)
    near_e, other_e = 1 - lax.rem(around, 2), lax.rem(around, 2)
    behind = jnp.logical_or(around == 0, around == 3)
    side = jnp.where(behind, 1, 0)
    onward, away = jnp.where(behind, yp, ym), jnp.where(behind, ym, yp)

    def amp_half(h):
        return pl.ds(pl.multiple_of(h * (GROUP // 2), GROUP // 2), GROUP // 2)

    def spread_amp(z0):
        block = ab.at[other_e, z0]
        send(block, block, ays.at[0, z0], ayr.at[0, z0], y1=yp)
        send(block, block, ays.at[1, z0], ayr.at[0, z0], y1=ym)

    def products(z0):
        @pl.when(jnp.logical_not(active))
        def _():
            for h in range(2):
                wait(ab.at[other_e, z0, amp_half(h)], ayr.at[1 + h, z0])

        def some(n, carry):
            for u in range(4):
                q = n * 4 + u
                a = jnp.concatenate([ab[0, z0, q], ab[1, z0, q]], axis=0)
                r = lax.dot_general(a, vb[z0, q], (((1,), (1,)), ((), ())), preferred_element_type=jnp.float32)
                w[pl.ds(z0 * GROUP + q, 2 * ROWS, stride=PITCH), :] = r[:, :SLOTS]
                tail = [r[m * 8 : m * 8 + 8, SLOTS:] for m in range(FOLD)]
                wt[pl.ds(z0 * GROUP + q, 8, stride=PITCH), :] = jnp.concatenate(tail, axis=1)
            return carry

        lax.fori_loop(0, GROUP // 4, some, 0)

    def adjacency(n, carry):
        at = pl.ds(pl.multiple_of(n * 32, 32), 32)
        named = tiles[at, :]
        block = lax.broadcasted_iota(jnp.int32, (32, TOTAL), 1)
        found = jnp.zeros((32, TOTAL), jnp.float32)
        for j in range(tiles.shape[1]):
            found = found + jnp.where(named[:, j : j + 1] == block, 1.0, 0.0)
        near[at, :TOTAL] = found.astype(jnp.bfloat16)
        near[at, TOTAL:] = found.astype(jnp.bfloat16)
        return carry

    lax.fori_loop(0, TOTAL // 32, adjacency, 0)

    def step(s, carry):
        @pl.when(s < NZ)
        def _():
            z0 = source(s)
            block = vb.at[z0, mine(x, c)]
            wait(block, vzr.at[z0])
            send(block, block, xs.at[0, z0], xr.at[0, z0], x1=xp)
            send(block, block, xs.at[1, z0], xr.at[1, z0], x1=xm)
            send(block, block, ss.at[0, z0], sr.at[0, z0], c1=mate)

        @pl.when(jnp.logical_and(s >= 1, s < NZ + 1))
        def _():
            z0 = source(s - 1)
            left, right = vb.at[z0, mine(xm, c)], vb.at[z0, mine(xp, c)]
            wait(left, xr.at[0, z0])
            half = vb.at[z0, part(xm, c, 0)]
            send(half, half, xs.at[2, z0], xr.at[2, z0], x1=xp)
            send(left, left, ss.at[1, z0], sr.at[1, z0], c1=mate)
            wait(right, xr.at[1, z0])
            half = vb.at[z0, part(xp, c, 1)]
            send(half, half, xs.at[3, z0], xr.at[3, z0], x1=xm)
            send(right, right, ss.at[2, z0], sr.at[2, z0], c1=mate)

        @pl.when(jnp.logical_and(s == 0, active))
        def _():
            for x0 in range(NX):
                for c0 in range(NC):
                    wait(ab.at[edge, z, mine(x0, c0)], axr.at[x0, c0])
            block = ab.at[edge, z]
            send(block, block, azs.at[z], azr.at[z], z1=zp)
            send(block, block, azs.at[NZ], azr.at[z], z1=zm)
            spread_amp(z)

        @pl.when(jnp.logical_and(jnp.logical_and(s >= 1, s < NZ), active))
        def _():
            z0 = source(s)
            block = ab.at[edge, z0]
            wait(block, azr.at[z0])

            @pl.when(s < NZ - 2)
            def _():
                send(block, block, azs.at[z0], azr.at[z0], z1=jnp.where(lax.rem(s, 2) == 1, zp, zm))

            spread_amp(z0)

        @pl.when(jnp.logical_and(s >= 1, s < NZ + 1))
        def _():
            z0 = source(s - 1)
            wait(ab.at[near_e, z0], ayr.at[0, z0])
            half = ab.at[near_e, z0, amp_half(side)]
            send(half, half, ayf.at[z0], ayr.at[1 + side, z0], y1=away)

        @pl.when(jnp.logical_and(s >= 2, s < NZ + 2))
        def _():
            z0 = source(s - 2)
            wait(vb.at[z0, part(xo, c, 0)], xr.at[2, z0])
            wait(vb.at[z0, part(xo, c, 1)], xr.at[3, z0])
            block = vb.at[z0, mine(xo, c)]
            send(block, block, ss.at[3, z0], sr.at[3, z0], c1=mate)

        @pl.when(s >= 3)
        def _():
            z0 = source(s - 3)
            for k, x0 in enumerate((x, xm, xp, xo)):
                wait(vb.at[z0, mine(x0, mate)], sr.at[k, z0])
            products(z0)

        return carry

    lax.fori_loop(0, NZ + 3, step, 0)

    def mix(ref):
        def some(i, carry):
            at = [pl.ds(pl.multiple_of((2 * i + h) * PITCH, 8), TOTAL) for h in range(2)]
            hi, lo = split(jnp.concatenate([ref[a, :] for a in at], axis=1))
            u = jnp.dot(near[...], jnp.concatenate([hi, lo], axis=0), preferred_element_type=jnp.float32)
            for h in range(2):
                ref[at[h], :] = u[:, h * SLOTS : (h + 1) * SLOTS]
            return carry

        lax.fori_loop(0, ref.shape[0] // PITCH // 2, some, 0)

    mix(w)
    mix(wt)
    row = lax.broadcasted_iota(jnp.int32, (2 * ROWS, SLOTS), 0)
    lane = lax.broadcasted_iota(jnp.int32, (2 * ROWS, SLOTS), 1)
    own_fold = lax.div(row, 8) == lax.div(lane, DEPTH - SLOTS)

    def residuals(zt):
        def some(n, carry):
            for u in range(4):
                p = n * 4 + u
                full = w[pl.ds(zt * GROUP + p, 2 * ROWS, stride=PITCH), :]
                tail = jnp.concatenate([wt[pl.ds(zt * GROUP + p, 8, stride=PITCH), :]] * FOLD, axis=0)
                u2 = jnp.concatenate([full, jnp.where(own_fold, tail, 0.0)], axis=1)
                left = jnp.concatenate(split(u2), axis=0)
                right = jnp.concatenate([vb[zt, p, :SLOTS, :]] + [vb[zt, p, SLOTS:, :]] * FOLD, axis=0)
                r = jnp.dot(left, right, preferred_element_type=jnp.float32)
                r = r[: 2 * ROWS] + r[2 * ROWS :]
                o[0, zt, p] = r[:ROWS]
                o[1, zt, p] = r[ROWS:]
            return carry

        lax.fori_loop(0, GROUP // 4, some, 0)

    def span(n):
        return (0, FIRST, yhf.at[n], yff.at[:, n]) if n < NZ else (FIRST, REST, yhg, yfg)

    def y1(n, zt):
        lo, size, hb, _ = span(n)

        @pl.when(jnp.logical_not(active))
        def _():
            send(o.at[other_e, zt, pl.ds(lo, size // 2)], hb, yhs.at[0, n], yhr.at[n], y1=ym)
            send(o.at[other_e, zt, pl.ds(lo + size // 2, size // 2)], hb, yhs.at[1, n], yhr.at[n], y1=yp)

    def y2(n, zt):
        lo, size, hb, fb_ = span(n)
        wait(hb, yhr.at[n])
        at = pl.ds(lo + side * (size // 2), size // 2)
        o[near_e, zt, at] = o[near_e, zt, at] + hb[...]
        send(o.at[near_e, zt, pl.ds(lo, size)], fb_.at[side], yfs.at[n], yfr.at[side, n], y1=onward)

    def y3(n, zt):
        lo, size, _, fb_ = span(n)

        @pl.when(active)
        def _():
            for k in range(2):
                wait(fb_.at[k], yfr.at[k, n])
            at = pl.ds(lo, size)
            o[other_e, zt, at] = o[other_e, zt, at] + (fb_[0] + fb_[1])

    def gview(zt, t, k):
        return o.at[pl.ds(k, 1), zt, pl.ds(FIRST, REST)] if t == 0 else o.at[:, zt, pl.ds(FIRST, REST)]

    def fview(zt, t, k):
        return o.at[other_e, zt, pl.ds(k * (FIRST // 2), FIRST // 2)] if t == 0 else o.at[other_e, zt, pl.ds(0, FIRST)]

    def gland(t, k):
        return gzb.at[k, t, pl.ds(0, 1)] if t == 0 else gzb.at[k, t]

    def fland(t, k):
        return fzb.at[k, t, pl.ds(0, FIRST // 2)] if t == 0 else fzb.at[k, t]

    def zsend(view, land, ssem, rsem, k, t):
        zt = mod(z + (4 - t), NZ) if k == 0 else mod(z - (4 - t), NZ)
        send(view(zt, t, k), land(t, k), ssem.at[k, t], rsem.at[k, t], z1=zp if k == 0 else zm)

    def zrecv(view, land, rsem, k, t):
        zt = mod(z + (3 - t), NZ) if k == 0 else mod(z - (3 - t), NZ)
        wait(land(t, k), rsem.at[k, t])
        into = view(zt, t, k)
        into[...] = into[...] + land(t, k)[...]

    def zwork(m, view, land, ssem, rsem):
        if m == 0:
            for k in range(2):
                zsend(view, land, ssem, rsem, k, 0)
        elif m < 7:
            k, t = (0, (m - 1) // 2) if m % 2 else (1, m // 2 - 1)
            zrecv(view, land, rsem, k, t)
            zsend(view, land, ssem, rsem, k, t + 1)
        else:
            for k in range(2):
                zrecv(view, land, rsem, k, 3)

    def g(m):
        zwork(m, gview, gland, gzs, gzr)

    def f(m):
        @pl.when(active)
        def _():
            zwork(m, fview, fland, fzs, fzr)

    order = [mod(z + d, NZ) for d in (4, 3, -3, 2, -2, 1, -1, 0)]
    for n in range(NZ):
        residuals(order[n])
        y1(n, order[n])
        if n >= 1:
            y2(n - 1, order[n - 1])
        if n < 7:
            g(n)
        if n >= 2:
            y3(n - 2, order[n - 2])
            f(n - 2)
    y2(7, z)
    y3(6, order[6])
    f(6)
    g(7)
    y1(8, z)
    y3(7, z)
    y2(8, z)
    f(7)
    y3(8, z)

    @pl.when(active)
    def _():
        fb[...] = o[other_e, z].astype(jnp.bfloat16)
        for d in range(NX):
            for e in range(NC):
                x1, c1 = mod(x + d, NX), mod(c + e, NC)
                src = fb.at[mine(x1, c1)]
                dst = fr.at[:, pl.ds(pl.multiple_of(x * ROWS, ROWS), ROWS), :]
                if d or e:
                    send(src, dst, es.at[2 * d + e], er.at[x], x1=x1, c1=c1)
                else:
                    pltpu.make_async_copy(src, dst, er.at[x]).start()

    for x0 in range(NX):
        wait(fr.at[:, pl.ds(x0 * ROWS, ROWS), :], er.at[x0])
    out[...] = fr[...]

    piece = amp.at[:, pl.ds(0, ROWS), :]
    for d in range(1, NX):
        wait(piece, axs.at[d])

    @pl.when(c != home)
    def _():
        wait(piece, axs.at[0])

    def sent(n, carry):
        z0 = mod(z + n, NZ)
        block, half = vb.at[z0, mine(x, c)], vb.at[z0, part(x, c, 0)]
        for k in range(2):
            wait(block, xs.at[k, z0])
            wait(half, xs.at[2 + k, z0])
        for k in range(4):
            wait(block, ss.at[k, z0])

        @pl.when(n > 0)
        def _():
            wait(block, vzs.at[z0])

        wait(ab.at[edge, z0, amp_half(0)], ayf.at[z0])

        @pl.when(active)
        def _():
            for k in range(2):
                wait(ab.at[edge, z0], ays.at[k, z0])

        return carry

    lax.fori_loop(0, NZ, sent, 0)

    @pl.when(active)
    def _():
        wait(ab.at[edge, z], azs.at[NZ])
        for d in (0, 1, -1, 2, -2, 3):
            wait(ab.at[edge, z], azs.at[mod(z - d, NZ)])

    for n in range(NZ + 1):
        lo, size, hb, fb_ = span(n)

        @pl.when(jnp.logical_not(active))
        def _():
            wait(hb, yhs.at[0, n])
            wait(hb, yhs.at[1, n])

        wait(fb_.at[0], yfs.at[n])
    for k in range(2):
        for t in range(4):
            wait(gland(t, k), gzs.at[k, t])

    @pl.when(active)
    def _():
        for k in range(2):
            for t in range(4):
                wait(fland(t, k), fzs.at[k, t])
        for n in range(1, NX * NC):
            wait(fb.at[pl.ds(0, BLOCKS)], es.at[n])


def body(amplitudes, vectors, pair_count, tile_map):
    live = lax.broadcasted_iota(jnp.int32, (BLOCKS, 1, SLOTS), 2) < pair_count[:, None, None]
    f32, bf16 = jnp.float32, jnp.bfloat16
    dma = pltpu.SemaphoreType.DMA
    out = pl.pallas_call(
        kernel,
        out_shape=jax.ShapeDtypeStruct(amplitudes.shape, bf16),
        in_specs=[
            pl.BlockSpec(memory_space=pltpu.VMEM),
            pl.BlockSpec(memory_space=pl.ANY),
            pl.BlockSpec(memory_space=pltpu.SMEM),
            pl.BlockSpec(memory_space=pltpu.VMEM),
        ],
        out_specs=pl.BlockSpec(memory_space=pltpu.VMEM),
        scratch_shapes=[
            pltpu.VMEM(amplitudes.shape, bf16),
            pltpu.VMEM((TOTAL, 2 * TOTAL), bf16),
            pltpu.VMEM((NZ, GROUP, DEPTH, SLOTS), bf16),
            pltpu.VMEM((2, NZ, GROUP, ROWS, SLOTS), bf16),
            pltpu.VMEM((2 * ROWS * PITCH, SLOTS), f32),
            pltpu.VMEM((8 * PITCH, SLOTS), f32),
            pltpu.VMEM((2, NZ, GROUP, ROWS, SLOTS), f32),
            pltpu.VMEM((2, 4, 2, REST, ROWS, SLOTS), f32),
            pltpu.VMEM((2, 4, FIRST, ROWS, SLOTS), f32),
            pltpu.VMEM((NZ, FIRST // 2, ROWS, SLOTS), f32),
            pltpu.VMEM((2, NZ, FIRST, ROWS, SLOTS), f32),
            pltpu.VMEM((REST // 2, ROWS, SLOTS), f32),
            pltpu.VMEM((2, REST, ROWS, SLOTS), f32),
            pltpu.VMEM((GROUP, ROWS, SLOTS), bf16),
            pltpu.VMEM((BLOCKS, NX * ROWS, SLOTS), bf16),
            dma((NZ,)), dma((NZ,)),
            dma((4, NZ)), dma((4, NZ)),
            dma((4, NZ)), dma((4, NZ)),
            dma((NX,)), dma((NX, NC)),
            dma((NZ + 1,)), dma((NZ,)),
            dma((2, NZ)), dma((NZ,)), dma((3, NZ)),
            dma((2, 4)), dma((2, 4)),
            dma((2, 4)), dma((2, 4)),
            dma((2, NZ + 1)), dma((NZ + 1,)),
            dma((NZ + 1,)), dma((2, NZ + 1)),
            dma((NX * NC,)), dma((NX,)),
        ],
        compiler_params=pltpu.CompilerParams(
            collective_id=0, has_side_effects=True, vmem_limit_bytes=60 * 2**20
        ),
        cost_estimate=pl.CostEstimate(flops=12 * 10**9, bytes_accessed=4 * 10**6, transcendentals=0),
    )(amplitudes, vectors, pair_count, tile_map)
    return jnp.where(live, out, jnp.zeros_like(out))


def solution(mesh):
    fine = Mesh(mesh.devices.reshape(NZ, NX, NC, NY), ("z", "x", "c", "y"))
    pair = ("z", "x", "c")
    return jax.shard_map(
        body,
        mesh=fine,
        in_specs=(P(pair, "y", None), P(pair, "y", None), P(pair), P()),
        out_specs=P(pair, "y", None),
        check_vma=False,
    )
```

```python
import jax
import jax.numpy as jnp
from jax import lax
from jax.experimental import pallas as pl
from jax.experimental.pallas import tpu as pltpu
from jax.sharding import Mesh, PartitionSpec as P

NZ, NX, NC, NY = 8, 4, 2, 4
BLOCKS = 4
GROUP = NX * NC * BLOCKS
TOTAL = NZ * GROUP
SLOTS = 128
DEPTH = 160
ROWS = 16
PITCH = TOTAL + 8
FOLD = SLOTS // (DEPTH - SLOTS)
AHEAD = 3
FIRST = 20
REST = GROUP - FIRST


def split(x):
    hi = x.astype(jnp.bfloat16)
    return hi, (x - hi.astype(jnp.float32)).astype(jnp.bfloat16)


def wait(view, sem):
    pltpu.make_async_copy(view, view, sem).wait()


def kernel(
    amp_in, vec, counts, tiles, out,
    amp, near, vb, ab, w, wt, o, gzb, fzb, yhf, yff, yhg, yfg, fb, fr,
    vzs, vzr, xs, xr, ss, sr, axs, axr, azs, azr, ays, ayf, ayr,
    gzs, gzr, fzs, fzr, yhs, yhr, yfs, yfr, es, er,
):
    z, x, c, y = (lax.axis_index(a) for a in ("z", "x", "c", "y"))

    def mod(a, n):
        return lax.rem(a + 4 * n, n)

    def send(src, dst, ssem, rsem, z1=z, x1=x, c1=c, y1=y):
        pltpu.make_async_remote_copy(
            src_ref=src, dst_ref=dst, send_sem=ssem, recv_sem=rsem,
            device_id=(z1, x1, c1, y1), device_id_type=pl.DeviceIdType.MESH,
        ).start()

    zp, zm = mod(z + 1, NZ), mod(z - 1, NZ)
    xp, xm, xo = mod(x + 1, NX), mod(x - 1, NX), mod(x + 2, NX)
    yp, ym = mod(y + 1, NY), mod(y - 1, NY)
    mate = 1 - c
    home, edge = lax.div(y, 2), lax.rem(y, 2)
    active = c == home

    def mine(x0, c0):
        return pl.ds(pl.multiple_of(x0 * (NC * BLOCKS) + c0 * BLOCKS, BLOCKS), BLOCKS)

    def part(x0, c0, h):
        return pl.ds(x0 * (NC * BLOCKS) + c0 * BLOCKS + 2 * h, 2)

    def rows(z1):
        return pl.ds(pl.multiple_of(z1 * DEPTH, DEPTH), DEPTH)

    own = pltpu.make_async_copy(vec.at[:, rows(z), :], vb.at[z, mine(x, c)], vzr.at[z])
    own.start()
    barrier = pltpu.get_barrier_semaphore()
    slot = lax.broadcasted_iota(jnp.int32, (NX * ROWS, SLOTS), 1)

    def greet(z1=z, x1=x, c1=c, y1=y):
        pl.semaphore_signal(barrier, inc=1, device_id=(z1, x1, c1, y1), device_id_type=pl.DeviceIdType.MESH)

    for d in range(1, NZ):
        greet(z1=mod(z + d, NZ))
    for d in range(NX):
        for e in range(NC):
            if d or e:
                greet(x1=mod(x + d, NX), c1=mod(c + e, NC))
    for d in range(1, NY):
        greet(y1=mod(y + d, NY))
    for b in range(BLOCKS):
        amp[b] = jnp.where(slot < counts[b], amp_in[b], jnp.zeros_like(amp_in[b]))
    pl.semaphore_wait(barrier, NZ - 1 + NX * NC - 1 + NY - 1)

    for d in range(NX):
        x1 = mod(x + d, NX)
        src = amp.at[:, pl.ds(pl.multiple_of(x1 * ROWS, ROWS), ROWS), :]
        dst = ab.at[edge, z, mine(x, c)]
        if d:
            send(src, dst, axs.at[d], axr.at[x, c], x1=x1, c1=home)
        else:

            @pl.when(active)
            def _():
                pltpu.make_async_copy(src, dst, axr.at[x, c]).start()

            @pl.when(c != home)
            def _():
                send(src, dst, axs.at[0], axr.at[x, c], c1=home)

    def away_from(s):
        return jnp.where(lax.rem(s, 2) == 1, lax.div(s + 1, 2), -lax.div(s, 2))

    def hand_out(s):
        z1 = mod(z + away_from(s), NZ)
        send(vec.at[:, rows(z1), :], vb.at[z, mine(x, c)], vzs.at[z1], vzr.at[z], z1=z1)

    for s in range(1, AHEAD):
        hand_out(jnp.int32(s))

    def source(s):
        return mod(z - away_from(s), NZ)

    around = mod(y - 2 * c, NY)
    near_e, other_e = 1 - lax.rem(around, 2), lax.rem(around, 2)
    behind = jnp.logical_or(around == 0, around == 3)
    side = jnp.where(behind, 1, 0)
    onward, away = jnp.where(behind, yp, ym), jnp.where(behind, ym, yp)

    def amp_half(h):
        return pl.ds(pl.multiple_of(h * (GROUP // 2), GROUP // 2), GROUP // 2)

    def spread_amp(z0):
        block = ab.at[other_e, z0]
        send(block, block, ays.at[0, z0], ayr.at[0, z0], y1=yp)
        send(block, block, ays.at[1, z0], ayr.at[0, z0], y1=ym)

    def products(z0):
        @pl.when(jnp.logical_not(active))
        def _():
            for h in range(2):
                wait(ab.at[other_e, z0, amp_half(h)], ayr.at[1 + h, z0])

        def some(n, carry):
            for u in range(4):
                q = n * 4 + u
                a = jnp.concatenate([ab[0, z0, q], ab[1, z0, q]], axis=0)
                r = lax.dot_general(a, vb[z0, q], (((1,), (1,)), ((), ())), preferred_element_type=jnp.float32)
                w[pl.ds(z0 * GROUP + q, 2 * ROWS, stride=PITCH), :] = r[:, :SLOTS]
                tail = [r[m * 8 : m * 8 + 8, SLOTS:] for m in range(FOLD)]
                wt[pl.ds(z0 * GROUP + q, 8, stride=PITCH), :] = jnp.concatenate(tail, axis=1)
            return carry

        lax.fori_loop(0, GROUP // 4, some, 0)

    def adjacency(n, carry):
        at = pl.ds(pl.multiple_of(n * 32, 32), 32)
        named = tiles[at, :]
        block = lax.broadcasted_iota(jnp.int32, (32, TOTAL), 1)
        found = jnp.zeros((32, TOTAL), jnp.float32)
        for j in range(tiles.shape[1]):
            found = found + jnp.where(named[:, j : j + 1] == block, 1.0, 0.0)
        near[at, :TOTAL] = found.astype(jnp.bfloat16)
        near[at, TOTAL:] = found.astype(jnp.bfloat16)
        return carry

    lax.fori_loop(0, TOTAL // 32, adjacency, 0)

    def step(s, carry):
        @pl.when(s < NZ)
        def _():
            z0 = source(s)
            block = vb.at[z0, mine(x, c)]
            wait(block, vzr.at[z0])

            @pl.when(s < NZ - AHEAD)
            def _():
                hand_out(s + AHEAD)

            send(block, block, xs.at[0, z0], xr.at[0, z0], x1=xp)
            send(block, block, xs.at[1, z0], xr.at[1, z0], x1=xm)
            send(block, block, ss.at[0, z0], sr.at[0, z0], c1=mate)

        @pl.when(jnp.logical_and(s >= 1, s < NZ + 1))
        def _():
            z0 = source(s - 1)
            left, right = vb.at[z0, mine(xm, c)], vb.at[z0, mine(xp, c)]
            wait(left, xr.at[0, z0])
            half = vb.at[z0, part(xm, c, 0)]
            send(half, half, xs.at[2, z0], xr.at[2, z0], x1=xp)
            send(left, left, ss.at[1, z0], sr.at[1, z0], c1=mate)
            wait(right, xr.at[1, z0])
            half = vb.at[z0, part(xp, c, 1)]
            send(half, half, xs.at[3, z0], xr.at[3, z0], x1=xm)
            send(right, right, ss.at[2, z0], sr.at[2, z0], c1=mate)

        @pl.when(jnp.logical_and(s == 0, active))
        def _():
            for x0 in range(NX):
                for c0 in range(NC):
                    wait(ab.at[edge, z, mine(x0, c0)], axr.at[x0, c0])
            block = ab.at[edge, z]
            send(block, block, azs.at[z], azr.at[z], z1=zp)
            send(block, block, azs.at[NZ], azr.at[z], z1=zm)
            spread_amp(z)

        @pl.when(jnp.logical_and(jnp.logical_and(s >= 1, s < NZ), active))
        def _():
            z0 = source(s)
            block = ab.at[edge, z0]
            wait(block, azr.at[z0])

            @pl.when(s < NZ - 2)
            def _():
                send(block, block, azs.at[z0], azr.at[z0], z1=jnp.where(lax.rem(s, 2) == 1, zp, zm))

            spread_amp(z0)

        @pl.when(jnp.logical_and(s >= 1, s < NZ + 1))
        def _():
            z0 = source(s - 1)
            wait(ab.at[near_e, z0], ayr.at[0, z0])
            half = ab.at[near_e, z0, amp_half(side)]
            send(half, half, ayf.at[z0], ayr.at[1 + side, z0], y1=away)

        @pl.when(jnp.logical_and(s >= 2, s < NZ + 2))
        def _():
            z0 = source(s - 2)
            wait(vb.at[z0, part(xo, c, 0)], xr.at[2, z0])
            wait(vb.at[z0, part(xo, c, 1)], xr.at[3, z0])
            block = vb.at[z0, mine(xo, c)]
            send(block, block, ss.at[3, z0], sr.at[3, z0], c1=mate)

        @pl.when(s >= 3)
        def _():
            z0 = source(s - 3)
            for k, x0 in enumerate((x, xm, xp, xo)):
                wait(vb.at[z0, mine(x0, mate)], sr.at[k, z0])
            products(z0)

        return carry

    lax.fori_loop(0, NZ + 3, step, 0)

    def mix(ref):
        def some(i, carry):
            at = [pl.ds(pl.multiple_of((2 * i + h) * PITCH, 8), TOTAL) for h in range(2)]
            hi, lo = split(jnp.concatenate([ref[a, :] for a in at], axis=1))
            u = jnp.dot(near[...], jnp.concatenate([hi, lo], axis=0), preferred_element_type=jnp.float32)
            for h in range(2):
                ref[at[h], :] = u[:, h * SLOTS : (h + 1) * SLOTS]
            return carry

        lax.fori_loop(0, ref.shape[0] // PITCH // 2, some, 0)

    mix(w)
    mix(wt)
    row = lax.broadcasted_iota(jnp.int32, (2 * ROWS, SLOTS), 0)
    lane = lax.broadcasted_iota(jnp.int32, (2 * ROWS, SLOTS), 1)
    own_fold = lax.div(row, 8) == lax.div(lane, DEPTH - SLOTS)

    def residuals(zt):
        def some(n, carry):
            for u in range(4):
                p = n * 4 + u
                full = w[pl.ds(zt * GROUP + p, 2 * ROWS, stride=PITCH), :]
                tail = jnp.concatenate([wt[pl.ds(zt * GROUP + p, 8, stride=PITCH), :]] * FOLD, axis=0)
                u2 = jnp.concatenate([full, jnp.where(own_fold, tail, 0.0)], axis=1)
                left = jnp.concatenate(split(u2), axis=0)
                right = jnp.concatenate([vb[zt, p, :SLOTS, :]] + [vb[zt, p, SLOTS:, :]] * FOLD, axis=0)
                r = jnp.dot(left, right, preferred_element_type=jnp.float32)
                r = r[: 2 * ROWS] + r[2 * ROWS :]
                o[0, zt, p] = r[:ROWS]
                o[1, zt, p] = r[ROWS:]
            return carry

        lax.fori_loop(0, GROUP // 4, some, 0)

    def span(n):
        return (0, FIRST, yhf.at[n], yff.at[:, n]) if n < NZ else (FIRST, REST, yhg, yfg)

    def y1(n, zt):
        lo, size, hb, _ = span(n)

        @pl.when(jnp.logical_not(active))
        def _():
            send(o.at[other_e, zt, pl.ds(lo, size // 2)], hb, yhs.at[0, n], yhr.at[n], y1=ym)
            send(o.at[other_e, zt, pl.ds(lo + size // 2, size // 2)], hb, yhs.at[1, n], yhr.at[n], y1=yp)

    def y2(n, zt):
        lo, size, hb, fb_ = span(n)
        wait(hb, yhr.at[n])
        at = pl.ds(lo + side * (size // 2), size // 2)
        o[near_e, zt, at] = o[near_e, zt, at] + hb[...]
        send(o.at[near_e, zt, pl.ds(lo, size)], fb_.at[side], yfs.at[n], yfr.at[side, n], y1=onward)

    def y3(n, zt):
        lo, size, _, fb_ = span(n)

        @pl.when(active)
        def _():
            for k in range(2):
                wait(fb_.at[k], yfr.at[k, n])
            at = pl.ds(lo, size)
            o[other_e, zt, at] = o[other_e, zt, at] + (fb_[0] + fb_[1])

    def gview(zt, t, k):
        return o.at[pl.ds(k, 1), zt, pl.ds(FIRST, REST)] if t == 0 else o.at[:, zt, pl.ds(FIRST, REST)]

    def fview(zt, t, k):
        return o.at[other_e, zt, pl.ds(k * (FIRST // 2), FIRST // 2)] if t == 0 else o.at[other_e, zt, pl.ds(0, FIRST)]

    def gland(t, k):
        return gzb.at[k, t, pl.ds(0, 1)] if t == 0 else gzb.at[k, t]

    def fland(t, k):
        return fzb.at[k, t, pl.ds(0, FIRST // 2)] if t == 0 else fzb.at[k, t]

    def zsend(view, land, ssem, rsem, k, t):
        zt = mod(z + (4 - t), NZ) if k == 0 else mod(z - (4 - t), NZ)
        send(view(zt, t, k), land(t, k), ssem.at[k, t], rsem.at[k, t], z1=zp if k == 0 else zm)

    def zrecv(view, land, rsem, k, t):
        zt = mod(z + (3 - t), NZ) if k == 0 else mod(z - (3 - t), NZ)
        wait(land(t, k), rsem.at[k, t])
        into = view(zt, t, k)
        into[...] = into[...] + land(t, k)[...]

    def zwork(m, view, land, ssem, rsem):
        if m == 0:
            for k in range(2):
                zsend(view, land, ssem, rsem, k, 0)
        elif m < 7:
            k, t = (0, (m - 1) // 2) if m % 2 else (1, m // 2 - 1)
            zrecv(view, land, rsem, k, t)
            zsend(view, land, ssem, rsem, k, t + 1)
        else:
            for k in range(2):
                zrecv(view, land, rsem, k, 3)

    def g(m):
        zwork(m, gview, gland, gzs, gzr)

    def f(m):
        @pl.when(active)
        def _():
            zwork(m, fview, fland, fzs, fzr)

    order = [mod(z + d, NZ) for d in (4, 3, -3, 2, -2, 1, -1, 0)]
    for n in range(NZ):
        residuals(order[n])
        y1(n, order[n])
        if n >= 1:
            y2(n - 1, order[n - 1])
        if n < 7:
            g(n)
        if n >= 2:
            y3(n - 2, order[n - 2])
            f(n - 2)
    y2(7, z)
    y3(6, order[6])
    f(6)
    g(7)
    y1(8, z)
    y3(7, z)
    y2(8, z)
    f(7)
    y3(8, z)

    @pl.when(active)
    def _():
        fb[...] = o[other_e, z].astype(jnp.bfloat16)
        for d in range(NX):
            for e in range(NC):
                x1, c1 = mod(x + d, NX), mod(c + e, NC)
                src = fb.at[mine(x1, c1)]
                dst = fr.at[:, pl.ds(pl.multiple_of(x * ROWS, ROWS), ROWS), :]
                if d or e:
                    send(src, dst, es.at[2 * d + e], er.at[x], x1=x1, c1=c1)
                else:
                    pltpu.make_async_copy(src, dst, er.at[x]).start()

    for x0 in range(NX):
        wait(fr.at[:, pl.ds(x0 * ROWS, ROWS), :], er.at[x0])
    out[...] = fr[...]

    piece = amp.at[:, pl.ds(0, ROWS), :]
    for d in range(1, NX):
        wait(piece, axs.at[d])

    @pl.when(c != home)
    def _():
        wait(piece, axs.at[0])

    def sent(n, carry):
        z0 = mod(z + n, NZ)
        block, half = vb.at[z0, mine(x, c)], vb.at[z0, part(x, c, 0)]
        for k in range(2):
            wait(block, xs.at[k, z0])
            wait(half, xs.at[2 + k, z0])
        for k in range(4):
            wait(block, ss.at[k, z0])

        @pl.when(n > 0)
        def _():
            wait(block, vzs.at[z0])

        wait(ab.at[edge, z0, amp_half(0)], ayf.at[z0])

        @pl.when(active)
        def _():
            for k in range(2):
                wait(ab.at[edge, z0], ays.at[k, z0])

        return carry

    lax.fori_loop(0, NZ, sent, 0)

    @pl.when(active)
    def _():
        wait(ab.at[edge, z], azs.at[NZ])
        for d in (0, 1, -1, 2, -2, 3):
            wait(ab.at[edge, z], azs.at[mod(z - d, NZ)])

    for n in range(NZ + 1):
        lo, size, hb, fb_ = span(n)

        @pl.when(jnp.logical_not(active))
        def _():
            wait(hb, yhs.at[0, n])
            wait(hb, yhs.at[1, n])

        wait(fb_.at[0], yfs.at[n])
    for k in range(2):
        for t in range(4):
            wait(gland(t, k), gzs.at[k, t])

    @pl.when(active)
    def _():
        for k in range(2):
            for t in range(4):
                wait(fland(t, k), fzs.at[k, t])
        for n in range(1, NX * NC):
            wait(fb.at[pl.ds(0, BLOCKS)], es.at[n])


def body(amplitudes, vectors, pair_count, tile_map):
    live = lax.broadcasted_iota(jnp.int32, (BLOCKS, 1, SLOTS), 2) < pair_count[:, None, None]
    f32, bf16 = jnp.float32, jnp.bfloat16
    dma = pltpu.SemaphoreType.DMA
    out = pl.pallas_call(
        kernel,
        out_shape=jax.ShapeDtypeStruct(amplitudes.shape, bf16),
        in_specs=[
            pl.BlockSpec(memory_space=pltpu.VMEM),
            pl.BlockSpec(memory_space=pl.ANY),
            pl.BlockSpec(memory_space=pltpu.SMEM),
            pl.BlockSpec(memory_space=pltpu.VMEM),
        ],
        out_specs=pl.BlockSpec(memory_space=pltpu.VMEM),
        scratch_shapes=[
            pltpu.VMEM(amplitudes.shape, bf16),
            pltpu.VMEM((TOTAL, 2 * TOTAL), bf16),
            pltpu.VMEM((NZ, GROUP, DEPTH, SLOTS), bf16),
            pltpu.VMEM((2, NZ, GROUP, ROWS, SLOTS), bf16),
            pltpu.VMEM((2 * ROWS * PITCH, SLOTS), f32),
            pltpu.VMEM((8 * PITCH, SLOTS), f32),
            pltpu.VMEM((2, NZ, GROUP, ROWS, SLOTS), f32),
            pltpu.VMEM((2, 4, 2, REST, ROWS, SLOTS), f32),
            pltpu.VMEM((2, 4, FIRST, ROWS, SLOTS), f32),
            pltpu.VMEM((NZ, FIRST // 2, ROWS, SLOTS), f32),
            pltpu.VMEM((2, NZ, FIRST, ROWS, SLOTS), f32),
            pltpu.VMEM((REST // 2, ROWS, SLOTS), f32),
            pltpu.VMEM((2, REST, ROWS, SLOTS), f32),
            pltpu.VMEM((GROUP, ROWS, SLOTS), bf16),
            pltpu.VMEM((BLOCKS, NX * ROWS, SLOTS), bf16),
            dma((NZ,)), dma((NZ,)),
            dma((4, NZ)), dma((4, NZ)),
            dma((4, NZ)), dma((4, NZ)),
            dma((NX,)), dma((NX, NC)),
            dma((NZ + 1,)), dma((NZ,)),
            dma((2, NZ)), dma((NZ,)), dma((3, NZ)),
            dma((2, 4)), dma((2, 4)),
            dma((2, 4)), dma((2, 4)),
            dma((2, NZ + 1)), dma((NZ + 1,)),
            dma((NZ + 1,)), dma((2, NZ + 1)),
            dma((NX * NC,)), dma((NX,)),
        ],
        compiler_params=pltpu.CompilerParams(
            collective_id=0, has_side_effects=True, vmem_limit_bytes=60 * 2**20
        ),
        cost_estimate=pl.CostEstimate(flops=12 * 10**9, bytes_accessed=4 * 10**6, transcendentals=0),
    )(amplitudes, vectors, pair_count, tile_map)
    return jnp.where(live, out, jnp.zeros_like(out))


def solution(mesh):
    fine = Mesh(mesh.devices.reshape(NZ, NX, NC, NY), ("z", "x", "c", "y"))
    pair = ("z", "x", "c")
    return jax.shard_map(
        body,
        mesh=fine,
        in_specs=(P(pair, "y", None), P(pair, "y", None), P(pair), P()),
        out_specs=P(pair, "y", None),
        check_vma=False,
    )
```

```python
import jax
import jax.numpy as jnp
from jax import lax
from jax.experimental import pallas as pl
from jax.experimental.pallas import tpu as pltpu
from jax.sharding import Mesh, PartitionSpec as P

NZ, NX, NC, NY = 8, 4, 2, 4
BLOCKS = 4
GROUP = NX * NC * BLOCKS
TOTAL = NZ * GROUP
SLOTS = 128
DEPTH = 160
ROWS = 16
PITCH = TOTAL + 8
FOLD = SLOTS // (DEPTH - SLOTS)
AHEAD = 3
FIRST = 20
REST = GROUP - FIRST


def split(x):
    hi = x.astype(jnp.bfloat16)
    return hi, (x - hi.astype(jnp.float32)).astype(jnp.bfloat16)


def wait(view, sem):
    pltpu.make_async_copy(view, view, sem).wait()


def kernel(
    amp_in, vec, counts, tiles, out,
    amp, near, vb, ab, w, wt, u, ut, o, gzb, fzb, yhf, yff, yhg, yfg, fb, fr,
    vzs, vzr, xs, xr, ss, sr, axs, axr, azs, azr, ays, ayf, ayr,
    gzs, gzr, fzs, fzr, yhs, yhr, yfs, yfr, es, er,
):
    z, x, c, y = (lax.axis_index(a) for a in ("z", "x", "c", "y"))

    def mod(a, n):
        return lax.rem(a + 4 * n, n)

    def send(src, dst, ssem, rsem, z1=z, x1=x, c1=c, y1=y):
        pltpu.make_async_remote_copy(
            src_ref=src, dst_ref=dst, send_sem=ssem, recv_sem=rsem,
            device_id=(z1, x1, c1, y1), device_id_type=pl.DeviceIdType.MESH,
        ).start()

    def away_from(s):
        return jnp.where(lax.rem(s, 2) == 1, lax.div(s + 1, 2), -lax.div(s, 2))

    def source(s):
        return mod(z - away_from(s), NZ)

    zp, zm = mod(z + 1, NZ), mod(z - 1, NZ)
    xp, xm, xo = mod(x + 1, NX), mod(x - 1, NX), mod(x + 2, NX)
    yp, ym = mod(y + 1, NY), mod(y - 1, NY)
    mate = 1 - c
    home, edge = lax.div(y, 2), lax.rem(y, 2)
    active = c == home

    def mine(x0, c0):
        return pl.ds(pl.multiple_of(x0 * (NC * BLOCKS) + c0 * BLOCKS, BLOCKS), BLOCKS)

    def part(x0, c0, h):
        return pl.ds(x0 * (NC * BLOCKS) + c0 * BLOCKS + 2 * h, 2)

    def rows(z1):
        return pl.ds(pl.multiple_of(z1 * DEPTH, DEPTH), DEPTH)

    own = pltpu.make_async_copy(vec.at[:, rows(z), :], vb.at[z, mine(x, c)], vzr.at[z])
    own.start()
    barrier = pltpu.get_barrier_semaphore()
    slot = lax.broadcasted_iota(jnp.int32, (NX * ROWS, SLOTS), 1)

    def greet(z1=z, x1=x, c1=c, y1=y):
        pl.semaphore_signal(barrier, inc=1, device_id=(z1, x1, c1, y1), device_id_type=pl.DeviceIdType.MESH)

    for d in range(1, NZ):
        greet(z1=mod(z + d, NZ))
    for d in range(NX):
        for e in range(NC):
            if d or e:
                greet(x1=mod(x + d, NX), c1=mod(c + e, NC))
    for d in range(1, NY):
        greet(y1=mod(y + d, NY))
    for b in range(BLOCKS):
        amp[b] = jnp.where(slot < counts[b], amp_in[b], jnp.zeros_like(amp_in[b]))

    column = lax.broadcasted_iota(jnp.int32, (32, TOTAL), 1)
    block_of = source(lax.div(column, GROUP)) * GROUP + lax.rem(column, GROUP)

    def adjacency(n, carry):
        at = pl.ds(pl.multiple_of(n * 32, 32), 32)
        named = tiles[at, :]
        found = jnp.zeros((32, TOTAL), jnp.float32)
        for j in range(tiles.shape[1]):
            found = found + jnp.where(named[:, j : j + 1] == block_of, 1.0, 0.0)
        found = found.astype(jnp.bfloat16)
        for k in range(4):
            near[at, k * SLOTS : (k + 1) * SLOTS] = found[:, k // 2 * SLOTS : (k // 2 + 1) * SLOTS]
        return carry

    lax.fori_loop(0, TOTAL // 32, adjacency, 0)
    pl.semaphore_wait(barrier, NZ - 1 + NX * NC - 1 + NY - 1)

    for d in range(NX):
        x1 = mod(x + d, NX)
        src = amp.at[:, pl.ds(pl.multiple_of(x1 * ROWS, ROWS), ROWS), :]
        dst = ab.at[edge, z, mine(x, c)]
        if d:
            send(src, dst, axs.at[d], axr.at[x, c], x1=x1, c1=home)
        else:

            @pl.when(active)
            def _():
                pltpu.make_async_copy(src, dst, axr.at[x, c]).start()

            @pl.when(c != home)
            def _():
                send(src, dst, axs.at[0], axr.at[x, c], c1=home)

    def hand_out(s):
        z1 = mod(z + away_from(s), NZ)
        send(vec.at[:, rows(z1), :], vb.at[z, mine(x, c)], vzs.at[z1], vzr.at[z], z1=z1)

    around = mod(y - 2 * c, NY)
    near_e, other_e = 1 - lax.rem(around, 2), lax.rem(around, 2)
    behind = jnp.logical_or(around == 0, around == 3)
    side = jnp.where(behind, 1, 0)
    onward, away = jnp.where(behind, yp, ym), jnp.where(behind, ym, yp)

    def amp_half(h):
        return pl.ds(pl.multiple_of(h * (GROUP // 2), GROUP // 2), GROUP // 2)

    def spread_amp(z0):
        block = ab.at[other_e, z0]
        send(block, block, ays.at[0, z0], ayr.at[0, z0], y1=yp)
        send(block, block, ays.at[1, z0], ayr.at[0, z0], y1=ym)

    def products(s, z0, x0, c0):
        for b in range(BLOCKS):
            q = x0 * (NC * BLOCKS) + c0 * BLOCKS + b
            a = jnp.concatenate([ab[0, z0, q], ab[1, z0, q]], axis=0)
            r = lax.dot_general(a, vb[z0, q], (((1,), (1,)), ((), ())), preferred_element_type=jnp.float32)
            w[pl.ds(s * GROUP + q, 2 * ROWS, stride=PITCH), :] = r[:, :SLOTS]
            tail = [r[m * 8 : m * 8 + 8, SLOTS:] for m in range(FOLD)]
            wt[pl.ds(s * GROUP + q, 8, stride=PITCH), :] = jnp.concatenate(tail, axis=1)

    def mix(src, dst, half):
        def some(i, carry):
            at = [pl.multiple_of((2 * i + h) * PITCH, 8) for h in range(2)]
            hi, lo = split(jnp.concatenate([src[pl.ds(a + half * SLOTS, SLOTS), :] for a in at], axis=1))
            pairs = near[:, half * TOTAL : (half + 1) * TOTAL]
            r = jnp.dot(pairs, jnp.concatenate([hi, lo], axis=0), preferred_element_type=jnp.float32)
            for h in range(2):
                to = pl.ds(at[h], TOTAL)
                part_sum = r[:, h * SLOTS : (h + 1) * SLOTS]
                dst[to, :] = dst[to, :] + part_sum if half else part_sum
            return carry

        lax.fori_loop(0, src.shape[0] // PITCH // 2, some, 0)

    def spread(z0):
        block = vb.at[z0, mine(x, c)]
        send(block, block, xs.at[0, z0], xr.at[0, z0], x1=xp)
        send(block, block, xs.at[1, z0], xr.at[1, z0], x1=xm)
        send(block, block, ss.at[0, z0], sr.at[0, z0], c1=mate)

    wait(vb.at[z, mine(x, c)], vzr.at[z])
    spread(z)

    @pl.when(active)
    def _():
        for x0 in range(NX):
            for c0 in range(NC):
                wait(ab.at[edge, z, mine(x0, c0)], axr.at[x0, c0])
        block = ab.at[edge, z]
        send(block, block, azs.at[z], azr.at[z], z1=zp)
        send(block, block, azs.at[NZ], azr.at[z], z1=zm)
        spread_amp(z)

    for s in range(1, AHEAD + 1):
        hand_out(jnp.int32(s))

    def step(s, carry):
        @pl.when(jnp.logical_and(jnp.logical_and(s >= 1, s < NZ), active))
        def _():
            z0 = source(s)
            block = ab.at[edge, z0]
            wait(block, azr.at[z0])

            @pl.when(s < NZ - 2)
            def _():
                send(block, block, azs.at[z0], azr.at[z0], z1=jnp.where(lax.rem(s, 2) == 1, zp, zm))

            spread_amp(z0)

        @pl.when(jnp.logical_and(s >= 1, s < NZ + 1))
        def _():
            z0 = source(s - 1)
            wait(ab.at[near_e, z0], ayr.at[0, z0])
            half = ab.at[near_e, z0, amp_half(side)]
            send(half, half, ayf.at[z0], ayr.at[1 + side, z0], y1=away)

        @pl.when(jnp.logical_and(s >= 1, s < NZ))
        def _():
            z0 = source(s)
            wait(vb.at[z0, mine(x, c)], vzr.at[z0])

            @pl.when(s < NZ - AHEAD)
            def _():
                hand_out(s + AHEAD)

            spread(z0)

        @pl.when(jnp.logical_and(s >= 1, s < NZ + 1))
        def _():
            z0 = source(s - 1)
            left, right = vb.at[z0, mine(xm, c)], vb.at[z0, mine(xp, c)]
            wait(left, xr.at[0, z0])
            half = vb.at[z0, part(xm, c, 0)]
            send(half, half, xs.at[2, z0], xr.at[2, z0], x1=xp)
            send(left, left, ss.at[1, z0], sr.at[1, z0], c1=mate)
            wait(right, xr.at[1, z0])
            half = vb.at[z0, part(xp, c, 1)]
            send(half, half, xs.at[3, z0], xr.at[3, z0], x1=xm)
            send(right, right, ss.at[2, z0], sr.at[2, z0], c1=mate)

        @pl.when(jnp.logical_and(s >= 2, s < NZ + 2))
        def _():
            z0 = source(s - 2)

            @pl.when(jnp.logical_not(active))
            def _():
                for h in range(2):
                    wait(ab.at[other_e, z0, amp_half(h)], ayr.at[1 + h, z0])

            for x0 in (x, xm, xp):
                products(s - 2, z0, x0, c)
            wait(vb.at[z0, mine(x, mate)], sr.at[0, z0])
            products(s - 2, z0, x, mate)
            wait(vb.at[z0, part(xo, c, 0)], xr.at[2, z0])
            wait(vb.at[z0, part(xo, c, 1)], xr.at[3, z0])
            block = vb.at[z0, mine(xo, c)]
            send(block, block, ss.at[3, z0], sr.at[3, z0], c1=mate)
            products(s - 2, z0, xo, c)
            for k, x0 in ((1, xm), (2, xp)):
                wait(vb.at[z0, mine(x0, mate)], sr.at[k, z0])
                products(s - 2, z0, x0, mate)

        @pl.when(s >= 3)
        def _():
            z0 = source(s - 3)
            wait(vb.at[z0, mine(xo, mate)], sr.at[3, z0])
            products(s - 3, z0, xo, mate)

        @pl.when(s == NZ - 1)
        def _():
            mix(w, u, 0)
            mix(wt, ut, 0)

        return carry

    lax.fori_loop(0, NZ + 3, step, 0)

    mix(w, u, 1)
    mix(wt, ut, 1)
    row = lax.broadcasted_iota(jnp.int32, (2 * ROWS, SLOTS), 0)
    lane = lax.broadcasted_iota(jnp.int32, (2 * ROWS, SLOTS), 1)
    own_fold = lax.div(row, 8) == lax.div(lane, DEPTH - SLOTS)

    def residuals(zt):
        def some(n, carry):
            for step_in in range(4):
                p = n * 4 + step_in
                full = u[pl.ds(zt * GROUP + p, 2 * ROWS, stride=PITCH), :]
                tail = jnp.concatenate([ut[pl.ds(zt * GROUP + p, 8, stride=PITCH), :]] * FOLD, axis=0)
                u2 = jnp.concatenate([full, jnp.where(own_fold, tail, 0.0)], axis=1)
                left = jnp.concatenate(split(u2), axis=0)
                right = jnp.concatenate([vb[zt, p, :SLOTS, :]] + [vb[zt, p, SLOTS:, :]] * FOLD, axis=0)
                r = jnp.dot(left, right, preferred_element_type=jnp.float32)
                r = r[: 2 * ROWS] + r[2 * ROWS :]
                o[0, zt, p] = r[:ROWS]
                o[1, zt, p] = r[ROWS:]
            return carry

        lax.fori_loop(0, GROUP // 4, some, 0)

    def span(n):
        return (0, FIRST, yhf.at[n], yff.at[:, n]) if n < NZ else (FIRST, REST, yhg, yfg)

    def y1(n, zt):
        lo, size, hb, _ = span(n)

        @pl.when(jnp.logical_not(active))
        def _():
            send(o.at[other_e, zt, pl.ds(lo, size // 2)], hb, yhs.at[0, n], yhr.at[n], y1=ym)
            send(o.at[other_e, zt, pl.ds(lo + size // 2, size // 2)], hb, yhs.at[1, n], yhr.at[n], y1=yp)

    def y2(n, zt):
        lo, size, hb, fb_ = span(n)
        wait(hb, yhr.at[n])
        at = pl.ds(lo + side * (size // 2), size // 2)
        o[near_e, zt, at] = o[near_e, zt, at] + hb[...]
        send(o.at[near_e, zt, pl.ds(lo, size)], fb_.at[side], yfs.at[n], yfr.at[side, n], y1=onward)

    def y3(n, zt):
        lo, size, _, fb_ = span(n)

        @pl.when(active)
        def _():
            for k in range(2):
                wait(fb_.at[k], yfr.at[k, n])
            at = pl.ds(lo, size)
            o[other_e, zt, at] = o[other_e, zt, at] + (fb_[0] + fb_[1])

    def gview(e):
        def view(zt, t, k):
            return o.at[e, zt, pl.ds(FIRST + k * (REST // 2), REST // 2)] if t == 0 else o.at[e, zt, pl.ds(FIRST, REST)]

        return view

    def fview(zt, t, k):
        return o.at[other_e, zt, pl.ds(k * (FIRST // 2), FIRST // 2)] if t == 0 else o.at[other_e, zt, pl.ds(0, FIRST)]

    def gland(e):
        def land(t, k):
            return gzb.at[e, k, t, pl.ds(0, REST // 2)] if t == 0 else gzb.at[e, k, t]

        return land

    def fland(t, k):
        return fzb.at[k, t, pl.ds(0, FIRST // 2)] if t == 0 else fzb.at[k, t]

    def zsend(view, land, ssem, rsem, k, t):
        zt = mod(z + (4 - t), NZ) if k == 0 else mod(z - (4 - t), NZ)
        send(view(zt, t, k), land(t, k), ssem.at[k, t], rsem.at[k, t], z1=zp if k == 0 else zm)

    def zrecv(view, land, rsem, k, t):
        zt = mod(z + (3 - t), NZ) if k == 0 else mod(z - (3 - t), NZ)
        wait(land(t, k), rsem.at[k, t])
        into = view(zt, t, k)
        into[...] = into[...] + land(t, k)[...]

    def zwork(m, view, land, ssem, rsem):
        if m == 0:
            for k in range(2):
                zsend(view, land, ssem, rsem, k, 0)
        elif m < 7:
            k, t = (0, (m - 1) // 2) if m % 2 else (1, m // 2 - 1)
            zrecv(view, land, rsem, k, t)
            zsend(view, land, ssem, rsem, k, t + 1)
        else:
            for k in range(2):
                zrecv(view, land, rsem, k, 3)

    def g(m):
        for e in range(2):
            zwork(m, gview(e), gland(e), gzs.at[e], gzr.at[e])

    def f(m):
        @pl.when(active)
        def _():
            zwork(m, fview, fland, fzs, fzr)

    def sent(n):
        z0 = mod(z + n, NZ)
        block, half = vb.at[z0, mine(x, c)], vb.at[z0, part(x, c, 0)]
        for k in range(2):
            wait(block, xs.at[k, z0])
            wait(half, xs.at[2 + k, z0])
        for k in range(4):
            wait(block, ss.at[k, z0])

        if n > 0:
            wait(block, vzs.at[z0])

        wait(ab.at[edge, z0, amp_half(0)], ayf.at[z0])

        @pl.when(active)
        def _():
            for k in range(2):
                wait(ab.at[edge, z0], ays.at[k, z0])

    def sent_first():
        piece = amp.at[:, pl.ds(0, ROWS), :]
        for d in range(1, NX):
            wait(piece, axs.at[d])

        @pl.when(c != home)
        def _():
            wait(piece, axs.at[0])


        @pl.when(active)
        def _():
            wait(ab.at[edge, z], azs.at[NZ])
            for d in (0, 1, -1, 2, -2, 3):
                wait(ab.at[edge, z], azs.at[mod(z - d, NZ)])

    order = [mod(z + d, NZ) for d in (4, 3, -3, 2, -2, 1, -1, 0)]
    for n in range(NZ):
        residuals(order[n])
        y1(n, order[n])
        if n >= 1:
            y2(n - 1, order[n - 1])
        if n < 7:
            g(n)
        if n >= 2:
            y3(n - 2, order[n - 2])
            f(n - 2)
        sent(n)
    sent_first()
    y2(7, z)
    y3(6, order[6])
    f(6)
    g(7)
    y1(8, z)
    y3(7, z)
    y2(8, z)
    f(7)
    y3(8, z)

    @pl.when(active)
    def _():
        fb[...] = o[other_e, z].astype(jnp.bfloat16)
        for d in range(NX):
            for e in range(NC):
                x1, c1 = mod(x + d, NX), mod(c + e, NC)
                src = fb.at[mine(x1, c1)]
                dst = fr.at[:, pl.ds(pl.multiple_of(x * ROWS, ROWS), ROWS), :]
                if d or e:
                    send(src, dst, es.at[2 * d + e], er.at[x], x1=x1, c1=c1)
                else:
                    pltpu.make_async_copy(src, dst, er.at[x]).start()

    for n in range(NZ + 1):
        lo, size, hb, fb_ = span(n)

        @pl.when(jnp.logical_not(active))
        def _():
            wait(hb, yhs.at[0, n])
            wait(hb, yhs.at[1, n])

        wait(fb_.at[0], yfs.at[n])
    for k in range(2):
        for t in range(4):
            for e in range(2):
                wait(gland(e)(t, k), gzs.at[e, k, t])

    @pl.when(active)
    def _():
        for k in range(2):
            for t in range(4):
                wait(fland(t, k), fzs.at[k, t])
        for n in range(1, NX * NC):
            wait(fb.at[pl.ds(0, BLOCKS)], es.at[n])

    for x0 in range(NX):
        wait(fr.at[:, pl.ds(x0 * ROWS, ROWS), :], er.at[x0])
    out[...] = fr[...]


def body(amplitudes, vectors, pair_count, tile_map):
    live = lax.broadcasted_iota(jnp.int32, (BLOCKS, 1, SLOTS), 2) < pair_count[:, None, None]
    f32, bf16 = jnp.float32, jnp.bfloat16
    dma = pltpu.SemaphoreType.DMA
    out = pl.pallas_call(
        kernel,
        out_shape=jax.ShapeDtypeStruct(amplitudes.shape, bf16),
        in_specs=[
            pl.BlockSpec(memory_space=pltpu.VMEM),
            pl.BlockSpec(memory_space=pl.ANY),
            pl.BlockSpec(memory_space=pltpu.SMEM),
            pl.BlockSpec(memory_space=pltpu.VMEM),
        ],
        out_specs=pl.BlockSpec(memory_space=pltpu.VMEM),
        scratch_shapes=[
            pltpu.VMEM(amplitudes.shape, bf16),
            pltpu.VMEM((TOTAL, 2 * TOTAL), bf16),
            pltpu.VMEM((NZ, GROUP, DEPTH, SLOTS), bf16),
            pltpu.VMEM((2, NZ, GROUP, ROWS, SLOTS), bf16),
            pltpu.VMEM((2 * ROWS * PITCH, SLOTS), f32),
            pltpu.VMEM((8 * PITCH, SLOTS), f32),
            pltpu.VMEM((2 * ROWS * PITCH, SLOTS), f32),
            pltpu.VMEM((8 * PITCH, SLOTS), f32),
            pltpu.VMEM((2, NZ, GROUP, ROWS, SLOTS), f32),
            pltpu.VMEM((2, 2, 4, REST, ROWS, SLOTS), f32),
            pltpu.VMEM((2, 4, FIRST, ROWS, SLOTS), f32),
            pltpu.VMEM((NZ, FIRST // 2, ROWS, SLOTS), f32),
            pltpu.VMEM((2, NZ, FIRST, ROWS, SLOTS), f32),
            pltpu.VMEM((REST // 2, ROWS, SLOTS), f32),
            pltpu.VMEM((2, REST, ROWS, SLOTS), f32),
            pltpu.VMEM((GROUP, ROWS, SLOTS), bf16),
            pltpu.VMEM((BLOCKS, NX * ROWS, SLOTS), bf16),
            dma((NZ,)), dma((NZ,)),
            dma((4, NZ)), dma((4, NZ)),
            dma((4, NZ)), dma((4, NZ)),
            dma((NX,)), dma((NX, NC)),
            dma((NZ + 1,)), dma((NZ,)),
            dma((2, NZ)), dma((NZ,)), dma((3, NZ)),
            dma((2, 2, 4)), dma((2, 2, 4)),
            dma((2, 4)), dma((2, 4)),
            dma((2, NZ + 1)), dma((NZ + 1,)),
            dma((NZ + 1,)), dma((2, NZ + 1)),
            dma((NX * NC,)), dma((NX,)),
        ],
        compiler_params=pltpu.CompilerParams(
            collective_id=0, has_side_effects=True, vmem_limit_bytes=60 * 2**20
        ),
        cost_estimate=pl.CostEstimate(flops=12 * 10**9, bytes_accessed=4 * 10**6, transcendentals=0),
    )(amplitudes, vectors, pair_count, tile_map)
    return jnp.where(live, out, jnp.zeros_like(out))


def solution(mesh):
    fine = Mesh(mesh.devices.reshape(NZ, NX, NC, NY), ("z", "x", "c", "y"))
    pair = ("z", "x", "c")
    return jax.shard_map(
        body,
        mesh=fine,
        in_specs=(P(pair, "y", None), P(pair, "y", None), P(pair), P()),
        out_specs=P(pair, "y", None),
        check_vma=False,
    )
```

```python
import jax
import jax.numpy as jnp
from jax import lax
from jax.experimental import pallas as pl
from jax.experimental.pallas import tpu as pltpu
from jax.sharding import Mesh, PartitionSpec as P

NZ, NX, NC, NY = 8, 4, 2, 4
BLOCKS = 4
GROUP = NX * NC * BLOCKS
TOTAL = NZ * GROUP
SLOTS = 128
DEPTH = 160
ROWS = 16
PITCH = TOTAL + 8
FOLD = SLOTS // (DEPTH - SLOTS)
AHEAD = 3
FIRST = 20
REST = GROUP - FIRST
G_HOPS = ((4, 2), (3, 2), (2, 1), (1, 0))
F_HOPS = ((4, 2), (3, 2), (2, 0), (1, 0))
F_LAST = tuple(i for i, (_, d) in enumerate(F_HOPS) if d == 0)
ORDER = (
    ("R", 0), ("g", 0, 0, 0), ("g", 0, 1, 0), ("g", 1, 0, 0), ("g", 1, 1, 0), ("y1", 0),
    ("R", 1), ("g", 0, 0, 1), ("g", 1, 0, 1), ("y1", 1), ("R", 2), ("g", 0, 1, 1),
    ("g", 1, 1, 1), ("y1", 2), ("R", 3), ("y2", 0), ("y1", 3), ("R", 4),
    ("y2", 1), ("y1", 4), ("R", 5), ("g", 0, 0, 2), ("g", 0, 1, 2), ("y2", 2),
    ("y1", 5), ("R", 6), ("g", 1, 0, 2), ("g", 1, 1, 2), ("y3", 0), ("f", 0, 0),
    ("f", 1, 0), ("y2", 3), ("y1", 6), ("R", 7), ("y3", 1), ("f", 0, 1),
    ("g", 0, 0, 3), ("g", 0, 1, 3), ("y2", 4), ("y1", 7), ("y3", 2), ("f", 1, 1),
    ("y2", 5), ("g", 1, 0, 3), ("g", 1, 1, 3), ("y3", 3), ("y2", 6), ("f", 0, 2),
    ("gr", 0, 1), ("y3", 4), ("y2", 7), ("gr", 0, 0), ("f", 1, 2), ("y3", 5),
    ("f", 0, 3), ("gr", 1, 0), ("gr", 1, 1), ("gfin",), ("y3", 6), ("f", 1, 3),
    ("y3", 7), ("fown",),
)


def split(x):
    hi = x.astype(jnp.bfloat16)
    return hi, (x - hi.astype(jnp.float32)).astype(jnp.bfloat16)


def wait(view, sem):
    pltpu.make_async_copy(view, view, sem).wait()


def kernel(
    amp_in, vec, counts, tiles, out,
    amp, near, vb, ab, w, wt, u, ut, o, gzb, fzb, yhf, yff, fin,
    vzs, vzr, xs, xr, ss, sr, axs, axr, azs, azr, ays, ayf, ayr,
    gzs, gzr, fzs, fzr, yhs, yhr, yfs, yfr, ffs, fos, fns, finr,
):
    z, x, c, y = (lax.axis_index(a) for a in ("z", "x", "c", "y"))

    def mod(a, n):
        return lax.rem(a + 4 * n, n)

    def send(src, dst, ssem, rsem, z1=z, x1=x, c1=c, y1=y):
        pltpu.make_async_remote_copy(
            src_ref=src, dst_ref=dst, send_sem=ssem, recv_sem=rsem,
            device_id=(z1, x1, c1, y1), device_id_type=pl.DeviceIdType.MESH,
        ).start()

    def away_from(s):
        return jnp.where(lax.rem(s, 2) == 1, lax.div(s + 1, 2), -lax.div(s, 2))

    def source(s):
        return mod(z - away_from(s), NZ)

    zp, zm = mod(z + 1, NZ), mod(z - 1, NZ)
    xp, xm, xo = mod(x + 1, NX), mod(x - 1, NX), mod(x + 2, NX)
    yp, ym = mod(y + 1, NY), mod(y - 1, NY)
    mate = 1 - c
    home, edge = lax.div(y, 2), lax.rem(y, 2)
    active = c == home

    def mine(x0, c0):
        return pl.ds(pl.multiple_of(x0 * (NC * BLOCKS) + c0 * BLOCKS, BLOCKS), BLOCKS)

    def part(x0, c0, h):
        return pl.ds(x0 * (NC * BLOCKS) + c0 * BLOCKS + 2 * h, 2)

    def rows(z1):
        return pl.ds(pl.multiple_of(z1 * DEPTH, DEPTH), DEPTH)

    own = pltpu.make_async_copy(vec.at[:, rows(z), :], vb.at[z, mine(x, c)], vzr.at[z])
    own.start()
    barrier = pltpu.get_barrier_semaphore()
    slot = lax.broadcasted_iota(jnp.int32, (NX * ROWS, SLOTS), 1)

    def greet(z1=z, x1=x, c1=c, y1=y):
        pl.semaphore_signal(barrier, inc=1, device_id=(z1, x1, c1, y1), device_id_type=pl.DeviceIdType.MESH)

    for d in range(1, NZ):
        greet(z1=mod(z + d, NZ))
    for d in range(NX):
        for e in range(NC):
            if d or e:
                greet(x1=mod(x + d, NX), c1=mod(c + e, NC))
    for d in range(1, NY):
        greet(y1=mod(y + d, NY))
    for b in range(BLOCKS):
        amp[b] = jnp.where(slot < counts[b], amp_in[b], jnp.zeros_like(amp_in[b]))

    column = lax.broadcasted_iota(jnp.int32, (32, TOTAL), 1)
    block_of = source(lax.div(column, GROUP)) * GROUP + lax.rem(column, GROUP)

    def adjacency(n, carry):
        at = pl.ds(pl.multiple_of(n * 32, 32), 32)
        named = tiles[at, :]
        found = jnp.zeros((32, TOTAL), jnp.float32)
        for j in range(tiles.shape[1]):
            found = found + jnp.where(named[:, j : j + 1] == block_of, 1.0, 0.0)
        found = found.astype(jnp.bfloat16)
        for k in range(4):
            near[at, k * SLOTS : (k + 1) * SLOTS] = found[:, k // 2 * SLOTS : (k // 2 + 1) * SLOTS]
        return carry

    lax.fori_loop(0, TOTAL // 32, adjacency, 0)
    pl.semaphore_wait(barrier, NZ - 1 + NX * NC - 1 + NY - 1)

    for d in range(NX):
        x1 = mod(x + d, NX)
        src = amp.at[:, pl.ds(pl.multiple_of(x1 * ROWS, ROWS), ROWS), :]
        dst = ab.at[edge, z, mine(x, c)]
        if d:
            send(src, dst, axs.at[d], axr.at[x, c], x1=x1, c1=home)
        else:

            @pl.when(active)
            def _():
                pltpu.make_async_copy(src, dst, axr.at[x, c]).start()

            @pl.when(c != home)
            def _():
                send(src, dst, axs.at[0], axr.at[x, c], c1=home)

    def hand_out(s):
        z1 = mod(z + away_from(s), NZ)
        send(vec.at[:, rows(z1), :], vb.at[z, mine(x, c)], vzs.at[z1], vzr.at[z], z1=z1)

    around = mod(y - 2 * c, NY)
    near_e, other_e = 1 - lax.rem(around, 2), lax.rem(around, 2)
    behind = jnp.logical_or(around == 0, around == 3)
    side = jnp.where(behind, 1, 0)
    onward, away = jnp.where(behind, yp, ym), jnp.where(behind, ym, yp)

    def amp_half(h):
        return pl.ds(pl.multiple_of(h * (GROUP // 2), GROUP // 2), GROUP // 2)

    def spread_amp(z0):
        block = ab.at[other_e, z0]
        send(block, block, ays.at[0, z0], ayr.at[0, z0], y1=yp)
        send(block, block, ays.at[1, z0], ayr.at[0, z0], y1=ym)

    def products(s, z0, x0, c0):
        for b in range(BLOCKS):
            q = x0 * (NC * BLOCKS) + c0 * BLOCKS + b
            a = jnp.concatenate([ab[0, z0, q], ab[1, z0, q]], axis=0)
            r = lax.dot_general(a, vb[z0, q], (((1,), (1,)), ((), ())), preferred_element_type=jnp.float32)
            w[pl.ds(s * GROUP + q, 2 * ROWS, stride=PITCH), :] = r[:, :SLOTS]
            tail = [r[m * 8 : m * 8 + 8, SLOTS:] for m in range(FOLD)]
            wt[pl.ds(s * GROUP + q, 8, stride=PITCH), :] = jnp.concatenate(tail, axis=1)

    def mix(src, dst, half):
        def some(i, carry):
            at = [pl.multiple_of((2 * i + h) * PITCH, 8) for h in range(2)]
            hi, lo = split(jnp.concatenate([src[pl.ds(a + half * SLOTS, SLOTS), :] for a in at], axis=1))
            pairs = near[:, half * TOTAL : (half + 1) * TOTAL]
            r = jnp.dot(pairs, jnp.concatenate([hi, lo], axis=0), preferred_element_type=jnp.float32)
            for h in range(2):
                to = pl.ds(at[h], TOTAL)
                part_sum = r[:, h * SLOTS : (h + 1) * SLOTS]
                dst[to, :] = dst[to, :] + part_sum if half else part_sum
            return carry

        lax.fori_loop(0, src.shape[0] // PITCH // 2, some, 0)

    def spread(z0):
        block = vb.at[z0, mine(x, c)]
        send(block, block, xs.at[0, z0], xr.at[0, z0], x1=xp)
        send(block, block, xs.at[1, z0], xr.at[1, z0], x1=xm)
        send(block, block, ss.at[0, z0], sr.at[0, z0], c1=mate)

    wait(vb.at[z, mine(x, c)], vzr.at[z])
    spread(z)

    @pl.when(active)
    def _():
        for x0 in range(NX):
            for c0 in range(NC):
                wait(ab.at[edge, z, mine(x0, c0)], axr.at[x0, c0])
        block = ab.at[edge, z]
        send(block, block, azs.at[z], azr.at[z], z1=zp)
        send(block, block, azs.at[NZ], azr.at[z], z1=zm)
        spread_amp(z)

    for s in range(1, AHEAD + 1):
        hand_out(jnp.int32(s))

    def step(s, carry):
        @pl.when(jnp.logical_and(jnp.logical_and(s >= 1, s < NZ), active))
        def _():
            z0 = source(s)
            block = ab.at[edge, z0]
            wait(block, azr.at[z0])

            @pl.when(s < NZ - 2)
            def _():
                send(block, block, azs.at[z0], azr.at[z0], z1=jnp.where(lax.rem(s, 2) == 1, zp, zm))

            spread_amp(z0)

        @pl.when(jnp.logical_and(s >= 1, s < NZ + 1))
        def _():
            z0 = source(s - 1)
            wait(ab.at[near_e, z0], ayr.at[0, z0])
            half = ab.at[near_e, z0, amp_half(side)]
            send(half, half, ayf.at[z0], ayr.at[1 + side, z0], y1=away)

        @pl.when(jnp.logical_and(s >= 1, s < NZ))
        def _():
            z0 = source(s)
            wait(vb.at[z0, mine(x, c)], vzr.at[z0])

            @pl.when(s < NZ - AHEAD)
            def _():
                hand_out(s + AHEAD)

            spread(z0)

        @pl.when(jnp.logical_and(s >= 1, s < NZ + 1))
        def _():
            z0 = source(s - 1)
            left, right = vb.at[z0, mine(xm, c)], vb.at[z0, mine(xp, c)]
            wait(left, xr.at[0, z0])
            half = vb.at[z0, part(xm, c, 0)]
            send(half, half, xs.at[2, z0], xr.at[2, z0], x1=xp)
            send(left, left, ss.at[1, z0], sr.at[1, z0], c1=mate)
            wait(right, xr.at[1, z0])
            half = vb.at[z0, part(xp, c, 1)]
            send(half, half, xs.at[3, z0], xr.at[3, z0], x1=xm)
            send(right, right, ss.at[2, z0], sr.at[2, z0], c1=mate)

        @pl.when(jnp.logical_and(s >= 2, s < NZ + 2))
        def _():
            z0 = source(s - 2)

            @pl.when(jnp.logical_not(active))
            def _():
                for h in range(2):
                    wait(ab.at[other_e, z0, amp_half(h)], ayr.at[1 + h, z0])

            for x0 in (x, xm, xp):
                products(s - 2, z0, x0, c)
            wait(vb.at[z0, mine(x, mate)], sr.at[0, z0])
            products(s - 2, z0, x, mate)
            wait(vb.at[z0, part(xo, c, 0)], xr.at[2, z0])
            wait(vb.at[z0, part(xo, c, 1)], xr.at[3, z0])
            block = vb.at[z0, mine(xo, c)]
            send(block, block, ss.at[3, z0], sr.at[3, z0], c1=mate)
            products(s - 2, z0, xo, c)
            for k, x0 in ((1, xm), (2, xp)):
                wait(vb.at[z0, mine(x0, mate)], sr.at[k, z0])
                products(s - 2, z0, x0, mate)

        @pl.when(s >= 3)
        def _():
            z0 = source(s - 3)
            wait(vb.at[z0, mine(xo, mate)], sr.at[3, z0])
            products(s - 3, z0, xo, mate)

        @pl.when(s == NZ - 1)
        def _():
            mix(w, u, 0)
            mix(wt, ut, 0)

        return carry

    lax.fori_loop(0, NZ + 3, step, 0)

    mix(w, u, 1)
    mix(wt, ut, 1)
    row = lax.broadcasted_iota(jnp.int32, (2 * ROWS, SLOTS), 0)
    lane = lax.broadcasted_iota(jnp.int32, (2 * ROWS, SLOTS), 1)
    own_fold = lax.div(row, 8) == lax.div(lane, DEPTH - SLOTS)

    def residuals(zt):
        def some(n, carry):
            for step_in in range(4):
                p = n * 4 + step_in
                full = u[pl.ds(zt * GROUP + p, 2 * ROWS, stride=PITCH), :]
                tail = jnp.concatenate([ut[pl.ds(zt * GROUP + p, 8, stride=PITCH), :]] * FOLD, axis=0)
                u2 = jnp.concatenate([full, jnp.where(own_fold, tail, 0.0)], axis=1)
                left = jnp.concatenate(split(u2), axis=0)
                right = jnp.concatenate([vb[zt, p, :SLOTS, :]] + [vb[zt, p, SLOTS:, :]] * FOLD, axis=0)
                r = jnp.dot(left, right, preferred_element_type=jnp.float32)
                r = r[: 2 * ROWS] + r[2 * ROWS :]
                o[0, zt, p] = r[:ROWS]
                o[1, zt, p] = r[ROWS:]
            return carry

        lax.fori_loop(0, GROUP // 4, some, 0)

    def y1(n, zt):
        @pl.when(jnp.logical_not(active))
        def _():
            for h, y1_ in enumerate((ym, yp)):
                half = o.at[other_e, zt, pl.ds(h * (FIRST // 2), FIRST // 2)]
                send(half, yhf.at[n], yhs.at[h, n], yhr.at[n], y1=y1_)

    def y2(n, zt):
        wait(yhf.at[n], yhr.at[n])
        at = pl.ds(side * (FIRST // 2), FIRST // 2)
        o[near_e, zt, at] = o[near_e, zt, at] + yhf[n]
        send(o.at[near_e, zt, pl.ds(0, FIRST)], yff.at[side, n], yfs.at[n], yfr.at[side, n], y1=onward)

    def y3(n, zt):
        @pl.when(active)
        def _():
            for k in range(2):
                wait(yff.at[k, n], yfr.at[k, n])
            at = pl.ds(0, FIRST)
            o[other_e, zt, at] = o[other_e, zt, at] + (yff[0, n] + yff[1, n])

    def gview(e):
        def view(zt, far, k):
            return o.at[e, zt, pl.ds(FIRST + k * (REST // 2), REST // 2)] if far else o.at[e, zt, pl.ds(FIRST, REST)]

        return view

    def fview(zt, far, k):
        return o.at[other_e, zt, pl.ds(k * (FIRST // 2), FIRST // 2)] if far else o.at[other_e, zt, pl.ds(0, FIRST)]

    def gland(e):
        def land(i, k):
            return gzb.at[e, k, i, pl.ds(0, REST // 2)] if G_HOPS[i][0] == 4 else gzb.at[e, k, i]

        return land

    def fland(i, k):
        return fzb.at[k, i, pl.ds(0, FIRST // 2)] if F_HOPS[i][0] == 4 else fzb.at[k, i]

    def ahead(k, d):
        return mod(z + d, NZ) if k == 0 else mod(z - d, NZ)

    def ztake(view, land, rsem, hops, k, dist):
        for i, (far, d) in enumerate(hops):
            if d == dist:
                wait(land(i, k), rsem.at[k, i])
                into = view(ahead(k, d), far == 4, k)
                into[...] = into[...] + land(i, k)[...]

    def zpass(view, land, ssem, rsem, hops, k, i):
        far, d = hops[i]
        ztake(view, land, rsem, hops, k, far)
        send(view(ahead(k, far), far == 4, k), land(i, k), ssem.at[k, i], rsem.at[k, i], z1=ahead(k, far - d))

    def deliver(src, zt, slot_to, ssem, groups, z1, y1, local):
        for i in groups:
            x1, c1 = i // NC, i % NC
            piece = src.at[zt, pl.ds(i * BLOCKS, BLOCKS)]
            dst, rsem = fin.at[x, slot_to], finr.at[x, slot_to]
            if local:

                @pl.when(x * NC + c == i)
                def _():
                    pltpu.make_async_copy(piece, dst, rsem).start()

                @pl.when(x * NC + c != i)
                def _():
                    send(piece, dst, ssem.at[i], rsem, z1=z1, x1=x1, c1=c1, y1=y1)
            else:
                send(piece, dst, ssem.at[i], rsem, z1=z1, x1=x1, c1=c1, y1=y1)

    f_groups, g_groups = range(FIRST // BLOCKS), range(FIRST // BLOCKS, NX * NC)

    def f_pass(k, i):
        @pl.when(active)
        def _():
            far, d = F_HOPS[i]
            if d:
                zpass(fview, fland, fzs, fzr, F_HOPS, k, i)
            else:
                ztake(fview, fland, fzr, F_HOPS, k, far)
                j = k * len(F_LAST) + F_LAST.index(i)
                deliver(o.at[other_e], ahead(k, far), 1 + j, ffs.at[j], f_groups, ahead(k, far), y, False)

    def f_own():
        @pl.when(active)
        def _():
            deliver(o.at[other_e], z, 0, fos, f_groups, z, y, True)

    def g_last():
        deliver(o.at[near_e], z, 1 + side, fns, g_groups, z, onward, False)

        @pl.when(active)
        def _():
            deliver(o.at[other_e], z, 0, fos, g_groups, z, y, True)

        @pl.when(jnp.logical_not(active))
        def _():
            deliver(o.at[other_e], z, 3, fos, g_groups, z, mod(y + 2, NY), False)

    def sent(n):
        z0 = mod(z + n, NZ)
        block, half = vb.at[z0, mine(x, c)], vb.at[z0, part(x, c, 0)]
        for k in range(2):
            wait(block, xs.at[k, z0])
            wait(half, xs.at[2 + k, z0])
        for k in range(4):
            wait(block, ss.at[k, z0])

        if n > 0:
            wait(block, vzs.at[z0])

        wait(ab.at[edge, z0, amp_half(0)], ayf.at[z0])

        @pl.when(active)
        def _():
            for k in range(2):
                wait(ab.at[edge, z0], ays.at[k, z0])

    def sent_first():
        piece = amp.at[:, pl.ds(0, ROWS), :]
        for d in range(1, NX):
            wait(piece, axs.at[d])

        @pl.when(c != home)
        def _():
            wait(piece, axs.at[0])


        @pl.when(active)
        def _():
            wait(ab.at[edge, z], azs.at[NZ])
            for d in (0, 1, -1, 2, -2, 3):
                wait(ab.at[edge, z], azs.at[mod(z - d, NZ)])

    chunk = [mod(z + d, NZ) for d in (4, 3, -3, 2, -2, 1, -1, 0)]

    def run(name, *a):
        if name == "R":
            residuals(chunk[a[0]])
            sent(a[0])
        elif name == "y1":
            y1(a[0], chunk[a[0]])
        elif name == "y2":
            y2(a[0], chunk[a[0]])
        elif name == "y3":
            y3(a[0], chunk[a[0]])
        elif name == "g":
            e, k, i = a
            zpass(gview(e), gland(e), gzs.at[e], gzr.at[e], G_HOPS, k, i)
        elif name == "gr":
            e, k = a
            ztake(gview(e), gland(e), gzr.at[e], G_HOPS, k, 0)
        elif name == "gfin":
            g_last()
        elif name == "f":
            f_pass(*a)
        elif name == "fown":
            f_own()

    for name, *a in ORDER:
        run(name, *a)
    sent_first()

    for n in range(NZ):

        @pl.when(jnp.logical_not(active))
        def _():
            wait(yhf.at[n], yhs.at[0, n])
            wait(yhf.at[n], yhs.at[1, n])

        wait(yff.at[0, n], yfs.at[n])
    for k in range(2):
        for i in range(len(G_HOPS)):
            for e in range(2):
                wait(gland(e)(i, k), gzs.at[e, k, i])
    piece = fin.at[0, 0]

    @pl.when(active)
    def _():
        for k in range(2):
            for i in range(len(F_HOPS)):
                if i not in F_LAST:
                    wait(fland(i, k), fzs.at[k, i])
        for j in range(2 * len(F_LAST)):
            for i in f_groups:
                wait(piece, ffs.at[j, i])
        for i in f_groups:

            @pl.when(x * NC + c != i)
            def _():
                wait(piece, fos.at[i])

    for i in g_groups:
        wait(piece, fns.at[i])

        @pl.when(jnp.logical_or(jnp.logical_not(active), x * NC + c != i))
        def _():
            wait(piece, fos.at[i])

    def collect(slots):
        for x0 in range(NX):
            for k in range(slots):
                wait(fin.at[x0, k], finr.at[x0, k])
            total = fin[x0, 0]
            for k in range(1, slots):
                total = total + fin[x0, k]
            out[:, x0 * ROWS : (x0 + 1) * ROWS, :] = total.astype(jnp.bfloat16)

    @pl.when(x * NC + c < FIRST // BLOCKS)
    def _():
        collect(1 + 2 * len(F_LAST))

    @pl.when(x * NC + c >= FIRST // BLOCKS)
    def _():
        collect(4)


def body(amplitudes, vectors, pair_count, tile_map):
    live = lax.broadcasted_iota(jnp.int32, (BLOCKS, 1, SLOTS), 2) < pair_count[:, None, None]
    f32, bf16 = jnp.float32, jnp.bfloat16
    dma = pltpu.SemaphoreType.DMA
    slots = max(4, 1 + 2 * len(F_LAST))
    out = pl.pallas_call(
        kernel,
        out_shape=jax.ShapeDtypeStruct(amplitudes.shape, bf16),
        in_specs=[
            pl.BlockSpec(memory_space=pltpu.VMEM),
            pl.BlockSpec(memory_space=pl.ANY),
            pl.BlockSpec(memory_space=pltpu.SMEM),
            pl.BlockSpec(memory_space=pltpu.VMEM),
        ],
        out_specs=pl.BlockSpec(memory_space=pltpu.VMEM),
        scratch_shapes=[
            pltpu.VMEM(amplitudes.shape, bf16),
            pltpu.VMEM((TOTAL, 2 * TOTAL), bf16),
            pltpu.VMEM((NZ, GROUP, DEPTH, SLOTS), bf16),
            pltpu.VMEM((2, NZ, GROUP, ROWS, SLOTS), bf16),
            pltpu.VMEM((2 * ROWS * PITCH, SLOTS), f32),
            pltpu.VMEM((8 * PITCH, SLOTS), f32),
            pltpu.VMEM((2 * ROWS * PITCH, SLOTS), f32),
            pltpu.VMEM((8 * PITCH, SLOTS), f32),
            pltpu.VMEM((2, NZ, GROUP, ROWS, SLOTS), f32),
            pltpu.VMEM((2, 2, 4, REST, ROWS, SLOTS), f32),
            pltpu.VMEM((2, 4, FIRST, ROWS, SLOTS), f32),
            pltpu.VMEM((NZ, FIRST // 2, ROWS, SLOTS), f32),
            pltpu.VMEM((2, NZ, FIRST, ROWS, SLOTS), f32),
            pltpu.VMEM((NX, slots, BLOCKS, ROWS, SLOTS), f32),
            dma((NZ,)), dma((NZ,)),
            dma((4, NZ)), dma((4, NZ)),
            dma((4, NZ)), dma((4, NZ)),
            dma((NX,)), dma((NX, NC)),
            dma((NZ + 1,)), dma((NZ,)),
            dma((2, NZ)), dma((NZ,)), dma((3, NZ)),
            dma((2, 2, 4)), dma((2, 2, 4)),
            dma((2, 4)), dma((2, 4)),
            dma((2, NZ)), dma((NZ,)),
            dma((NZ,)), dma((2, NZ)),
            dma((2 * len(F_LAST), NX * NC)), dma((NX * NC,)), dma((NX * NC,)),
            dma((NX, slots)),
        ],
        compiler_params=pltpu.CompilerParams(
            collective_id=0, has_side_effects=True, vmem_limit_bytes=60 * 2**20
        ),
        cost_estimate=pl.CostEstimate(flops=12 * 10**9, bytes_accessed=4 * 10**6, transcendentals=0),
    )(amplitudes, vectors, pair_count, tile_map)
    return jnp.where(live, out, jnp.zeros_like(out))


def solution(mesh):
    fine = Mesh(mesh.devices.reshape(NZ, NX, NC, NY), ("z", "x", "c", "y"))
    pair = ("z", "x", "c")
    return jax.shard_map(
        body,
        mesh=fine,
        in_specs=(P(pair, "y", None), P(pair, "y", None), P(pair), P()),
        out_specs=P(pair, "y", None),
        check_vma=False,
    )
```

```python
import jax
import jax.numpy as jnp
from jax import lax
from jax.experimental import pallas as pl
from jax.experimental.pallas import tpu as pltpu
from jax.sharding import Mesh, PartitionSpec as P

NZ, NX, NC, NY = 8, 4, 2, 4
BLOCKS = 4
GROUP = NX * NC * BLOCKS
TOTAL = NZ * GROUP
SLOTS = 128
DEPTH = 160
ROWS = 16
PITCH = TOTAL + 8
FOLD = SLOTS // (DEPTH - SLOTS)
AHEAD = 3
FIRST = 20
REST = GROUP - FIRST
G_HOPS = ((4, 2), (3, 2), (2, 1), (1, 0))
F_HOPS = ((4, 2), (3, 2), (2, 0), (1, 0))
F_LAST = tuple(i for i, (_, d) in enumerate(F_HOPS) if d == 0)
ORDER = (
    ("R", 0), ("g", 0, 0, 0), ("g", 0, 1, 0), ("g", 1, 0, 0), ("g", 1, 1, 0), ("y1", 0),
    ("R", 1), ("g", 0, 0, 1), ("g", 1, 0, 1), ("y1", 1), ("R", 2), ("g", 0, 1, 1),
    ("g", 1, 1, 1), ("y1", 2), ("R", 3), ("y2", 0), ("y1", 3), ("R", 4),
    ("y2", 1), ("y1", 4), ("R", 5), ("g", 0, 0, 2), ("g", 0, 1, 2), ("y2", 2),
    ("y1", 5), ("R", 6), ("g", 1, 0, 2), ("g", 1, 1, 2), ("y3", 0), ("f", 0, 0),
    ("f", 1, 0), ("y2", 3), ("y1", 6), ("R", 7), ("y3", 1), ("f", 0, 1),
    ("g", 0, 0, 3), ("g", 0, 1, 3), ("y2", 4), ("y1", 7), ("y3", 2), ("f", 1, 1),
    ("y2", 5), ("g", 1, 0, 3), ("g", 1, 1, 3), ("y3", 3), ("y2", 6), ("f", 0, 2),
    ("gr", 0, 1), ("y3", 4), ("y2", 7), ("gr", 0, 0), ("f", 1, 2), ("y3", 5),
    ("f", 0, 3), ("gr", 1, 0), ("gr", 1, 1), ("gfin",), ("y3", 6), ("f", 1, 3),
    ("y3", 7), ("fown",),
)


def split(x):
    hi = x.astype(jnp.bfloat16)
    return hi, (x - hi.astype(jnp.float32)).astype(jnp.bfloat16)


def wait(view, sem):
    pltpu.make_async_copy(view, view, sem).wait()


def kernel(
    amp_in, vec, counts, tiles, out,
    amp, near, vb, ab, w, wt, u, ut, o, gzb, fzb, yhf, yff, fin,
    vzs, vzr, xs, xr, ss, sr, axs, axr, azs, azr, ays, ayf, ayr,
    gzs, gzr, fzs, fzr, yhs, yhr, yfs, yfr, ffs, fos, fns, finr,
):
    z, x, c, y = (lax.axis_index(a) for a in ("z", "x", "c", "y"))

    def mod(a, n):
        return lax.rem(a + 4 * n, n)

    def send(src, dst, ssem, rsem, z1=z, x1=x, c1=c, y1=y):
        pltpu.make_async_remote_copy(
            src_ref=src, dst_ref=dst, send_sem=ssem, recv_sem=rsem,
            device_id=(z1, x1, c1, y1), device_id_type=pl.DeviceIdType.MESH,
        ).start()

    def away_from(s):
        return jnp.where(lax.rem(s, 2) == 1, lax.div(s + 1, 2), -lax.div(s, 2))

    def source(s):
        return mod(z - away_from(s), NZ)

    zp, zm = mod(z + 1, NZ), mod(z - 1, NZ)
    xp, xm, xo = mod(x + 1, NX), mod(x - 1, NX), mod(x + 2, NX)
    yp, ym = mod(y + 1, NY), mod(y - 1, NY)
    mate = 1 - c
    home, edge = lax.div(y, 2), lax.rem(y, 2)
    active = c == home

    def mine(x0, c0):
        return pl.ds(pl.multiple_of(x0 * (NC * BLOCKS) + c0 * BLOCKS, BLOCKS), BLOCKS)

    def part(x0, c0, h):
        return pl.ds(x0 * (NC * BLOCKS) + c0 * BLOCKS + 2 * h, 2)

    def rows(z1):
        return pl.ds(pl.multiple_of(z1 * DEPTH, DEPTH), DEPTH)

    own = pltpu.make_async_copy(vec.at[:, rows(z), :], vb.at[z, mine(x, c)], vzr.at[z])
    own.start()
    barrier = pltpu.get_barrier_semaphore()
    slot = lax.broadcasted_iota(jnp.int32, (NX * ROWS, SLOTS), 1)

    def greet(z1=z, x1=x, c1=c, y1=y):
        pl.semaphore_signal(barrier, inc=1, device_id=(z1, x1, c1, y1), device_id_type=pl.DeviceIdType.MESH)

    for d in range(1, NZ):
        greet(z1=mod(z + d, NZ))
    for d in range(NX):
        for e in range(NC):
            if d or e:
                greet(x1=mod(x + d, NX), c1=mod(c + e, NC))
    for d in range(1, NY):
        greet(y1=mod(y + d, NY))
    for b in range(BLOCKS):
        amp[b] = jnp.where(slot < counts[b], amp_in[b], jnp.zeros_like(amp_in[b]))

    column = lax.broadcasted_iota(jnp.int32, (32, TOTAL), 1)
    block_of = source(lax.div(column, GROUP)) * GROUP + lax.rem(column, GROUP)

    def adjacency(n, carry):
        at = pl.ds(pl.multiple_of(n * 32, 32), 32)
        named = tiles[at, :]
        found = jnp.zeros((32, TOTAL), jnp.float32)
        for j in range(tiles.shape[1]):
            found = found + jnp.where(named[:, j : j + 1] == block_of, 1.0, 0.0)
        found = found.astype(jnp.bfloat16)
        for k in range(4):
            near[at, k * SLOTS : (k + 1) * SLOTS] = found[:, k // 2 * SLOTS : (k // 2 + 1) * SLOTS]
        return carry

    lax.fori_loop(0, TOTAL // 32, adjacency, 0)
    pl.semaphore_wait(barrier, NZ - 1 + NX * NC - 1 + NY - 1)

    for d in range(NX):
        x1 = mod(x + d, NX)
        src = amp.at[:, pl.ds(pl.multiple_of(x1 * ROWS, ROWS), ROWS), :]
        dst = ab.at[edge, z, mine(x, c)]
        if d:
            send(src, dst, axs.at[d], axr.at[x, c], x1=x1, c1=home)
        else:

            @pl.when(active)
            def _():
                pltpu.make_async_copy(src, dst, axr.at[x, c]).start()

            @pl.when(c != home)
            def _():
                send(src, dst, axs.at[0], axr.at[x, c], c1=home)

    def hand_out(s):
        z1 = mod(z + away_from(s), NZ)
        send(vec.at[:, rows(z1), :], vb.at[z, mine(x, c)], vzs.at[z1], vzr.at[z], z1=z1)

    around = mod(y - 2 * c, NY)
    near_e, other_e = 1 - lax.rem(around, 2), lax.rem(around, 2)
    behind = jnp.logical_or(around == 0, around == 3)
    side = jnp.where(behind, 1, 0)
    onward, away = jnp.where(behind, yp, ym), jnp.where(behind, ym, yp)

    def amp_half(h):
        return pl.ds(pl.multiple_of(h * (GROUP // 2), GROUP // 2), GROUP // 2)

    def spread_amp(z0):
        block = ab.at[other_e, z0]
        send(block, block, ays.at[0, z0], ayr.at[0, z0], y1=yp)
        send(block, block, ays.at[1, z0], ayr.at[0, z0], y1=ym)

    def products(s, z0, x0, c0):
        for b in range(BLOCKS):
            q = x0 * (NC * BLOCKS) + c0 * BLOCKS + b
            a = jnp.concatenate([ab[0, z0, q], ab[1, z0, q]], axis=0)
            r = lax.dot_general(a, vb[z0, q], (((1,), (1,)), ((), ())), preferred_element_type=jnp.float32)
            w[pl.ds(s * GROUP + q, 2 * ROWS, stride=PITCH), :] = r[:, :SLOTS]
            tail = [r[m * 8 : m * 8 + 8, SLOTS:] for m in range(FOLD)]
            wt[pl.ds(s * GROUP + q, 8, stride=PITCH), :] = jnp.concatenate(tail, axis=1)

    def mix(src, dst, half):
        def some(i, carry):
            at = [pl.multiple_of((2 * i + h) * PITCH, 8) for h in range(2)]
            hi, lo = split(jnp.concatenate([src[pl.ds(a + half * SLOTS, SLOTS), :] for a in at], axis=1))
            pairs = near[:, half * TOTAL : (half + 1) * TOTAL]
            r = jnp.dot(pairs, jnp.concatenate([hi, lo], axis=0), preferred_element_type=jnp.float32)
            for h in range(2):
                to = pl.ds(at[h], TOTAL)
                part_sum = r[:, h * SLOTS : (h + 1) * SLOTS]
                dst[to, :] = dst[to, :] + part_sum if half else part_sum
            return carry

        lax.fori_loop(0, src.shape[0] // PITCH // 2, some, 0, unroll=4)

    def spread(z0):
        block = vb.at[z0, mine(x, c)]
        send(block, block, xs.at[0, z0], xr.at[0, z0], x1=xp)
        send(block, block, xs.at[1, z0], xr.at[1, z0], x1=xm)
        send(block, block, ss.at[0, z0], sr.at[0, z0], c1=mate)

    wait(vb.at[z, mine(x, c)], vzr.at[z])
    spread(z)

    @pl.when(active)
    def _():
        for x0 in range(NX):
            for c0 in range(NC):
                wait(ab.at[edge, z, mine(x0, c0)], axr.at[x0, c0])
        block = ab.at[edge, z]
        send(block, block, azs.at[z], azr.at[z], z1=zp)
        send(block, block, azs.at[NZ], azr.at[z], z1=zm)
        spread_amp(z)

    for s in range(1, AHEAD + 1):
        hand_out(jnp.int32(s))

    def step(s, carry):
        @pl.when(jnp.logical_and(jnp.logical_and(s >= 1, s < NZ), active))
        def _():
            z0 = source(s)
            block = ab.at[edge, z0]
            wait(block, azr.at[z0])

            @pl.when(s < NZ - 2)
            def _():
                send(block, block, azs.at[z0], azr.at[z0], z1=jnp.where(lax.rem(s, 2) == 1, zp, zm))

            spread_amp(z0)

        @pl.when(jnp.logical_and(s >= 1, s < NZ + 1))
        def _():
            z0 = source(s - 1)
            wait(ab.at[near_e, z0], ayr.at[0, z0])
            half = ab.at[near_e, z0, amp_half(side)]
            send(half, half, ayf.at[z0], ayr.at[1 + side, z0], y1=away)

        @pl.when(jnp.logical_and(s >= 1, s < NZ))
        def _():
            z0 = source(s)
            wait(vb.at[z0, mine(x, c)], vzr.at[z0])

            @pl.when(s < NZ - AHEAD)
            def _():
                hand_out(s + AHEAD)

            spread(z0)

        @pl.when(jnp.logical_and(s >= 1, s < NZ + 1))
        def _():
            z0 = source(s - 1)
            left, right = vb.at[z0, mine(xm, c)], vb.at[z0, mine(xp, c)]
            wait(left, xr.at[0, z0])
            half = vb.at[z0, part(xm, c, 0)]
            send(half, half, xs.at[2, z0], xr.at[2, z0], x1=xp)
            send(left, left, ss.at[1, z0], sr.at[1, z0], c1=mate)
            wait(right, xr.at[1, z0])
            half = vb.at[z0, part(xp, c, 1)]
            send(half, half, xs.at[3, z0], xr.at[3, z0], x1=xm)
            send(right, right, ss.at[2, z0], sr.at[2, z0], c1=mate)

        @pl.when(jnp.logical_and(s >= 2, s < NZ + 2))
        def _():
            z0 = source(s - 2)

            @pl.when(jnp.logical_not(active))
            def _():
                for h in range(2):
                    wait(ab.at[other_e, z0, amp_half(h)], ayr.at[1 + h, z0])

            for x0 in (x, xm, xp):
                products(s - 2, z0, x0, c)
            wait(vb.at[z0, mine(x, mate)], sr.at[0, z0])
            products(s - 2, z0, x, mate)
            wait(vb.at[z0, part(xo, c, 0)], xr.at[2, z0])
            wait(vb.at[z0, part(xo, c, 1)], xr.at[3, z0])
            block = vb.at[z0, mine(xo, c)]
            send(block, block, ss.at[3, z0], sr.at[3, z0], c1=mate)
            products(s - 2, z0, xo, c)
            for k, x0 in ((1, xm), (2, xp)):
                wait(vb.at[z0, mine(x0, mate)], sr.at[k, z0])
                products(s - 2, z0, x0, mate)

        @pl.when(s >= 3)
        def _():
            z0 = source(s - 3)
            wait(vb.at[z0, mine(xo, mate)], sr.at[3, z0])
            products(s - 3, z0, xo, mate)

        @pl.when(s == NZ - 1)
        def _():
            mix(w, u, 0)
            mix(wt, ut, 0)

        return carry

    lax.fori_loop(0, NZ + 3, step, 0)

    mix(w, u, 1)
    mix(wt, ut, 1)
    row = lax.broadcasted_iota(jnp.int32, (2 * ROWS, SLOTS), 0)
    lane = lax.broadcasted_iota(jnp.int32, (2 * ROWS, SLOTS), 1)
    own_fold = lax.div(row, 8) == lax.div(lane, DEPTH - SLOTS)

    def residuals(zt):
        def some(n, carry):
            for step_in in range(4):
                p = n * 4 + step_in
                full = u[pl.ds(zt * GROUP + p, 2 * ROWS, stride=PITCH), :]
                tail = jnp.concatenate([ut[pl.ds(zt * GROUP + p, 8, stride=PITCH), :]] * FOLD, axis=0)
                u2 = jnp.concatenate([full, jnp.where(own_fold, tail, 0.0)], axis=1)
                left = jnp.concatenate(split(u2), axis=0)
                right = jnp.concatenate([vb[zt, p, :SLOTS, :]] + [vb[zt, p, SLOTS:, :]] * FOLD, axis=0)
                r = jnp.dot(left, right, preferred_element_type=jnp.float32)
                r = r[: 2 * ROWS] + r[2 * ROWS :]
                o[0, zt, p] = r[:ROWS]
                o[1, zt, p] = r[ROWS:]
            return carry

        lax.fori_loop(0, GROUP // 4, some, 0, unroll=2)

    def y1(n, zt):
        @pl.when(jnp.logical_not(active))
        def _():
            for h, y1_ in enumerate((ym, yp)):
                half = o.at[other_e, zt, pl.ds(h * (FIRST // 2), FIRST // 2)]
                send(half, yhf.at[n], yhs.at[h, n], yhr.at[n], y1=y1_)

    def y2(n, zt):
        wait(yhf.at[n], yhr.at[n])
        at = pl.ds(side * (FIRST // 2), FIRST // 2)
        o[near_e, zt, at] = o[near_e, zt, at] + yhf[n]
        send(o.at[near_e, zt, pl.ds(0, FIRST)], yff.at[side, n], yfs.at[n], yfr.at[side, n], y1=onward)

    def y3(n, zt):
        @pl.when(active)
        def _():
            for k in range(2):
                wait(yff.at[k, n], yfr.at[k, n])
            at = pl.ds(0, FIRST)
            o[other_e, zt, at] = o[other_e, zt, at] + (yff[0, n] + yff[1, n])

    def gview(e):
        def view(zt, far, k):
            return o.at[e, zt, pl.ds(FIRST + k * (REST // 2), REST // 2)] if far else o.at[e, zt, pl.ds(FIRST, REST)]

        return view

    def fview(zt, far, k):
        return o.at[other_e, zt, pl.ds(k * (FIRST // 2), FIRST // 2)] if far else o.at[other_e, zt, pl.ds(0, FIRST)]

    def gland(e):
        def land(i, k):
            return gzb.at[e, k, i, pl.ds(0, REST // 2)] if G_HOPS[i][0] == 4 else gzb.at[e, k, i]

        return land

    def fland(i, k):
        return fzb.at[k, i, pl.ds(0, FIRST // 2)] if F_HOPS[i][0] == 4 else fzb.at[k, i]

    def ahead(k, d):
        return mod(z + d, NZ) if k == 0 else mod(z - d, NZ)

    def ztake(view, land, rsem, hops, k, dist):
        for i, (far, d) in enumerate(hops):
            if d == dist:
                wait(land(i, k), rsem.at[k, i])
                into = view(ahead(k, d), far == 4, k)
                into[...] = into[...] + land(i, k)[...]

    def zpass(view, land, ssem, rsem, hops, k, i):
        far, d = hops[i]
        ztake(view, land, rsem, hops, k, far)
        send(view(ahead(k, far), far == 4, k), land(i, k), ssem.at[k, i], rsem.at[k, i], z1=ahead(k, far - d))

    def deliver(src, zt, slot_to, ssem, groups, z1, y1, local):
        for i in groups:
            x1, c1 = i // NC, i % NC
            piece = src.at[zt, pl.ds(i * BLOCKS, BLOCKS)]
            dst, rsem = fin.at[x, slot_to], finr.at[x, slot_to]
            if local:

                @pl.when(x * NC + c == i)
                def _():
                    pltpu.make_async_copy(piece, dst, rsem).start()

                @pl.when(x * NC + c != i)
                def _():
                    send(piece, dst, ssem.at[i], rsem, z1=z1, x1=x1, c1=c1, y1=y1)
            else:
                send(piece, dst, ssem.at[i], rsem, z1=z1, x1=x1, c1=c1, y1=y1)

    f_groups, g_groups = range(FIRST // BLOCKS), range(FIRST // BLOCKS, NX * NC)

    def f_pass(k, i):
        @pl.when(active)
        def _():
            far, d = F_HOPS[i]
            if d:
                zpass(fview, fland, fzs, fzr, F_HOPS, k, i)
            else:
                ztake(fview, fland, fzr, F_HOPS, k, far)
                j = k * len(F_LAST) + F_LAST.index(i)
                deliver(o.at[other_e], ahead(k, far), 1 + j, ffs.at[j], f_groups, ahead(k, far), y, False)

    def f_own():
        @pl.when(active)
        def _():
            deliver(o.at[other_e], z, 0, fos, f_groups, z, y, True)

    def g_last():
        deliver(o.at[near_e], z, 1 + side, fns, g_groups, z, onward, False)

        @pl.when(active)
        def _():
            deliver(o.at[other_e], z, 0, fos, g_groups, z, y, True)

        @pl.when(jnp.logical_not(active))
        def _():
            deliver(o.at[other_e], z, 3, fos, g_groups, z, mod(y + 2, NY), False)

    def sent(n):
        z0 = mod(z + n, NZ)
        block, half = vb.at[z0, mine(x, c)], vb.at[z0, part(x, c, 0)]
        for k in range(2):
            wait(block, xs.at[k, z0])
            wait(half, xs.at[2 + k, z0])
        for k in range(4):
            wait(block, ss.at[k, z0])

        if n > 0:
            wait(block, vzs.at[z0])

        wait(ab.at[edge, z0, amp_half(0)], ayf.at[z0])

        @pl.when(active)
        def _():
            for k in range(2):
                wait(ab.at[edge, z0], ays.at[k, z0])

    def sent_first():
        piece = amp.at[:, pl.ds(0, ROWS), :]
        for d in range(1, NX):
            wait(piece, axs.at[d])

        @pl.when(c != home)
        def _():
            wait(piece, axs.at[0])


        @pl.when(active)
        def _():
            wait(ab.at[edge, z], azs.at[NZ])
            for d in (0, 1, -1, 2, -2, 3):
                wait(ab.at[edge, z], azs.at[mod(z - d, NZ)])

    chunk = [mod(z + d, NZ) for d in (4, 3, -3, 2, -2, 1, -1, 0)]

    def run(name, *a):
        if name == "R":
            residuals(chunk[a[0]])
            sent(a[0])
        elif name == "y1":
            y1(a[0], chunk[a[0]])
        elif name == "y2":
            y2(a[0], chunk[a[0]])
        elif name == "y3":
            y3(a[0], chunk[a[0]])
        elif name == "g":
            e, k, i = a
            zpass(gview(e), gland(e), gzs.at[e], gzr.at[e], G_HOPS, k, i)
        elif name == "gr":
            e, k = a
            ztake(gview(e), gland(e), gzr.at[e], G_HOPS, k, 0)
        elif name == "gfin":
            g_last()
        elif name == "f":
            f_pass(*a)
        elif name == "fown":
            f_own()

    for name, *a in ORDER:
        run(name, *a)
    sent_first()

    for n in range(NZ):

        @pl.when(jnp.logical_not(active))
        def _():
            wait(yhf.at[n], yhs.at[0, n])
            wait(yhf.at[n], yhs.at[1, n])

        wait(yff.at[0, n], yfs.at[n])
    for k in range(2):
        for i in range(len(G_HOPS)):
            for e in range(2):
                wait(gland(e)(i, k), gzs.at[e, k, i])
    piece = fin.at[0, 0]

    @pl.when(active)
    def _():
        for k in range(2):
            for i in range(len(F_HOPS)):
                if i not in F_LAST:
                    wait(fland(i, k), fzs.at[k, i])
        for j in range(2 * len(F_LAST)):
            for i in f_groups:
                wait(piece, ffs.at[j, i])
        for i in f_groups:

            @pl.when(x * NC + c != i)
            def _():
                wait(piece, fos.at[i])

    for i in g_groups:
        wait(piece, fns.at[i])

        @pl.when(jnp.logical_or(jnp.logical_not(active), x * NC + c != i))
        def _():
            wait(piece, fos.at[i])

    def collect(slots):
        for x0 in range(NX):
            for k in range(slots):
                wait(fin.at[x0, k], finr.at[x0, k])
            total = fin[x0, 0]
            for k in range(1, slots):
                total = total + fin[x0, k]
            out[:, x0 * ROWS : (x0 + 1) * ROWS, :] = total.astype(jnp.bfloat16)

    @pl.when(x * NC + c < FIRST // BLOCKS)
    def _():
        collect(1 + 2 * len(F_LAST))

    @pl.when(x * NC + c >= FIRST // BLOCKS)
    def _():
        collect(4)


def body(amplitudes, vectors, pair_count, tile_map):
    live = lax.broadcasted_iota(jnp.int32, (BLOCKS, 1, SLOTS), 2) < pair_count[:, None, None]
    f32, bf16 = jnp.float32, jnp.bfloat16
    dma = pltpu.SemaphoreType.DMA
    slots = max(4, 1 + 2 * len(F_LAST))
    out = pl.pallas_call(
        kernel,
        out_shape=jax.ShapeDtypeStruct(amplitudes.shape, bf16),
        in_specs=[
            pl.BlockSpec(memory_space=pltpu.VMEM),
            pl.BlockSpec(memory_space=pl.ANY),
            pl.BlockSpec(memory_space=pltpu.SMEM),
            pl.BlockSpec(memory_space=pltpu.VMEM),
        ],
        out_specs=pl.BlockSpec(memory_space=pltpu.VMEM),
        scratch_shapes=[
            pltpu.VMEM(amplitudes.shape, bf16),
            pltpu.VMEM((TOTAL, 2 * TOTAL), bf16),
            pltpu.VMEM((NZ, GROUP, DEPTH, SLOTS), bf16),
            pltpu.VMEM((2, NZ, GROUP, ROWS, SLOTS), bf16),
            pltpu.VMEM((2 * ROWS * PITCH, SLOTS), f32),
            pltpu.VMEM((8 * PITCH, SLOTS), f32),
            pltpu.VMEM((2 * ROWS * PITCH, SLOTS), f32),
            pltpu.VMEM((8 * PITCH, SLOTS), f32),
            pltpu.VMEM((2, NZ, GROUP, ROWS, SLOTS), f32),
            pltpu.VMEM((2, 2, 4, REST, ROWS, SLOTS), f32),
            pltpu.VMEM((2, 4, FIRST, ROWS, SLOTS), f32),
            pltpu.VMEM((NZ, FIRST // 2, ROWS, SLOTS), f32),
            pltpu.VMEM((2, NZ, FIRST, ROWS, SLOTS), f32),
            pltpu.VMEM((NX, slots, BLOCKS, ROWS, SLOTS), f32),
            dma((NZ,)), dma((NZ,)),
            dma((4, NZ)), dma((4, NZ)),
            dma((4, NZ)), dma((4, NZ)),
            dma((NX,)), dma((NX, NC)),
            dma((NZ + 1,)), dma((NZ,)),
            dma((2, NZ)), dma((NZ,)), dma((3, NZ)),
            dma((2, 2, 4)), dma((2, 2, 4)),
            dma((2, 4)), dma((2, 4)),
            dma((2, NZ)), dma((NZ,)),
            dma((NZ,)), dma((2, NZ)),
            dma((2 * len(F_LAST), NX * NC)), dma((NX * NC,)), dma((NX * NC,)),
            dma((NX, slots)),
        ],
        compiler_params=pltpu.CompilerParams(
            collective_id=0, has_side_effects=True, vmem_limit_bytes=60 * 2**20
        ),
        cost_estimate=pl.CostEstimate(flops=12 * 10**9, bytes_accessed=4 * 10**6, transcendentals=0),
    )(amplitudes, vectors, pair_count, tile_map)
    return jnp.where(live, out, jnp.zeros_like(out))


def solution(mesh):
    fine = Mesh(mesh.devices.reshape(NZ, NX, NC, NY), ("z", "x", "c", "y"))
    pair = ("z", "x", "c")
    return jax.shard_map(
        body,
        mesh=fine,
        in_specs=(P(pair, "y", None), P(pair, "y", None), P(pair), P()),
        out_specs=P(pair, "y", None),
        check_vma=False,
    )
```

```python
import jax
import jax.numpy as jnp
from jax import lax
from jax.experimental import pallas as pl
from jax.experimental.pallas import tpu as pltpu
from jax.sharding import Mesh, PartitionSpec as P

NZ, NX, NC, NY = 8, 4, 2, 4
BLOCKS = 4
GROUP = NX * NC * BLOCKS
TOTAL = NZ * GROUP
SLOTS = 128
DEPTH = 160
ROWS = 16
PITCH = TOTAL + 8
FOLD = SLOTS // (DEPTH - SLOTS)
AHEAD = 3
FIRST = 20
REST = GROUP - FIRST
G_HOPS = ((4, 2), (3, 2), (2, 1), (1, 0))
F_HOPS = ((4, 2), (3, 2), (2, 0), (1, 0))
F_LAST = tuple(i for i, (_, d) in enumerate(F_HOPS) if d == 0)
ORDER = (
    ("R", 0), ("g", 0, 0, 0), ("g", 0, 1, 0), ("g", 1, 0, 0), ("g", 1, 1, 0), ("y1", 0),
    ("R", 1), ("g", 0, 0, 1), ("g", 1, 0, 1), ("y1", 1), ("R", 2), ("g", 0, 1, 1),
    ("g", 1, 1, 1), ("y1", 2), ("R", 3), ("y1", 3), ("R", 4), ("y2", 0),
    ("y1", 4), ("R", 5), ("y2", 1), ("y1", 5), ("R", 6), ("y2", 2),
    ("y2", 3), ("y1", 6), ("R", 7), ("g", 0, 0, 2), ("g", 0, 1, 2), ("y1", 7),
    ("y3", 0), ("f", 0, 0), ("f", 1, 0), ("y2", 4), ("g", 1, 0, 2), ("g", 1, 1, 2),
    ("y3", 1), ("f", 0, 1), ("y2", 5), ("g", 0, 0, 3), ("g", 0, 1, 3), ("y3", 2),
    ("f", 1, 1), ("y3", 3), ("y2", 6), ("g", 1, 0, 3), ("g", 1, 1, 3), ("y2", 7),
    ("f", 0, 2), ("y3", 4), ("gr", 0, 1), ("gr", 0, 0), ("f", 1, 2), ("y3", 5),
    ("f", 0, 3), ("y3", 6), ("f", 1, 3), ("gr", 1, 0), ("gr", 1, 1), ("gfin",),
    ("y3", 7), ("fown",),
)


def split(x):
    hi = x.astype(jnp.bfloat16)
    return hi, (x - hi.astype(jnp.float32)).astype(jnp.bfloat16)


def wait(view, sem):
    pltpu.make_async_copy(view, view, sem).wait()


def kernel(
    amp_in, vec, counts, tiles, out,
    amp, near, vb, ab, w, wt, u, ut, o, gzb, fzb, yhf, yff, fin,
    vzs, vzr, xs, xr, ss, sr, axs, axr, azs, azr, ays, ayf, ayr,
    gzs, gzr, fzs, fzr, yhs, yhr, yfs, yfr, ffs, fos, fns, finr,
):
    z, x, c, y = (lax.axis_index(a) for a in ("z", "x", "c", "y"))

    def mod(a, n):
        return lax.rem(a + 4 * n, n)

    def send(src, dst, ssem, rsem, z1=z, x1=x, c1=c, y1=y):
        pltpu.make_async_remote_copy(
            src_ref=src, dst_ref=dst, send_sem=ssem, recv_sem=rsem,
            device_id=(z1, x1, c1, y1), device_id_type=pl.DeviceIdType.MESH,
        ).start()

    def away_from(s):
        return jnp.where(lax.rem(s, 2) == 1, lax.div(s + 1, 2), -lax.div(s, 2))

    def source(s):
        return mod(z - away_from(s), NZ)

    zp, zm = mod(z + 1, NZ), mod(z - 1, NZ)
    xp, xm, xo = mod(x + 1, NX), mod(x - 1, NX), mod(x + 2, NX)
    yp, ym = mod(y + 1, NY), mod(y - 1, NY)
    mate = 1 - c
    home, edge = lax.div(y, 2), lax.rem(y, 2)
    active = c == home

    def mine(x0, c0):
        return pl.ds(pl.multiple_of(x0 * (NC * BLOCKS) + c0 * BLOCKS, BLOCKS), BLOCKS)

    def part(x0, c0, h):
        return pl.ds(x0 * (NC * BLOCKS) + c0 * BLOCKS + 2 * h, 2)

    def rows(z1):
        return pl.ds(pl.multiple_of(z1 * DEPTH, DEPTH), DEPTH)

    own = pltpu.make_async_copy(vec.at[:, rows(z), :], vb.at[z, mine(x, c)], vzr.at[z])
    own.start()
    barrier = pltpu.get_barrier_semaphore()
    slot = lax.broadcasted_iota(jnp.int32, (NX * ROWS, SLOTS), 1)

    def greet(z1=z, x1=x, c1=c, y1=y):
        pl.semaphore_signal(barrier, inc=1, device_id=(z1, x1, c1, y1), device_id_type=pl.DeviceIdType.MESH)

    for d in range(1, NZ):
        greet(z1=mod(z + d, NZ))
    for d in range(NX):
        for e in range(NC):
            if d or e:
                greet(x1=mod(x + d, NX), c1=mod(c + e, NC))
    for d in range(1, NY):
        greet(y1=mod(y + d, NY))
    for b in range(BLOCKS):
        amp[b] = jnp.where(slot < counts[b], amp_in[b], jnp.zeros_like(amp_in[b]))

    block_row = lax.broadcasted_iota(jnp.int32, (GROUP, TOTAL), 0)

    def adjacency(n, carry):
        block_of = block_row + source(n) * GROUP
        found = jnp.zeros((GROUP, TOTAL), jnp.float32)
        for j in range(tiles.shape[0]):
            found = found + jnp.where(tiles[j : j + 1, :] == block_of, 1.0, 0.0)
        for h in range(2):
            u[pl.ds(pl.multiple_of(h * TOTAL + n * GROUP, GROUP), GROUP), :] = found[:, h * SLOTS : (h + 1) * SLOTS]
        return carry

    lax.fori_loop(0, NZ, adjacency, 0)
    for h in range(2):
        found = u[h * TOTAL : (h + 1) * TOTAL, :].T.astype(jnp.bfloat16)
        for k in range(4):
            near[h * SLOTS : (h + 1) * SLOTS, k * SLOTS : (k + 1) * SLOTS] = found[:, k // 2 * SLOTS : (k // 2 + 1) * SLOTS]
    pl.semaphore_wait(barrier, NZ - 1 + NX * NC - 1 + NY - 1)

    for d in range(NX):
        x1 = mod(x + d, NX)
        src = amp.at[:, pl.ds(pl.multiple_of(x1 * ROWS, ROWS), ROWS), :]
        dst = ab.at[edge, z, mine(x, c)]
        if d:
            send(src, dst, axs.at[d], axr.at[x, c], x1=x1, c1=home)
        else:

            @pl.when(active)
            def _():
                pltpu.make_async_copy(src, dst, axr.at[x, c]).start()

            @pl.when(c != home)
            def _():
                send(src, dst, axs.at[0], axr.at[x, c], c1=home)

    def hand_out(s):
        z1 = mod(z + away_from(s), NZ)
        send(vec.at[:, rows(z1), :], vb.at[z, mine(x, c)], vzs.at[z1], vzr.at[z], z1=z1)

    around = mod(y - 2 * c, NY)
    near_e, other_e = 1 - lax.rem(around, 2), lax.rem(around, 2)
    behind = jnp.logical_or(around == 0, around == 3)
    side = jnp.where(behind, 1, 0)
    onward, away = jnp.where(behind, yp, ym), jnp.where(behind, ym, yp)

    def amp_half(h):
        return pl.ds(pl.multiple_of(h * (GROUP // 2), GROUP // 2), GROUP // 2)

    def spread_amp(z0):
        block = ab.at[other_e, z0]
        send(block, block, ays.at[0, z0], ayr.at[0, z0], y1=yp)
        send(block, block, ays.at[1, z0], ayr.at[0, z0], y1=ym)

    def products(s, z0, x0, c0):
        for b in range(BLOCKS):
            q = x0 * (NC * BLOCKS) + c0 * BLOCKS + b
            a = jnp.concatenate([ab[0, z0, q], ab[1, z0, q]], axis=0)
            r = lax.dot_general(a, vb[z0, q], (((1,), (1,)), ((), ())), preferred_element_type=jnp.float32)
            w[pl.ds(s * GROUP + q, 2 * ROWS, stride=PITCH), :] = r[:, :SLOTS]
            tail = [r[m * 8 : m * 8 + 8, SLOTS:] for m in range(FOLD)]
            wt[pl.ds(s * GROUP + q, 8, stride=PITCH), :] = jnp.concatenate(tail, axis=1)

    def mix(src, dst, half):
        def some(i, carry):
            at = [pl.multiple_of((2 * i + h) * PITCH, 8) for h in range(2)]
            hi, lo = split(jnp.concatenate([src[pl.ds(a + half * SLOTS, SLOTS), :] for a in at], axis=1))
            pairs = near[:, half * TOTAL : (half + 1) * TOTAL]
            r = jnp.dot(pairs, jnp.concatenate([hi, lo], axis=0), preferred_element_type=jnp.float32)
            for h in range(2):
                to = pl.ds(at[h], TOTAL)
                part_sum = r[:, h * SLOTS : (h + 1) * SLOTS]
                dst[to, :] = dst[to, :] + part_sum if half else part_sum
            return carry

        lax.fori_loop(0, src.shape[0] // PITCH // 2, some, 0, unroll=4)

    def spread(z0):
        block = vb.at[z0, mine(x, c)]
        ha, hb = vb.at[z0, part(x, c, 0)], vb.at[z0, part(x, c, 1)]
        send(ha, ha, xs.at[0, z0], xr.at[0, z0], x1=xp)
        send(hb, hb, xs.at[1, z0], xr.at[1, z0], x1=xm)
        send(hb, hb, xs.at[4, z0], xr.at[4, z0], x1=xp)
        send(ha, ha, xs.at[5, z0], xr.at[5, z0], x1=xm)
        send(block, block, ss.at[0, z0], sr.at[0, z0], c1=mate)

    wait(vb.at[z, mine(x, c)], vzr.at[z])
    spread(z)

    @pl.when(active)
    def _():
        for x0 in range(NX):
            for c0 in range(NC):
                wait(ab.at[edge, z, mine(x0, c0)], axr.at[x0, c0])
        block = ab.at[edge, z]
        send(block, block, azs.at[z], azr.at[z], z1=zp)
        send(block, block, azs.at[NZ], azr.at[z], z1=zm)
        spread_amp(z)

    for s in range(1, AHEAD + 1):
        hand_out(jnp.int32(s))

    def step(s, carry):
        @pl.when(jnp.logical_and(jnp.logical_and(s >= 1, s < NZ), active))
        def _():
            z0 = source(s)
            block = ab.at[edge, z0]
            wait(block, azr.at[z0])

            @pl.when(s < NZ - 2)
            def _():
                send(block, block, azs.at[z0], azr.at[z0], z1=jnp.where(lax.rem(s, 2) == 1, zp, zm))

            spread_amp(z0)

        @pl.when(jnp.logical_and(s >= 1, s < NZ + 1))
        def _():
            z0 = source(s - 1)
            wait(ab.at[near_e, z0], ayr.at[0, z0])
            half = ab.at[near_e, z0, amp_half(side)]
            send(half, half, ayf.at[z0], ayr.at[1 + side, z0], y1=away)

        @pl.when(jnp.logical_and(s >= 1, s < NZ))
        def _():
            z0 = source(s)
            wait(vb.at[z0, mine(x, c)], vzr.at[z0])

            @pl.when(s < NZ - AHEAD)
            def _():
                hand_out(s + AHEAD)

            spread(z0)

        @pl.when(jnp.logical_and(s >= 1, s < NZ + 1))
        def _():
            z0 = source(s - 1)
            left, right = vb.at[z0, mine(xm, c)], vb.at[z0, mine(xp, c)]
            half = vb.at[z0, part(xm, c, 0)]
            wait(half, xr.at[0, z0])
            send(half, half, xs.at[2, z0], xr.at[2, z0], x1=xp)
            half = vb.at[z0, part(xp, c, 1)]
            wait(half, xr.at[1, z0])
            send(half, half, xs.at[3, z0], xr.at[3, z0], x1=xm)
            wait(vb.at[z0, part(xm, c, 1)], xr.at[4, z0])
            send(left, left, ss.at[1, z0], sr.at[1, z0], c1=mate)
            wait(vb.at[z0, part(xp, c, 0)], xr.at[5, z0])
            send(right, right, ss.at[2, z0], sr.at[2, z0], c1=mate)

        @pl.when(jnp.logical_and(s >= 2, s < NZ + 2))
        def _():
            z0 = source(s - 2)

            wait(vb.at[z0, part(xo, c, 0)], xr.at[2, z0])
            wait(vb.at[z0, part(xo, c, 1)], xr.at[3, z0])
            block = vb.at[z0, mine(xo, c)]
            send(block, block, ss.at[3, z0], sr.at[3, z0], c1=mate)

            @pl.when(jnp.logical_not(active))
            def _():
                for h in range(2):
                    wait(ab.at[other_e, z0, amp_half(h)], ayr.at[1 + h, z0])

            for x0 in (x, xm, xp):
                products(s - 2, z0, x0, c)
            wait(vb.at[z0, mine(x, mate)], sr.at[0, z0])
            products(s - 2, z0, x, mate)
            products(s - 2, z0, xo, c)
            for k, x0 in ((1, xm), (2, xp)):
                wait(vb.at[z0, mine(x0, mate)], sr.at[k, z0])
                products(s - 2, z0, x0, mate)

        @pl.when(s >= 3)
        def _():
            z0 = source(s - 3)
            wait(vb.at[z0, mine(xo, mate)], sr.at[3, z0])
            products(s - 3, z0, xo, mate)

        @pl.when(s == NZ - 1)
        def _():
            mix(w, u, 0)
            mix(wt, ut, 0)

        return carry

    lax.fori_loop(0, NZ + 3, step, 0)

    mix(w, u, 1)
    mix(wt, ut, 1)
    row = lax.broadcasted_iota(jnp.int32, (2 * ROWS, SLOTS), 0)
    lane = lax.broadcasted_iota(jnp.int32, (2 * ROWS, SLOTS), 1)
    own_fold = lax.div(row, 8) == lax.div(lane, DEPTH - SLOTS)

    def residuals(zt):
        def some(n, carry):
            for step_in in range(4):
                p = n * 4 + step_in
                full = u[pl.ds(zt * GROUP + p, 2 * ROWS, stride=PITCH), :]
                tail = jnp.concatenate([ut[pl.ds(zt * GROUP + p, 8, stride=PITCH), :]] * FOLD, axis=0)
                u2 = jnp.concatenate([full, jnp.where(own_fold, tail, 0.0)], axis=1)
                left = jnp.concatenate(split(u2), axis=0)
                right = jnp.concatenate([vb[zt, p, :SLOTS, :]] + [vb[zt, p, SLOTS:, :]] * FOLD, axis=0)
                r = jnp.dot(left, right, preferred_element_type=jnp.float32)
                r = r[: 2 * ROWS] + r[2 * ROWS :]
                o[0, zt, p] = r[:ROWS]
                o[1, zt, p] = r[ROWS:]
            return carry

        lax.fori_loop(0, GROUP // 4, some, 0, unroll=2)

    def y1(n, zt):
        @pl.when(jnp.logical_not(active))
        def _():
            for h, y1_ in enumerate((ym, yp)):
                half = o.at[other_e, zt, pl.ds(h * (FIRST // 2), FIRST // 2)]
                send(half, yhf.at[n], yhs.at[h, n], yhr.at[n], y1=y1_)

    def y2(n, zt):
        wait(yhf.at[n], yhr.at[n])
        at = pl.ds(side * (FIRST // 2), FIRST // 2)
        o[near_e, zt, at] = o[near_e, zt, at] + yhf[n]
        send(o.at[near_e, zt, pl.ds(0, FIRST)], yff.at[side, n], yfs.at[n], yfr.at[side, n], y1=onward)

    def y3(n, zt):
        @pl.when(active)
        def _():
            for k in range(2):
                wait(yff.at[k, n], yfr.at[k, n])
            at = pl.ds(0, FIRST)
            o[other_e, zt, at] = o[other_e, zt, at] + (yff[0, n] + yff[1, n])

    def gview(e):
        def view(zt, far, k):
            return o.at[e, zt, pl.ds(FIRST + k * (REST // 2), REST // 2)] if far else o.at[e, zt, pl.ds(FIRST, REST)]

        return view

    def fview(zt, far, k):
        return o.at[other_e, zt, pl.ds(k * (FIRST // 2), FIRST // 2)] if far else o.at[other_e, zt, pl.ds(0, FIRST)]

    def gland(e):
        def land(i, k):
            return gzb.at[e, k, i, pl.ds(0, REST // 2)] if G_HOPS[i][0] == 4 else gzb.at[e, k, i]

        return land

    def fland(i, k):
        return fzb.at[k, i, pl.ds(0, FIRST // 2)] if F_HOPS[i][0] == 4 else fzb.at[k, i]

    def ahead(k, d):
        return mod(z + d, NZ) if k == 0 else mod(z - d, NZ)

    def ztake(view, land, rsem, hops, k, dist):
        for i, (far, d) in enumerate(hops):
            if d == dist:
                wait(land(i, k), rsem.at[k, i])
                into = view(ahead(k, d), far == 4, k)
                into[...] = into[...] + land(i, k)[...]

    def zpass(view, land, ssem, rsem, hops, k, i):
        far, d = hops[i]
        ztake(view, land, rsem, hops, k, far)
        send(view(ahead(k, far), far == 4, k), land(i, k), ssem.at[k, i], rsem.at[k, i], z1=ahead(k, far - d))

    def deliver(src, zt, slot_to, ssem, groups, z1, y1, local):
        for i in groups:
            x1, c1 = i // NC, i % NC
            piece = src.at[zt, pl.ds(i * BLOCKS, BLOCKS)]
            dst, rsem = fin.at[x, slot_to], finr.at[x, slot_to]
            if local:

                @pl.when(x * NC + c == i)
                def _():
                    pltpu.make_async_copy(piece, dst, rsem).start()

                @pl.when(x * NC + c != i)
                def _():
                    send(piece, dst, ssem.at[i], rsem, z1=z1, x1=x1, c1=c1, y1=y1)
            else:
                send(piece, dst, ssem.at[i], rsem, z1=z1, x1=x1, c1=c1, y1=y1)

    f_groups, g_groups = range(FIRST // BLOCKS), range(FIRST // BLOCKS, NX * NC)

    def f_pass(k, i):
        @pl.when(active)
        def _():
            far, d = F_HOPS[i]
            if d:
                zpass(fview, fland, fzs, fzr, F_HOPS, k, i)
            else:
                ztake(fview, fland, fzr, F_HOPS, k, far)
                j = k * len(F_LAST) + F_LAST.index(i)
                deliver(o.at[other_e], ahead(k, far), 1 + j, ffs.at[j], f_groups, ahead(k, far), y, False)

    def f_own():
        @pl.when(active)
        def _():
            deliver(o.at[other_e], z, 0, fos, f_groups, z, y, True)

    def g_last():
        deliver(o.at[near_e], z, 1 + side, fns, g_groups, z, onward, False)

        @pl.when(active)
        def _():
            deliver(o.at[other_e], z, 0, fos, g_groups, z, y, True)

        @pl.when(jnp.logical_not(active))
        def _():
            deliver(o.at[other_e], z, 3, fos, g_groups, z, mod(y + 2, NY), False)

    def sent(n):
        z0 = mod(z + n, NZ)
        block, half = vb.at[z0, mine(x, c)], vb.at[z0, part(x, c, 0)]
        for k in range(6):
            wait(half, xs.at[k, z0])
        for k in range(4):
            wait(block, ss.at[k, z0])

        if n > 0:
            wait(block, vzs.at[z0])

        wait(ab.at[edge, z0, amp_half(0)], ayf.at[z0])

        @pl.when(active)
        def _():
            for k in range(2):
                wait(ab.at[edge, z0], ays.at[k, z0])

    def sent_first():
        piece = amp.at[:, pl.ds(0, ROWS), :]
        for d in range(1, NX):
            wait(piece, axs.at[d])

        @pl.when(c != home)
        def _():
            wait(piece, axs.at[0])


        @pl.when(active)
        def _():
            wait(ab.at[edge, z], azs.at[NZ])
            for d in (0, 1, -1, 2, -2, 3):
                wait(ab.at[edge, z], azs.at[mod(z - d, NZ)])

    chunk = [mod(z + d, NZ) for d in (4, 3, -3, 2, -2, 1, -1, 0)]

    def run(name, *a):
        if name == "R":
            residuals(chunk[a[0]])
            sent(a[0])
        elif name == "y1":
            y1(a[0], chunk[a[0]])
        elif name == "y2":
            y2(a[0], chunk[a[0]])
        elif name == "y3":
            y3(a[0], chunk[a[0]])
        elif name == "g":
            e, k, i = a
            zpass(gview(e), gland(e), gzs.at[e], gzr.at[e], G_HOPS, k, i)
        elif name == "gr":
            e, k = a
            ztake(gview(e), gland(e), gzr.at[e], G_HOPS, k, 0)
        elif name == "gfin":
            g_last()
        elif name == "f":
            f_pass(*a)
        elif name == "fown":
            f_own()

    for name, *a in ORDER:
        run(name, *a)
    sent_first()

    for n in range(NZ):

        @pl.when(jnp.logical_not(active))
        def _():
            wait(yhf.at[n], yhs.at[0, n])
            wait(yhf.at[n], yhs.at[1, n])

        wait(yff.at[0, n], yfs.at[n])
    for k in range(2):
        for i in range(len(G_HOPS)):
            for e in range(2):
                wait(gland(e)(i, k), gzs.at[e, k, i])
    piece = fin.at[0, 0]

    @pl.when(active)
    def _():
        for k in range(2):
            for i in range(len(F_HOPS)):
                if i not in F_LAST:
                    wait(fland(i, k), fzs.at[k, i])
        for j in range(2 * len(F_LAST)):
            for i in f_groups:
                wait(piece, ffs.at[j, i])
        for i in f_groups:

            @pl.when(x * NC + c != i)
            def _():
                wait(piece, fos.at[i])

    for i in g_groups:
        wait(piece, fns.at[i])

        @pl.when(jnp.logical_or(jnp.logical_not(active), x * NC + c != i))
        def _():
            wait(piece, fos.at[i])

    def collect(slots):
        for x0 in range(NX):
            for k in range(slots):
                wait(fin.at[x0, k], finr.at[x0, k])
            total = fin[x0, 0]
            for k in range(1, slots):
                total = total + fin[x0, k]
            out[:, x0 * ROWS : (x0 + 1) * ROWS, :] = total.astype(jnp.bfloat16)

    @pl.when(x * NC + c < FIRST // BLOCKS)
    def _():
        collect(1 + 2 * len(F_LAST))

    @pl.when(x * NC + c >= FIRST // BLOCKS)
    def _():
        collect(4)


def body(amplitudes, vectors, pair_count, tile_map):
    live = lax.broadcasted_iota(jnp.int32, (BLOCKS, 1, SLOTS), 2) < pair_count[:, None, None]
    f32, bf16 = jnp.float32, jnp.bfloat16
    dma = pltpu.SemaphoreType.DMA
    slots = max(4, 1 + 2 * len(F_LAST))
    out = pl.pallas_call(
        kernel,
        out_shape=jax.ShapeDtypeStruct(amplitudes.shape, bf16),
        in_specs=[
            pl.BlockSpec(memory_space=pltpu.VMEM),
            pl.BlockSpec(memory_space=pl.ANY),
            pl.BlockSpec(memory_space=pltpu.SMEM),
            pl.BlockSpec(memory_space=pltpu.VMEM),
        ],
        out_specs=pl.BlockSpec(memory_space=pltpu.VMEM),
        scratch_shapes=[
            pltpu.VMEM(amplitudes.shape, bf16),
            pltpu.VMEM((TOTAL, 2 * TOTAL), bf16),
            pltpu.VMEM((NZ, GROUP, DEPTH, SLOTS), bf16),
            pltpu.VMEM((2, NZ, GROUP, ROWS, SLOTS), bf16),
            pltpu.VMEM((2 * ROWS * PITCH, SLOTS), f32),
            pltpu.VMEM((8 * PITCH, SLOTS), f32),
            pltpu.VMEM((2 * ROWS * PITCH, SLOTS), f32),
            pltpu.VMEM((8 * PITCH, SLOTS), f32),
            pltpu.VMEM((2, NZ, GROUP, ROWS, SLOTS), f32),
            pltpu.VMEM((2, 2, 4, REST, ROWS, SLOTS), f32),
            pltpu.VMEM((2, 4, FIRST, ROWS, SLOTS), f32),
            pltpu.VMEM((NZ, FIRST // 2, ROWS, SLOTS), f32),
            pltpu.VMEM((2, NZ, FIRST, ROWS, SLOTS), f32),
            pltpu.VMEM((NX, slots, BLOCKS, ROWS, SLOTS), f32),
            dma((NZ,)), dma((NZ,)),
            dma((6, NZ)), dma((6, NZ)),
            dma((4, NZ)), dma((4, NZ)),
            dma((NX,)), dma((NX, NC)),
            dma((NZ + 1,)), dma((NZ,)),
            dma((2, NZ)), dma((NZ,)), dma((3, NZ)),
            dma((2, 2, 4)), dma((2, 2, 4)),
            dma((2, 4)), dma((2, 4)),
            dma((2, NZ)), dma((NZ,)),
            dma((NZ,)), dma((2, NZ)),
            dma((2 * len(F_LAST), NX * NC)), dma((NX * NC,)), dma((NX * NC,)),
            dma((NX, slots)),
        ],
        compiler_params=pltpu.CompilerParams(
            collective_id=0, has_side_effects=True, vmem_limit_bytes=60 * 2**20
        ),
        cost_estimate=pl.CostEstimate(flops=12 * 10**9, bytes_accessed=4 * 10**6, transcendentals=0),
    )(amplitudes, vectors, pair_count, tile_map.T)
    return jnp.where(live, out, jnp.zeros_like(out))


def solution(mesh):
    fine = Mesh(mesh.devices.reshape(NZ, NX, NC, NY), ("z", "x", "c", "y"))
    pair = ("z", "x", "c")
    return jax.shard_map(
        body,
        mesh=fine,
        in_specs=(P(pair, "y", None), P(pair, "y", None), P(pair), P()),
        out_specs=P(pair, "y", None),
        check_vma=False,
    )
```

```python
import jax
import jax.numpy as jnp
from jax import lax
from jax.experimental import pallas as pl
from jax.experimental.pallas import tpu as pltpu
from jax.sharding import Mesh, PartitionSpec as P

NZ, NX, NC, NY = 8, 4, 2, 4
BLOCKS = 4
GROUP = NX * NC * BLOCKS
TOTAL = NZ * GROUP
SLOTS = 128
DEPTH = 160
ROWS = 16
PITCH = TOTAL + 8
FOLD = SLOTS // (DEPTH - SLOTS)
AHEAD = 3
FIRST = 20
REST = GROUP - FIRST
G_HOPS = ((4, 2), (3, 2), (2, 1), (1, 0))
F_HOPS = ((4, 2), (3, 2), (2, 0), (1, 0))
F_LAST = tuple(i for i, (_, d) in enumerate(F_HOPS) if d == 0)
ORDER = (
    ("R", 0), ("g", 0, 0, 0), ("g", 0, 1, 0), ("g", 1, 0, 0), ("g", 1, 1, 0), ("y1", 0),
    ("R", 1), ("g", 0, 0, 1), ("g", 1, 0, 1), ("y1", 1), ("R", 2), ("g", 0, 1, 1),
    ("g", 1, 1, 1), ("y1", 2), ("R", 3), ("y1", 3), ("R", 4), ("y2", 0),
    ("y1", 4), ("R", 5), ("y2", 1), ("y1", 5), ("R", 6), ("y2", 2),
    ("y1", 6), ("R", 7), ("y2", 3), ("y1", 7), ("g", 0, 0, 2), ("g", 0, 1, 2),
    ("y3", 0), ("f", 0, 0), ("f", 1, 0), ("y2", 4), ("g", 1, 0, 2), ("g", 1, 1, 2),
    ("y3", 1), ("f", 0, 1), ("y2", 5), ("g", 0, 0, 3), ("g", 0, 1, 3), ("y3", 2),
    ("f", 1, 1), ("y2", 6), ("y3", 3), ("g", 1, 0, 3), ("g", 1, 1, 3), ("y2", 7),
    ("f", 0, 2), ("y3", 4), ("gr", 0, 1), ("y3", 5), ("f", 0, 3), ("f", 1, 2),
    ("gr", 0, 0), ("y3", 6), ("f", 1, 3), ("gr", 1, 0), ("gr", 1, 1), ("gfin",),
    ("y3", 7), ("fown",),
)


def split(x):
    hi = x.astype(jnp.bfloat16)
    return hi, (x - hi.astype(jnp.float32)).astype(jnp.bfloat16)


def wait(view, sem):
    pltpu.make_async_copy(view, view, sem).wait()


def kernel(
    amp_in, vec, counts, tiles_in, out,
    amp, tiles, near, vb, ab, w, wt, u, ut, o, gzb, fzb, yhf, yff, fin,
    vzs, vzr, xs, xr, ss, sr, axs, axr, azs, azr, ays, ayf, ayr,
    gzs, gzr, fzs, fzr, yhs, yhr, yfs, yfr, ffs, fos, fns, finr, loads,
):
    z, x, c, y = (lax.axis_index(a) for a in ("z", "x", "c", "y"))

    def mod(a, n):
        return lax.rem(a + 4 * n, n)

    def send(src, dst, ssem, rsem, z1=z, x1=x, c1=c, y1=y):
        pltpu.make_async_remote_copy(
            src_ref=src, dst_ref=dst, send_sem=ssem, recv_sem=rsem,
            device_id=(z1, x1, c1, y1), device_id_type=pl.DeviceIdType.MESH,
        ).start()

    def away_from(s):
        return jnp.where(lax.rem(s, 2) == 1, lax.div(s + 1, 2), -lax.div(s, 2))

    def source(s):
        return mod(z - away_from(s), NZ)

    zp, zm = mod(z + 1, NZ), mod(z - 1, NZ)
    xp, xm, xo = mod(x + 1, NX), mod(x - 1, NX), mod(x + 2, NX)
    yp, ym = mod(y + 1, NY), mod(y - 1, NY)
    mate = 1 - c
    home, edge = lax.div(y, 2), lax.rem(y, 2)
    active = c == home

    def mine(x0, c0):
        return pl.ds(pl.multiple_of(x0 * (NC * BLOCKS) + c0 * BLOCKS, BLOCKS), BLOCKS)

    def part(x0, c0, h):
        return pl.ds(x0 * (NC * BLOCKS) + c0 * BLOCKS + 2 * h, 2)

    def rows(z1):
        return pl.ds(pl.multiple_of(z1 * DEPTH, DEPTH), DEPTH)

    own = pltpu.make_async_copy(vec.at[:, rows(z), :], vb.at[z, mine(x, c)], vzr.at[z])
    load_amp = pltpu.make_async_copy(amp_in, amp, loads.at[0])
    load_amp.start()
    own.start()
    load_tiles = pltpu.make_async_copy(tiles_in, tiles, loads.at[1])
    load_tiles.start()
    barrier = pltpu.get_barrier_semaphore()
    slot = lax.broadcasted_iota(jnp.int32, (NX * ROWS, SLOTS), 1)

    def greet(z1=z, x1=x, c1=c, y1=y):
        pl.semaphore_signal(barrier, inc=1, device_id=(z1, x1, c1, y1), device_id_type=pl.DeviceIdType.MESH)

    for d in range(1, NZ):
        greet(z1=mod(z + d, NZ))
    for d in range(NX):
        for e in range(NC):
            if d or e:
                greet(x1=mod(x + d, NX), c1=mod(c + e, NC))
    for d in range(1, NY):
        greet(y1=mod(y + d, NY))
    load_amp.wait()
    for b in range(BLOCKS):
        amp[b] = jnp.where(slot < counts[b], amp[b], jnp.zeros_like(amp[b]))
    block_row = lax.broadcasted_iota(jnp.int32, (GROUP, TOTAL), 0)

    load_tiles.wait()

    def adjacency(n, carry):
        block_of = block_row + source(n) * GROUP
        found = jnp.zeros((GROUP, TOTAL), jnp.float32)
        for j in range(tiles.shape[0]):
            found = found + jnp.where(tiles[j : j + 1, :] == block_of, 1.0, 0.0)
        for h in range(2):
            u[pl.ds(pl.multiple_of(h * TOTAL + n * GROUP, GROUP), GROUP), :] = found[:, h * SLOTS : (h + 1) * SLOTS]
        return carry

    lax.fori_loop(0, NZ, adjacency, 0)
    for h in range(2):
        found = u[h * TOTAL : (h + 1) * TOTAL, :].T.astype(jnp.bfloat16)
        for k in range(4):
            near[h * SLOTS : (h + 1) * SLOTS, k * SLOTS : (k + 1) * SLOTS] = found[:, k // 2 * SLOTS : (k // 2 + 1) * SLOTS]
    pl.semaphore_wait(barrier, NZ - 1 + NX * NC - 1 + NY - 1)

    for d in range(NX):
        x1 = mod(x + d, NX)
        src = amp.at[:, pl.ds(pl.multiple_of(x1 * ROWS, ROWS), ROWS), :]
        dst = ab.at[edge, z, mine(x, c)]
        if d:
            send(src, dst, axs.at[d], axr.at[x, c], x1=x1, c1=home)
        else:

            @pl.when(active)
            def _():
                pltpu.make_async_copy(src, dst, axr.at[x, c]).start()

            @pl.when(c != home)
            def _():
                send(src, dst, axs.at[0], axr.at[x, c], c1=home)

    def hand_out(s):
        z1 = mod(z + away_from(s), NZ)
        send(vec.at[:, rows(z1), :], vb.at[z, mine(x, c)], vzs.at[z1], vzr.at[z], z1=z1)

    around = mod(y - 2 * c, NY)
    near_e, other_e = 1 - lax.rem(around, 2), lax.rem(around, 2)
    behind = jnp.logical_or(around == 0, around == 3)
    side = jnp.where(behind, 1, 0)
    onward, away = jnp.where(behind, yp, ym), jnp.where(behind, ym, yp)

    def amp_half(h):
        return pl.ds(pl.multiple_of(h * (GROUP // 2), GROUP // 2), GROUP // 2)

    def spread_amp(z0):
        block = ab.at[other_e, z0]
        send(block, block, ays.at[0, z0], ayr.at[0, z0], y1=yp)
        send(block, block, ays.at[1, z0], ayr.at[0, z0], y1=ym)

    def products(s, z0, x0, c0):
        for b in range(BLOCKS):
            q = x0 * (NC * BLOCKS) + c0 * BLOCKS + b
            a = jnp.concatenate([ab[0, z0, q], ab[1, z0, q]], axis=0)
            r = lax.dot_general(a, vb[z0, q], (((1,), (1,)), ((), ())), preferred_element_type=jnp.float32)
            w[pl.ds(s * GROUP + q, 2 * ROWS, stride=PITCH), :] = r[:, :SLOTS]
            tail = [r[m * 8 : m * 8 + 8, SLOTS:] for m in range(FOLD)]
            wt[pl.ds(s * GROUP + q, 8, stride=PITCH), :] = jnp.concatenate(tail, axis=1)

    def mix(src, dst, half):
        def some(i, carry):
            at = [pl.multiple_of((2 * i + h) * PITCH, 8) for h in range(2)]
            hi, lo = split(jnp.concatenate([src[pl.ds(a + half * SLOTS, SLOTS), :] for a in at], axis=1))
            pairs = near[:, half * TOTAL : (half + 1) * TOTAL]
            r = jnp.dot(pairs, jnp.concatenate([hi, lo], axis=0), preferred_element_type=jnp.float32)
            for h in range(2):
                to = pl.ds(at[h], TOTAL)
                part_sum = r[:, h * SLOTS : (h + 1) * SLOTS]
                dst[to, :] = dst[to, :] + part_sum if half else part_sum
            return carry

        lax.fori_loop(0, src.shape[0] // PITCH // 2, some, 0, unroll=8 if src.shape[0] == 2 * ROWS * PITCH else 4)

    def spread(z0):
        block = vb.at[z0, mine(x, c)]
        ha, hb = vb.at[z0, part(x, c, 0)], vb.at[z0, part(x, c, 1)]
        send(ha, ha, xs.at[0, z0], xr.at[0, z0], x1=xp)
        send(hb, hb, xs.at[1, z0], xr.at[1, z0], x1=xm)
        send(hb, hb, xs.at[4, z0], xr.at[4, z0], x1=xp)
        send(ha, ha, xs.at[5, z0], xr.at[5, z0], x1=xm)
        send(block, block, ss.at[0, z0], sr.at[0, z0], c1=mate)

    wait(vb.at[z, mine(x, c)], vzr.at[z])
    spread(z)

    def hand_first():
        for n in range(1, AHEAD + 1):
            hand_out(jnp.int32(n))

    @pl.when(jnp.logical_not(active))
    def _():
        hand_first()

    @pl.when(active)
    def _():
        for x0 in range(NX):
            for c0 in range(NC):
                wait(ab.at[edge, z, mine(x0, c0)], axr.at[x0, c0])
        block = ab.at[edge, z]
        send(block, block, azs.at[z], azr.at[z], z1=zp)
        send(block, block, azs.at[NZ], azr.at[z], z1=zm)
        spread_amp(z)
        hand_first()

    def step(s, carry):
        @pl.when(jnp.logical_and(jnp.logical_and(s >= 1, s < NZ), active))
        def _():
            z0 = source(s)
            block = ab.at[edge, z0]
            wait(block, azr.at[z0])

            @pl.when(s < NZ - 2)
            def _():
                send(block, block, azs.at[z0], azr.at[z0], z1=jnp.where(lax.rem(s, 2) == 1, zp, zm))

            spread_amp(z0)

        @pl.when(jnp.logical_and(s >= 1, s < NZ + 1))
        def _():
            z0 = source(s - 1)
            wait(ab.at[near_e, z0], ayr.at[0, z0])
            half = ab.at[near_e, z0, amp_half(side)]
            send(half, half, ayf.at[z0], ayr.at[1 + side, z0], y1=away)

        @pl.when(jnp.logical_and(s >= 1, s < NZ))
        def _():
            z0 = source(s)
            wait(vb.at[z0, mine(x, c)], vzr.at[z0])

            @pl.when(s < NZ - AHEAD)
            def _():
                hand_out(s + AHEAD)

            spread(z0)

        @pl.when(jnp.logical_and(s >= 1, s < NZ + 1))
        def _():
            z0 = source(s - 1)
            left, right = vb.at[z0, mine(xm, c)], vb.at[z0, mine(xp, c)]
            half = vb.at[z0, part(xm, c, 0)]
            wait(half, xr.at[0, z0])
            send(half, half, xs.at[2, z0], xr.at[2, z0], x1=xp)
            half = vb.at[z0, part(xp, c, 1)]
            wait(half, xr.at[1, z0])
            send(half, half, xs.at[3, z0], xr.at[3, z0], x1=xm)
            wait(vb.at[z0, part(xm, c, 1)], xr.at[4, z0])
            send(left, left, ss.at[1, z0], sr.at[1, z0], c1=mate)
            wait(vb.at[z0, part(xp, c, 0)], xr.at[5, z0])
            send(right, right, ss.at[2, z0], sr.at[2, z0], c1=mate)

        @pl.when(jnp.logical_and(s >= 2, s < NZ + 2))
        def _():
            z0 = source(s - 2)

            wait(vb.at[z0, part(xo, c, 0)], xr.at[2, z0])
            wait(vb.at[z0, part(xo, c, 1)], xr.at[3, z0])
            block = vb.at[z0, mine(xo, c)]
            send(block, block, ss.at[3, z0], sr.at[3, z0], c1=mate)

            @pl.when(jnp.logical_not(active))
            def _():
                for h in range(2):
                    wait(ab.at[other_e, z0, amp_half(h)], ayr.at[1 + h, z0])

            for x0 in (x, xm, xp):
                products(s - 2, z0, x0, c)
            wait(vb.at[z0, mine(x, mate)], sr.at[0, z0])
            products(s - 2, z0, x, mate)
            products(s - 2, z0, xo, c)
            for k, x0 in ((1, xm), (2, xp)):
                wait(vb.at[z0, mine(x0, mate)], sr.at[k, z0])
                products(s - 2, z0, x0, mate)

        @pl.when(s >= 3)
        def _():
            z0 = source(s - 3)
            wait(vb.at[z0, mine(xo, mate)], sr.at[3, z0])
            products(s - 3, z0, xo, mate)

        @pl.when(s == NZ - 1)
        def _():
            mix(w, u, 0)
            mix(wt, ut, 0)

        return carry

    lax.fori_loop(0, NZ + 3, step, 0)

    mix(w, u, 1)
    mix(wt, ut, 1)
    row = lax.broadcasted_iota(jnp.int32, (2 * ROWS, SLOTS), 0)
    lane = lax.broadcasted_iota(jnp.int32, (2 * ROWS, SLOTS), 1)
    own_fold = lax.div(row, 8) == lax.div(lane, DEPTH - SLOTS)

    def residuals(zt):
        def some(n, carry):
            for step_in in range(4):
                p = n * 4 + step_in
                full = u[pl.ds(zt * GROUP + p, 2 * ROWS, stride=PITCH), :]
                tail = jnp.concatenate([ut[pl.ds(zt * GROUP + p, 8, stride=PITCH), :]] * FOLD, axis=0)
                u2 = jnp.concatenate([full, jnp.where(own_fold, tail, 0.0)], axis=1)
                left = jnp.concatenate(split(u2), axis=0)
                right = jnp.concatenate([vb[zt, p, :SLOTS, :]] + [vb[zt, p, SLOTS:, :]] * FOLD, axis=0)
                r = jnp.dot(left, right, preferred_element_type=jnp.float32)
                r = r[: 2 * ROWS] + r[2 * ROWS :]
                o[0, zt, p] = r[:ROWS]
                o[1, zt, p] = r[ROWS:]
            return carry

        lax.fori_loop(0, GROUP // 4, some, 0, unroll=2)

    def y1(n, zt):
        @pl.when(jnp.logical_not(active))
        def _():
            for h, y1_ in enumerate((ym, yp)):
                half = o.at[other_e, zt, pl.ds(h * (FIRST // 2), FIRST // 2)]
                send(half, yhf.at[n], yhs.at[h, n], yhr.at[n], y1=y1_)

    def y2(n, zt):
        wait(yhf.at[n], yhr.at[n])
        at = pl.ds(side * (FIRST // 2), FIRST // 2)
        o[near_e, zt, at] = o[near_e, zt, at] + yhf[n]
        send(o.at[near_e, zt, pl.ds(0, FIRST)], yff.at[side, n], yfs.at[n], yfr.at[side, n], y1=onward)

    def y3(n, zt):
        @pl.when(active)
        def _():
            for k in range(2):
                wait(yff.at[k, n], yfr.at[k, n])
            at = pl.ds(0, FIRST)
            o[other_e, zt, at] = o[other_e, zt, at] + (yff[0, n] + yff[1, n])

    def gview(e):
        def view(zt, far, k):
            return o.at[e, zt, pl.ds(FIRST + k * (REST // 2), REST // 2)] if far else o.at[e, zt, pl.ds(FIRST, REST)]

        return view

    def fview(zt, far, k):
        return o.at[other_e, zt, pl.ds(k * (FIRST // 2), FIRST // 2)] if far else o.at[other_e, zt, pl.ds(0, FIRST)]

    def gland(e):
        def land(i, k):
            return gzb.at[e, k, i, pl.ds(0, REST // 2)] if G_HOPS[i][0] == 4 else gzb.at[e, k, i]

        return land

    def fland(i, k):
        return fzb.at[k, i, pl.ds(0, FIRST // 2)] if F_HOPS[i][0] == 4 else fzb.at[k, i]

    def ahead(k, d):
        return mod(z + d, NZ) if k == 0 else mod(z - d, NZ)

    def ztake(view, land, rsem, hops, k, dist):
        for i, (far, d) in enumerate(hops):
            if d == dist:
                wait(land(i, k), rsem.at[k, i])
                into = view(ahead(k, d), far == 4, k)
                into[...] = into[...] + land(i, k)[...]

    def zpass(view, land, ssem, rsem, hops, k, i):
        far, d = hops[i]
        ztake(view, land, rsem, hops, k, far)
        send(view(ahead(k, far), far == 4, k), land(i, k), ssem.at[k, i], rsem.at[k, i], z1=ahead(k, far - d))

    def deliver(src, zt, slot_to, ssem, groups, z1, y1, local):
        for i in groups:
            x1, c1 = i // NC, i % NC
            piece = src.at[zt, pl.ds(i * BLOCKS, BLOCKS)]
            dst, rsem = fin.at[x, slot_to], finr.at[x, slot_to]
            if local:

                @pl.when(x * NC + c == i)
                def _():
                    pltpu.make_async_copy(piece, dst, rsem).start()

                @pl.when(x * NC + c != i)
                def _():
                    send(piece, dst, ssem.at[i], rsem, z1=z1, x1=x1, c1=c1, y1=y1)
            else:
                send(piece, dst, ssem.at[i], rsem, z1=z1, x1=x1, c1=c1, y1=y1)

    f_groups, g_groups = range(FIRST // BLOCKS), range(FIRST // BLOCKS, NX * NC)

    def f_pass(k, i):
        @pl.when(active)
        def _():
            far, d = F_HOPS[i]
            if d:
                zpass(fview, fland, fzs, fzr, F_HOPS, k, i)
            else:
                ztake(fview, fland, fzr, F_HOPS, k, far)
                j = k * len(F_LAST) + F_LAST.index(i)
                deliver(o.at[other_e], ahead(k, far), 1 + j, ffs.at[j], f_groups, ahead(k, far), y, False)

    def f_own():
        @pl.when(active)
        def _():
            deliver(o.at[other_e], z, 0, fos, f_groups, z, y, True)

    def g_last():
        deliver(o.at[near_e], z, 1 + side, fns, g_groups, z, onward, False)

        @pl.when(active)
        def _():
            deliver(o.at[other_e], z, 0, fos, g_groups, z, y, True)

        @pl.when(jnp.logical_not(active))
        def _():
            deliver(o.at[other_e], z, 3, fos, g_groups, z, mod(y + 2, NY), False)

    def sent(n):
        z0 = mod(z + n, NZ)
        block, half = vb.at[z0, mine(x, c)], vb.at[z0, part(x, c, 0)]
        for k in range(6):
            wait(half, xs.at[k, z0])
        for k in range(4):
            wait(block, ss.at[k, z0])

        if n > 0:
            wait(block, vzs.at[z0])

        wait(ab.at[edge, z0, amp_half(0)], ayf.at[z0])

        @pl.when(active)
        def _():
            for k in range(2):
                wait(ab.at[edge, z0], ays.at[k, z0])

    def sent_first():
        piece = amp.at[:, pl.ds(0, ROWS), :]
        for d in range(1, NX):
            wait(piece, axs.at[d])

        @pl.when(c != home)
        def _():
            wait(piece, axs.at[0])


        @pl.when(active)
        def _():
            wait(ab.at[edge, z], azs.at[NZ])
            for d in (0, 1, -1, 2, -2, 3):
                wait(ab.at[edge, z], azs.at[mod(z - d, NZ)])

    chunk = [mod(z + d, NZ) for d in (4, 3, -3, 2, -2, 1, -1, 0)]

    def run(name, *a):
        if name == "R":
            residuals(chunk[a[0]])
            sent(a[0])
        elif name == "y1":
            y1(a[0], chunk[a[0]])
        elif name == "y2":
            y2(a[0], chunk[a[0]])
        elif name == "y3":
            y3(a[0], chunk[a[0]])
        elif name == "g":
            e, k, i = a
            zpass(gview(e), gland(e), gzs.at[e], gzr.at[e], G_HOPS, k, i)
        elif name == "gr":
            e, k = a
            ztake(gview(e), gland(e), gzr.at[e], G_HOPS, k, 0)
        elif name == "gfin":
            g_last()
        elif name == "f":
            f_pass(*a)
        elif name == "fown":
            f_own()

    for name, *a in ORDER:
        run(name, *a)
    sent_first()

    for n in range(NZ):

        @pl.when(jnp.logical_not(active))
        def _():
            wait(yhf.at[n], yhs.at[0, n])
            wait(yhf.at[n], yhs.at[1, n])

        wait(yff.at[0, n], yfs.at[n])
    for k in range(2):
        for i in range(len(G_HOPS)):
            for e in range(2):
                wait(gland(e)(i, k), gzs.at[e, k, i])
    piece = fin.at[0, 0]

    @pl.when(active)
    def _():
        for k in range(2):
            for i in range(len(F_HOPS)):
                if i not in F_LAST:
                    wait(fland(i, k), fzs.at[k, i])
        for j in range(2 * len(F_LAST)):
            for i in f_groups:
                wait(piece, ffs.at[j, i])
        for i in f_groups:

            @pl.when(x * NC + c != i)
            def _():
                wait(piece, fos.at[i])

    for i in g_groups:
        wait(piece, fns.at[i])

        @pl.when(jnp.logical_or(jnp.logical_not(active), x * NC + c != i))
        def _():
            wait(piece, fos.at[i])

    def collect(slots):
        for x0 in range(NX):
            for k in range(slots):
                wait(fin.at[x0, k], finr.at[x0, k])
            total = fin[x0, 0]
            for k in range(1, slots):
                total = total + fin[x0, k]
            out[:, x0 * ROWS : (x0 + 1) * ROWS, :] = total.astype(jnp.bfloat16)

    @pl.when(x * NC + c < FIRST // BLOCKS)
    def _():
        collect(1 + 2 * len(F_LAST))

    @pl.when(x * NC + c >= FIRST // BLOCKS)
    def _():
        collect(4)


def body(amplitudes, vectors, pair_count, tile_map):
    live = lax.broadcasted_iota(jnp.int32, (BLOCKS, 1, SLOTS), 2) < pair_count[:, None, None]
    f32, bf16 = jnp.float32, jnp.bfloat16
    dma = pltpu.SemaphoreType.DMA
    slots = max(4, 1 + 2 * len(F_LAST))
    out = pl.pallas_call(
        kernel,
        out_shape=jax.ShapeDtypeStruct(amplitudes.shape, bf16),
        in_specs=[
            pl.BlockSpec(memory_space=pl.ANY),
            pl.BlockSpec(memory_space=pl.ANY),
            pl.BlockSpec(memory_space=pltpu.SMEM),
            pl.BlockSpec(memory_space=pl.ANY),
        ],
        out_specs=pl.BlockSpec(memory_space=pltpu.VMEM),
        scratch_shapes=[
            pltpu.VMEM(amplitudes.shape, bf16),
            pltpu.VMEM(tile_map.shape[::-1], jnp.int32),
            pltpu.VMEM((TOTAL, 2 * TOTAL), bf16),
            pltpu.VMEM((NZ, GROUP, DEPTH, SLOTS), bf16),
            pltpu.VMEM((2, NZ, GROUP, ROWS, SLOTS), bf16),
            pltpu.VMEM((2 * ROWS * PITCH, SLOTS), f32),
            pltpu.VMEM((8 * PITCH, SLOTS), f32),
            pltpu.VMEM((2 * ROWS * PITCH, SLOTS), f32),
            pltpu.VMEM((8 * PITCH, SLOTS), f32),
            pltpu.VMEM((2, NZ, GROUP, ROWS, SLOTS), f32),
            pltpu.VMEM((2, 2, 4, REST, ROWS, SLOTS), f32),
            pltpu.VMEM((2, 4, FIRST, ROWS, SLOTS), f32),
            pltpu.VMEM((NZ, FIRST // 2, ROWS, SLOTS), f32),
            pltpu.VMEM((2, NZ, FIRST, ROWS, SLOTS), f32),
            pltpu.VMEM((NX, slots, BLOCKS, ROWS, SLOTS), f32),
            dma((NZ,)), dma((NZ,)),
            dma((6, NZ)), dma((6, NZ)),
            dma((4, NZ)), dma((4, NZ)),
            dma((NX,)), dma((NX, NC)),
            dma((NZ + 1,)), dma((NZ,)),
            dma((2, NZ)), dma((NZ,)), dma((3, NZ)),
            dma((2, 2, 4)), dma((2, 2, 4)),
            dma((2, 4)), dma((2, 4)),
            dma((2, NZ)), dma((NZ,)),
            dma((NZ,)), dma((2, NZ)),
            dma((2 * len(F_LAST), NX * NC)), dma((NX * NC,)), dma((NX * NC,)),
            dma((NX, slots)),
            dma((2,)),
        ],
        compiler_params=pltpu.CompilerParams(
            collective_id=0, has_side_effects=True, vmem_limit_bytes=60 * 2**20
        ),
        cost_estimate=pl.CostEstimate(flops=12 * 10**9, bytes_accessed=4 * 10**6, transcendentals=0),
    )(amplitudes, vectors, pair_count, tile_map.T)
    return jnp.where(live, out, jnp.zeros_like(out))


def solution(mesh):
    fine = Mesh(mesh.devices.reshape(NZ, NX, NC, NY), ("z", "x", "c", "y"))
    pair = ("z", "x", "c")
    return jax.shard_map(
        body,
        mesh=fine,
        in_specs=(P(pair, "y", None), P(pair, "y", None), P(pair), P()),
        out_specs=P(pair, "y", None),
        check_vma=False,
    )
```

```python
import jax
import jax.numpy as jnp
from jax import lax
from jax.experimental import pallas as pl
from jax.experimental.pallas import tpu as pltpu
from jax.sharding import Mesh, PartitionSpec as P

NZ, NX, NC, NY = 8, 4, 2, 4
BLOCKS = 4
GROUP = NX * NC * BLOCKS
TOTAL = NZ * GROUP
SLOTS = 128
DEPTH = 160
ROWS = 16
PITCH = TOTAL + 8
FOLD = SLOTS // (DEPTH - SLOTS)
AHEAD = 3
FIRST = 20
REST = GROUP - FIRST
G_HOPS = ((4, 2), (3, 2), (2, 1), (1, 0))
F_HOPS = ((4, 2), (3, 2), (2, 0), (1, 0))
F_LAST = tuple(i for i, (_, d) in enumerate(F_HOPS) if d == 0)
ORDER = (
    ("R", 0), ("g", 0, 0, 0), ("g", 0, 1, 0), ("g", 1, 0, 0), ("g", 1, 1, 0), ("y1", 0),
    ("R", 1), ("g", 0, 0, 1), ("g", 1, 0, 1), ("y1", 1), ("R", 2), ("g", 0, 1, 1),
    ("g", 1, 1, 1), ("y1", 2), ("R", 3), ("y1", 3), ("R", 4), ("y2", 0),
    ("y1", 4), ("R", 5), ("y2", 1), ("y1", 5), ("R", 6), ("y2", 2),
    ("y1", 6), ("R", 7), ("y2", 3), ("y1", 7), ("g", 0, 0, 2), ("g", 0, 1, 2),
    ("y3", 0), ("f", 0, 0), ("f", 1, 0), ("y2", 4), ("g", 1, 0, 2), ("g", 1, 1, 2),
    ("y3", 1), ("f", 0, 1), ("y2", 5), ("g", 0, 0, 3), ("g", 0, 1, 3), ("y3", 2),
    ("f", 1, 1), ("y2", 6), ("y3", 3), ("g", 1, 0, 3), ("g", 1, 1, 3), ("y2", 7),
    ("f", 0, 2), ("y3", 4), ("gr", 0, 1), ("y3", 5), ("f", 0, 3), ("f", 1, 2),
    ("gr", 0, 0), ("y3", 6), ("f", 1, 3), ("gr", 1, 0), ("gr", 1, 1), ("gfin",),
    ("y3", 7), ("fown",),
)


def split(x):
    hi = x.astype(jnp.bfloat16)
    return hi, (x - hi.astype(jnp.float32)).astype(jnp.bfloat16)


def wait(view, sem):
    pltpu.make_async_copy(view, view, sem).wait()


def kernel(
    amp_in, vec, counts, tiles_in, out,
    amp, tiles, near, vb, ab, w, wt, u, ut, o, gzb, fzb, yhf, yff, fin,
    vzs, vzr, xs, xr, ss, sr, axs, axr, azs, azr, ays, ayf, ayr,
    gzs, gzr, fzs, fzr, yhs, yhr, yfs, yfr, ffs, fos, fns, finr, loads,
):
    z, x, c, y = (lax.axis_index(a) for a in ("z", "x", "c", "y"))

    def mod(a, n):
        return lax.rem(a + 4 * n, n)

    def send(src, dst, ssem, rsem, z1=z, x1=x, c1=c, y1=y):
        pltpu.make_async_remote_copy(
            src_ref=src, dst_ref=dst, send_sem=ssem, recv_sem=rsem,
            device_id=(z1, x1, c1, y1), device_id_type=pl.DeviceIdType.MESH,
        ).start()

    def away_from(s):
        return jnp.where(lax.rem(s, 2) == 1, lax.div(s + 1, 2), -lax.div(s, 2))

    def source(s):
        return mod(z - away_from(s), NZ)

    zp, zm = mod(z + 1, NZ), mod(z - 1, NZ)
    xp, xm, xo = mod(x + 1, NX), mod(x - 1, NX), mod(x + 2, NX)
    yp, ym = mod(y + 1, NY), mod(y - 1, NY)
    mate = 1 - c
    home, edge = lax.div(y, 2), lax.rem(y, 2)
    active = c == home

    def mine(x0, c0):
        return pl.ds(pl.multiple_of(x0 * (NC * BLOCKS) + c0 * BLOCKS, BLOCKS), BLOCKS)

    def part(x0, c0, h):
        return pl.ds(x0 * (NC * BLOCKS) + c0 * BLOCKS + 2 * h, 2)

    def rows(z1):
        return pl.ds(pl.multiple_of(z1 * DEPTH, DEPTH), DEPTH)

    own = pltpu.make_async_copy(vec.at[:, rows(z), :], vb.at[z, mine(x, c)], vzr.at[z])
    load_amp = pltpu.make_async_copy(amp_in, amp, loads.at[0])
    load_amp.start()
    own.start()
    load_tiles = pltpu.make_async_copy(tiles_in, tiles, loads.at[1])
    load_tiles.start()
    barrier = pltpu.get_barrier_semaphore()
    slot = lax.broadcasted_iota(jnp.int32, (NX * ROWS, SLOTS), 1)

    def greet(z1=z, x1=x, c1=c, y1=y):
        pl.semaphore_signal(barrier, inc=1, device_id=(z1, x1, c1, y1), device_id_type=pl.DeviceIdType.MESH)

    for d in range(1, NZ):
        greet(z1=mod(z + d, NZ))
    for d in range(NX):
        for e in range(NC):
            if d or e:
                greet(x1=mod(x + d, NX), c1=mod(c + e, NC))
    for d in range(1, NY):
        greet(y1=mod(y + d, NY))
    load_amp.wait()
    for b in range(BLOCKS):
        amp[b] = jnp.where(slot < counts[b], amp[b], jnp.zeros_like(amp[b]))
    block_row = lax.broadcasted_iota(jnp.int32, (GROUP, TOTAL), 0)

    load_tiles.wait()

    def adjacency(n, carry):
        block_of = block_row + source(n) * GROUP
        found = jnp.zeros((GROUP, TOTAL), jnp.float32)
        for j in range(tiles.shape[0]):
            found = found + jnp.where(tiles[j : j + 1, :] == block_of, 1.0, 0.0)
        for h in range(2):
            u[pl.ds(pl.multiple_of(h * TOTAL + n * GROUP, GROUP), GROUP), :] = found[:, h * SLOTS : (h + 1) * SLOTS]
        return carry

    lax.fori_loop(0, NZ, adjacency, 0)
    for h in range(2):
        found = u[h * TOTAL : (h + 1) * TOTAL, :].T.astype(jnp.bfloat16)
        for k in range(4):
            near[h * SLOTS : (h + 1) * SLOTS, k * SLOTS : (k + 1) * SLOTS] = found[:, k // 2 * SLOTS : (k // 2 + 1) * SLOTS]
    pl.semaphore_wait(barrier, NZ - 1 + NX * NC - 1 + NY - 1)

    for d in range(NX):
        x1 = mod(x + d, NX)
        src = amp.at[:, pl.ds(pl.multiple_of(x1 * ROWS, ROWS), ROWS), :]
        dst = ab.at[edge, z, mine(x, c)]
        if d:
            send(src, dst, axs.at[d], axr.at[x, c], x1=x1, c1=home)
        else:

            @pl.when(active)
            def _():
                pltpu.make_async_copy(src, dst, axr.at[x, c]).start()

            @pl.when(c != home)
            def _():
                send(src, dst, axs.at[0], axr.at[x, c], c1=home)

    def hand_out(s):
        z1 = mod(z + away_from(s), NZ)
        send(vec.at[:, rows(z1), :], vb.at[z, mine(x, c)], vzs.at[z1], vzr.at[z], z1=z1)

    around = mod(y - 2 * c, NY)
    near_e, other_e = 1 - lax.rem(around, 2), lax.rem(around, 2)
    behind = jnp.logical_or(around == 0, around == 3)
    side = jnp.where(behind, 1, 0)
    onward, away = jnp.where(behind, yp, ym), jnp.where(behind, ym, yp)

    def amp_half(h):
        return pl.ds(pl.multiple_of(h * (GROUP // 2), GROUP // 2), GROUP // 2)

    def spread_amp(z0):
        block = ab.at[other_e, z0]
        send(block, block, ays.at[0, z0], ayr.at[0, z0], y1=yp)
        send(block, block, ays.at[1, z0], ayr.at[0, z0], y1=ym)

    def products(s, z0, x0, c0):
        for b in range(BLOCKS):
            q = x0 * (NC * BLOCKS) + c0 * BLOCKS + b
            a = jnp.concatenate([ab[0, z0, q], ab[1, z0, q]], axis=0)
            r = lax.dot_general(a, vb[z0, q], (((1,), (1,)), ((), ())), preferred_element_type=jnp.float32)
            w[pl.ds(s * GROUP + q, 2 * ROWS, stride=PITCH), :] = r[:, :SLOTS]
            tail = [r[m * 8 : m * 8 + 8, SLOTS:] for m in range(FOLD)]
            wt[pl.ds(s * GROUP + q, 8, stride=PITCH), :] = jnp.concatenate(tail, axis=1)

    def mix(src, dst, half):
        def some(i, carry):
            at = [pl.multiple_of((2 * i + h) * PITCH, 8) for h in range(2)]
            hi, lo = split(jnp.concatenate([src[pl.ds(a + half * SLOTS, SLOTS), :] for a in at], axis=1))
            pairs = near[:, half * TOTAL : (half + 1) * TOTAL]
            r = jnp.dot(pairs, jnp.concatenate([hi, lo], axis=0), preferred_element_type=jnp.float32)
            for h in range(2):
                to = pl.ds(at[h], TOTAL)
                part_sum = r[:, h * SLOTS : (h + 1) * SLOTS]
                dst[to, :] = dst[to, :] + part_sum if half else part_sum
            return carry

        lax.fori_loop(0, src.shape[0] // PITCH // 2, some, 0, unroll=True)

    def spread(z0):
        block = vb.at[z0, mine(x, c)]
        ha, hb = vb.at[z0, part(x, c, 0)], vb.at[z0, part(x, c, 1)]
        send(ha, ha, xs.at[0, z0], xr.at[0, z0], x1=xp)
        send(hb, hb, xs.at[1, z0], xr.at[1, z0], x1=xm)
        send(hb, hb, xs.at[4, z0], xr.at[4, z0], x1=xp)
        send(ha, ha, xs.at[5, z0], xr.at[5, z0], x1=xm)
        send(block, block, ss.at[0, z0], sr.at[0, z0], c1=mate)

    wait(vb.at[z, mine(x, c)], vzr.at[z])
    spread(z)

    def hand_first():
        for n in range(1, AHEAD + 1):
            hand_out(jnp.int32(n))

    @pl.when(jnp.logical_not(active))
    def _():
        hand_first()

    @pl.when(active)
    def _():
        for x0 in range(NX):
            for c0 in range(NC):
                wait(ab.at[edge, z, mine(x0, c0)], axr.at[x0, c0])
        block = ab.at[edge, z]
        send(block, block, azs.at[z], azr.at[z], z1=zp)
        send(block, block, azs.at[NZ], azr.at[z], z1=zm)
        spread_amp(z)
        hand_first()

    def step(s, carry):
        @pl.when(jnp.logical_and(jnp.logical_and(s >= 1, s < NZ), active))
        def _():
            z0 = source(s)
            block = ab.at[edge, z0]
            wait(block, azr.at[z0])

            @pl.when(s < NZ - 2)
            def _():
                send(block, block, azs.at[z0], azr.at[z0], z1=jnp.where(lax.rem(s, 2) == 1, zp, zm))

            spread_amp(z0)

        @pl.when(jnp.logical_and(s >= 1, s < NZ + 1))
        def _():
            z0 = source(s - 1)
            wait(ab.at[near_e, z0], ayr.at[0, z0])
            half = ab.at[near_e, z0, amp_half(side)]
            send(half, half, ayf.at[z0], ayr.at[1 + side, z0], y1=away)

        @pl.when(jnp.logical_and(s >= 1, s < NZ))
        def _():
            z0 = source(s)
            wait(vb.at[z0, mine(x, c)], vzr.at[z0])

            @pl.when(s < NZ - AHEAD)
            def _():
                hand_out(s + AHEAD)

            spread(z0)

        @pl.when(jnp.logical_and(s >= 1, s < NZ + 1))
        def _():
            z0 = source(s - 1)
            left, right = vb.at[z0, mine(xm, c)], vb.at[z0, mine(xp, c)]
            half = vb.at[z0, part(xm, c, 0)]
            wait(half, xr.at[0, z0])
            send(half, half, xs.at[2, z0], xr.at[2, z0], x1=xp)
            half = vb.at[z0, part(xp, c, 1)]
            wait(half, xr.at[1, z0])
            send(half, half, xs.at[3, z0], xr.at[3, z0], x1=xm)
            wait(vb.at[z0, part(xm, c, 1)], xr.at[4, z0])
            send(left, left, ss.at[1, z0], sr.at[1, z0], c1=mate)
            wait(vb.at[z0, part(xp, c, 0)], xr.at[5, z0])
            send(right, right, ss.at[2, z0], sr.at[2, z0], c1=mate)

        @pl.when(jnp.logical_and(s >= 2, s < NZ + 2))
        def _():
            z0 = source(s - 2)

            wait(vb.at[z0, part(xo, c, 0)], xr.at[2, z0])
            wait(vb.at[z0, part(xo, c, 1)], xr.at[3, z0])
            block = vb.at[z0, mine(xo, c)]
            send(block, block, ss.at[3, z0], sr.at[3, z0], c1=mate)

            @pl.when(jnp.logical_not(active))
            def _():
                for h in range(2):
                    wait(ab.at[other_e, z0, amp_half(h)], ayr.at[1 + h, z0])

            for x0 in (x, xm, xp):
                products(s - 2, z0, x0, c)
            wait(vb.at[z0, mine(x, mate)], sr.at[0, z0])
            products(s - 2, z0, x, mate)
            products(s - 2, z0, xo, c)
            for k, x0 in ((1, xm), (2, xp)):
                wait(vb.at[z0, mine(x0, mate)], sr.at[k, z0])
                products(s - 2, z0, x0, mate)

        @pl.when(s >= 3)
        def _():
            z0 = source(s - 3)
            wait(vb.at[z0, mine(xo, mate)], sr.at[3, z0])
            products(s - 3, z0, xo, mate)

        @pl.when(s == NZ - 1)
        def _():
            mix(w, u, 0)
            mix(wt, ut, 0)

        return carry

    lax.fori_loop(0, NZ + 3, step, 0)

    mix(w, u, 1)
    mix(wt, ut, 1)
    row = lax.broadcasted_iota(jnp.int32, (2 * ROWS, SLOTS), 0)
    lane = lax.broadcasted_iota(jnp.int32, (2 * ROWS, SLOTS), 1)
    own_fold = lax.div(row, 8) == lax.div(lane, DEPTH - SLOTS)

    def residuals(zt):
        def some(n, carry):
            for step_in in range(4):
                p = n * 4 + step_in
                full = u[pl.ds(zt * GROUP + p, 2 * ROWS, stride=PITCH), :]
                tail = jnp.concatenate([ut[pl.ds(zt * GROUP + p, 8, stride=PITCH), :]] * FOLD, axis=0)
                u2 = jnp.concatenate([full, jnp.where(own_fold, tail, 0.0)], axis=1)
                left = jnp.concatenate(split(u2), axis=0)
                right = jnp.concatenate([vb[zt, p, :SLOTS, :]] + [vb[zt, p, SLOTS:, :]] * FOLD, axis=0)
                r = jnp.dot(left, right, preferred_element_type=jnp.float32)
                r = r[: 2 * ROWS] + r[2 * ROWS :]
                o[0, zt, p] = r[:ROWS]
                o[1, zt, p] = r[ROWS:]
            return carry

        lax.fori_loop(0, GROUP // 4, some, 0, unroll=2)

    def y1(n, zt):
        @pl.when(jnp.logical_not(active))
        def _():
            for h, y1_ in enumerate((ym, yp)):
                half = o.at[other_e, zt, pl.ds(h * (FIRST // 2), FIRST // 2)]
                send(half, yhf.at[n], yhs.at[h, n], yhr.at[n], y1=y1_)

    def y2(n, zt):
        wait(yhf.at[n], yhr.at[n])
        at = pl.ds(side * (FIRST // 2), FIRST // 2)
        o[near_e, zt, at] = o[near_e, zt, at] + yhf[n]
        send(o.at[near_e, zt, pl.ds(0, FIRST)], yff.at[side, n], yfs.at[n], yfr.at[side, n], y1=onward)

    def y3(n, zt):
        @pl.when(active)
        def _():
            for k in range(2):
                wait(yff.at[k, n], yfr.at[k, n])
            at = pl.ds(0, FIRST)
            o[other_e, zt, at] = o[other_e, zt, at] + (yff[0, n] + yff[1, n])

    def gview(e):
        def view(zt, far, k):
            return o.at[e, zt, pl.ds(FIRST + k * (REST // 2), REST // 2)] if far else o.at[e, zt, pl.ds(FIRST, REST)]

        return view

    def fview(zt, far, k):
        return o.at[other_e, zt, pl.ds(k * (FIRST // 2), FIRST // 2)] if far else o.at[other_e, zt, pl.ds(0, FIRST)]

    def gland(e):
        def land(i, k):
            return gzb.at[e, k, i, pl.ds(0, REST // 2)] if G_HOPS[i][0] == 4 else gzb.at[e, k, i]

        return land

    def fland(i, k):
        return fzb.at[k, i, pl.ds(0, FIRST // 2)] if F_HOPS[i][0] == 4 else fzb.at[k, i]

    def ahead(k, d):
        return mod(z + d, NZ) if k == 0 else mod(z - d, NZ)

    def ztake(view, land, rsem, hops, k, dist):
        for i, (far, d) in enumerate(hops):
            if d == dist:
                wait(land(i, k), rsem.at[k, i])
                into = view(ahead(k, d), far == 4, k)
                into[...] = into[...] + land(i, k)[...]

    def zpass(view, land, ssem, rsem, hops, k, i):
        far, d = hops[i]
        ztake(view, land, rsem, hops, k, far)
        send(view(ahead(k, far), far == 4, k), land(i, k), ssem.at[k, i], rsem.at[k, i], z1=ahead(k, far - d))

    def deliver(src, zt, slot_to, ssem, groups, z1, y1, local):
        for i in groups:
            x1, c1 = i // NC, i % NC
            piece = src.at[zt, pl.ds(i * BLOCKS, BLOCKS)]
            dst, rsem = fin.at[x, slot_to], finr.at[x, slot_to]
            if local:

                @pl.when(x * NC + c == i)
                def _():
                    pltpu.make_async_copy(piece, dst, rsem).start()

                @pl.when(x * NC + c != i)
                def _():
                    send(piece, dst, ssem.at[i], rsem, z1=z1, x1=x1, c1=c1, y1=y1)
            else:
                send(piece, dst, ssem.at[i], rsem, z1=z1, x1=x1, c1=c1, y1=y1)

    f_groups, g_groups = range(FIRST // BLOCKS), range(FIRST // BLOCKS, NX * NC)

    def f_pass(k, i):
        @pl.when(active)
        def _():
            far, d = F_HOPS[i]
            if d:
                zpass(fview, fland, fzs, fzr, F_HOPS, k, i)
            else:
                ztake(fview, fland, fzr, F_HOPS, k, far)
                j = k * len(F_LAST) + F_LAST.index(i)
                deliver(o.at[other_e], ahead(k, far), 1 + j, ffs.at[j], f_groups, ahead(k, far), y, False)

    def f_own():
        @pl.when(active)
        def _():
            deliver(o.at[other_e], z, 0, fos, f_groups, z, y, True)

    def g_last():
        deliver(o.at[near_e], z, 1 + side, fns, g_groups, z, onward, False)

        @pl.when(active)
        def _():
            deliver(o.at[other_e], z, 0, fos, g_groups, z, y, True)

        @pl.when(jnp.logical_not(active))
        def _():
            deliver(o.at[other_e], z, 3, fos, g_groups, z, mod(y + 2, NY), False)

    def sent(n):
        z0 = mod(z + n, NZ)
        block, half = vb.at[z0, mine(x, c)], vb.at[z0, part(x, c, 0)]
        for k in range(6):
            wait(half, xs.at[k, z0])
        for k in range(4):
            wait(block, ss.at[k, z0])

        if n > 0:
            wait(block, vzs.at[z0])

        wait(ab.at[edge, z0, amp_half(0)], ayf.at[z0])

        @pl.when(active)
        def _():
            for k in range(2):
                wait(ab.at[edge, z0], ays.at[k, z0])

    def sent_first():
        piece = amp.at[:, pl.ds(0, ROWS), :]
        for d in range(1, NX):
            wait(piece, axs.at[d])

        @pl.when(c != home)
        def _():
            wait(piece, axs.at[0])


        @pl.when(active)
        def _():
            wait(ab.at[edge, z], azs.at[NZ])
            for d in (0, 1, -1, 2, -2, 3):
                wait(ab.at[edge, z], azs.at[mod(z - d, NZ)])

    chunk = [mod(z + d, NZ) for d in (4, 3, -3, 2, -2, 1, -1, 0)]

    def run(name, *a):
        if name == "R":
            residuals(chunk[a[0]])
            sent(a[0])
        elif name == "y1":
            y1(a[0], chunk[a[0]])
        elif name == "y2":
            y2(a[0], chunk[a[0]])
        elif name == "y3":
            y3(a[0], chunk[a[0]])
        elif name == "g":
            e, k, i = a
            zpass(gview(e), gland(e), gzs.at[e], gzr.at[e], G_HOPS, k, i)
        elif name == "gr":
            e, k = a
            ztake(gview(e), gland(e), gzr.at[e], G_HOPS, k, 0)
        elif name == "gfin":
            g_last()
        elif name == "f":
            f_pass(*a)
        elif name == "fown":
            f_own()

    for name, *a in ORDER:
        run(name, *a)
    sent_first()

    for n in range(NZ):

        @pl.when(jnp.logical_not(active))
        def _():
            wait(yhf.at[n], yhs.at[0, n])
            wait(yhf.at[n], yhs.at[1, n])

        wait(yff.at[0, n], yfs.at[n])
    for k in range(2):
        for i in range(len(G_HOPS)):
            for e in range(2):
                wait(gland(e)(i, k), gzs.at[e, k, i])
    piece = fin.at[0, 0]

    @pl.when(active)
    def _():
        for k in range(2):
            for i in range(len(F_HOPS)):
                if i not in F_LAST:
                    wait(fland(i, k), fzs.at[k, i])
        for j in range(2 * len(F_LAST)):
            for i in f_groups:
                wait(piece, ffs.at[j, i])
        for i in f_groups:

            @pl.when(x * NC + c != i)
            def _():
                wait(piece, fos.at[i])

    for i in g_groups:
        wait(piece, fns.at[i])

        @pl.when(jnp.logical_or(jnp.logical_not(active), x * NC + c != i))
        def _():
            wait(piece, fos.at[i])

    def collect(slots):
        for x0 in range(NX):
            for k in range(slots):
                wait(fin.at[x0, k], finr.at[x0, k])
            total = fin[x0, 0]
            for k in range(1, slots):
                total = total + fin[x0, k]
            out[:, x0 * ROWS : (x0 + 1) * ROWS, :] = total.astype(jnp.bfloat16)

    @pl.when(x * NC + c < FIRST // BLOCKS)
    def _():
        collect(1 + 2 * len(F_LAST))

    @pl.when(x * NC + c >= FIRST // BLOCKS)
    def _():
        collect(4)


def body(amplitudes, vectors, pair_count, tile_map):
    live = lax.broadcasted_iota(jnp.int32, (BLOCKS, 1, SLOTS), 2) < pair_count[:, None, None]
    f32, bf16 = jnp.float32, jnp.bfloat16
    dma = pltpu.SemaphoreType.DMA
    slots = max(4, 1 + 2 * len(F_LAST))
    out = pl.pallas_call(
        kernel,
        out_shape=jax.ShapeDtypeStruct(amplitudes.shape, bf16),
        in_specs=[
            pl.BlockSpec(memory_space=pl.ANY),
            pl.BlockSpec(memory_space=pl.ANY),
            pl.BlockSpec(memory_space=pltpu.SMEM),
            pl.BlockSpec(memory_space=pl.ANY),
        ],
        out_specs=pl.BlockSpec(memory_space=pltpu.VMEM),
        scratch_shapes=[
            pltpu.VMEM(amplitudes.shape, bf16),
            pltpu.VMEM(tile_map.shape[::-1], jnp.int32),
            pltpu.VMEM((TOTAL, 2 * TOTAL), bf16),
            pltpu.VMEM((NZ, GROUP, DEPTH, SLOTS), bf16),
            pltpu.VMEM((2, NZ, GROUP, ROWS, SLOTS), bf16),
            pltpu.VMEM(((2 * ROWS + 1) * PITCH, SLOTS), f32),
            pltpu.VMEM((9 * PITCH, SLOTS), f32),
            pltpu.VMEM(((2 * ROWS + 1) * PITCH, SLOTS), f32),
            pltpu.VMEM((9 * PITCH, SLOTS), f32),
            pltpu.VMEM((2, NZ, GROUP, ROWS, SLOTS), f32),
            pltpu.VMEM((2, 2, 4, REST, ROWS, SLOTS), f32),
            pltpu.VMEM((2, 4, FIRST, ROWS, SLOTS), f32),
            pltpu.VMEM((NZ, FIRST // 2, ROWS, SLOTS), f32),
            pltpu.VMEM((2, NZ, FIRST, ROWS, SLOTS), f32),
            pltpu.VMEM((NX, slots, BLOCKS, ROWS, SLOTS), f32),
            dma((NZ,)), dma((NZ,)),
            dma((6, NZ)), dma((6, NZ)),
            dma((4, NZ)), dma((4, NZ)),
            dma((NX,)), dma((NX, NC)),
            dma((NZ + 1,)), dma((NZ,)),
            dma((2, NZ)), dma((NZ,)), dma((3, NZ)),
            dma((2, 2, 4)), dma((2, 2, 4)),
            dma((2, 4)), dma((2, 4)),
            dma((2, NZ)), dma((NZ,)),
            dma((NZ,)), dma((2, NZ)),
            dma((2 * len(F_LAST), NX * NC)), dma((NX * NC,)), dma((NX * NC,)),
            dma((NX, slots)),
            dma((2,)),
        ],
        compiler_params=pltpu.CompilerParams(
            collective_id=0, has_side_effects=True, vmem_limit_bytes=60 * 2**20
        ),
        cost_estimate=pl.CostEstimate(flops=12 * 10**9, bytes_accessed=4 * 10**6, transcendentals=0),
    )(amplitudes, vectors, pair_count, tile_map.T)
    return jnp.where(live, out, jnp.zeros_like(out))


def solution(mesh):
    fine = Mesh(mesh.devices.reshape(NZ, NX, NC, NY), ("z", "x", "c", "y"))
    pair = ("z", "x", "c")
    return jax.shard_map(
        body,
        mesh=fine,
        in_specs=(P(pair, "y", None), P(pair, "y", None), P(pair), P()),
        out_specs=P(pair, "y", None),
        check_vma=False,
    )
```

```python
import jax
import jax.numpy as jnp
from jax import lax
from jax.experimental import pallas as pl
from jax.experimental.pallas import tpu as pltpu
from jax.sharding import Mesh, PartitionSpec as P

NZ, NX, NC, NY = 8, 4, 2, 4
BLOCKS = 4
GROUP = NX * NC * BLOCKS
TOTAL = NZ * GROUP
SLOTS = 128
DEPTH = 160
ROWS = 16
PITCH = TOTAL + 8
FOLD = SLOTS // (DEPTH - SLOTS)
AHEAD = 3
FIRST = 20
REST = GROUP - FIRST
G_HOPS = ((4, 2), (3, 2), (2, 1), (1, 0))
F_HOPS = ((4, 2), (3, 2), (2, 0), (1, 0))
F_LAST = tuple(i for i, (_, d) in enumerate(F_HOPS) if d == 0)
ORDER = (
    ("R", 0), ("g", 0, 0, 0), ("g", 0, 1, 0), ("g", 1, 0, 0), ("g", 1, 1, 0), ("y1", 0),
    ("R", 1), ("g", 0, 0, 1), ("g", 1, 0, 1), ("y1", 1), ("R", 2), ("g", 0, 1, 1),
    ("g", 1, 1, 1), ("y1", 2), ("R", 3), ("y1", 3), ("R", 4), ("y2", 0),
    ("y1", 4), ("R", 5), ("y2", 1), ("y1", 5), ("R", 6), ("y2", 2),
    ("y1", 6), ("R", 7), ("y2", 3), ("f7",), ("g", 0, 0, 2), ("g", 0, 1, 2),
    ("y3", 0), ("f", 0, 0), ("f", 1, 0), ("y2", 4), ("g", 1, 0, 2), ("g", 1, 1, 2),
    ("y3", 1), ("f", 0, 1), ("y2", 5), ("g", 0, 0, 3), ("g", 0, 1, 3), ("y3", 2),
    ("f", 1, 1), ("y2", 6), ("y3", 3), ("g", 1, 0, 3), ("g", 1, 1, 3), ("f", 0, 2),
    ("gr", 0, 1), ("gr", 0, 0), ("y3", 4), ("f", 1, 2), ("gr", 1, 0), ("gr", 1, 1),
    ("gfin",), ("y3", 5), ("f", 0, 3), ("y3", 6), ("f", 1, 3),
)


def split(x):
    hi = x.astype(jnp.bfloat16)
    return hi, (x - hi.astype(jnp.float32)).astype(jnp.bfloat16)


def wait(view, sem):
    pltpu.make_async_copy(view, view, sem).wait()


def kernel(
    amp_in, vec, counts, tiles_in, out,
    amp, tiles, near, vb, ab, w, wt, u, ut, o, gzb, fzb, yhf, yff, fin,
    vzs, vzr, xs, xr, ss, sr, axs, axr, azs, azr, ays, ayf, ayr,
    gzs, gzr, fzs, fzr, yhs, yhr, yfs, yfr, ffs, fos, fns, finr, loads,
):
    z, x, c, y = (lax.axis_index(a) for a in ("z", "x", "c", "y"))

    def mod(a, n):
        return lax.rem(a + 4 * n, n)

    def send(src, dst, ssem, rsem, z1=z, x1=x, c1=c, y1=y):
        pltpu.make_async_remote_copy(
            src_ref=src, dst_ref=dst, send_sem=ssem, recv_sem=rsem,
            device_id=(z1, x1, c1, y1), device_id_type=pl.DeviceIdType.MESH,
        ).start()

    def away_from(s):
        return jnp.where(lax.rem(s, 2) == 1, lax.div(s + 1, 2), -lax.div(s, 2))

    def source(s):
        return mod(z - away_from(s), NZ)

    zp, zm = mod(z + 1, NZ), mod(z - 1, NZ)
    xp, xm, xo = mod(x + 1, NX), mod(x - 1, NX), mod(x + 2, NX)
    yp, ym = mod(y + 1, NY), mod(y - 1, NY)
    mate = 1 - c
    home, edge = lax.div(y, 2), lax.rem(y, 2)
    active = c == home

    def mine(x0, c0):
        return pl.ds(pl.multiple_of(x0 * (NC * BLOCKS) + c0 * BLOCKS, BLOCKS), BLOCKS)

    def part(x0, c0, h):
        return pl.ds(x0 * (NC * BLOCKS) + c0 * BLOCKS + 2 * h, 2)

    def rows(z1):
        return pl.ds(pl.multiple_of(z1 * DEPTH, DEPTH), DEPTH)

    own = pltpu.make_async_copy(vec.at[:, rows(z), :], vb.at[z, mine(x, c)], vzr.at[z])
    load_amp = pltpu.make_async_copy(amp_in, amp, loads.at[0])
    load_amp.start()
    own.start()
    load_tiles = pltpu.make_async_copy(tiles_in, tiles, loads.at[1])
    load_tiles.start()
    barrier = pltpu.get_barrier_semaphore()
    slot = lax.broadcasted_iota(jnp.int32, (NX * ROWS, SLOTS), 1)

    def greet(z1=z, x1=x, c1=c, y1=y):
        pl.semaphore_signal(barrier, inc=1, device_id=(z1, x1, c1, y1), device_id_type=pl.DeviceIdType.MESH)

    for d in range(1, NZ):
        greet(z1=mod(z + d, NZ))
    for d in range(NX):
        for e in range(NC):
            if d or e:
                greet(x1=mod(x + d, NX), c1=mod(c + e, NC))
    for d in range(1, NY):
        greet(y1=mod(y + d, NY))
    load_amp.wait()
    for b in range(BLOCKS):
        amp[b] = jnp.where(slot < counts[b], amp[b], jnp.zeros_like(amp[b]))
    block_row = lax.broadcasted_iota(jnp.int32, (GROUP, TOTAL), 0)

    load_tiles.wait()

    def adjacency(n, carry):
        block_of = block_row + source(n) * GROUP
        found = jnp.zeros((GROUP, TOTAL), jnp.float32)
        for j in range(tiles.shape[0]):
            found = found + jnp.where(tiles[j : j + 1, :] == block_of, 1.0, 0.0)
        for h in range(2):
            u[pl.ds(pl.multiple_of(h * TOTAL + n * GROUP, GROUP), GROUP), :] = found[:, h * SLOTS : (h + 1) * SLOTS]
        return carry

    lax.fori_loop(0, NZ, adjacency, 0)
    for h in range(2):
        found = u[h * TOTAL : (h + 1) * TOTAL, :].T.astype(jnp.bfloat16)
        for k in range(4):
            near[h * SLOTS : (h + 1) * SLOTS, k * SLOTS : (k + 1) * SLOTS] = found[:, k // 2 * SLOTS : (k // 2 + 1) * SLOTS]
    pl.semaphore_wait(barrier, NZ - 1 + NX * NC - 1 + NY - 1)

    for d in range(NX):
        x1 = mod(x + d, NX)
        src = amp.at[:, pl.ds(pl.multiple_of(x1 * ROWS, ROWS), ROWS), :]
        dst = ab.at[edge, z, mine(x, c)]
        if d:
            send(src, dst, axs.at[d], axr.at[x, c], x1=x1, c1=home)
        else:

            @pl.when(active)
            def _():
                pltpu.make_async_copy(src, dst, axr.at[x, c]).start()

            @pl.when(c != home)
            def _():
                send(src, dst, axs.at[0], axr.at[x, c], c1=home)

    def hand_out(s):
        z1 = mod(z + away_from(s), NZ)
        send(vec.at[:, rows(z1), :], vb.at[z, mine(x, c)], vzs.at[z1], vzr.at[z], z1=z1)

    around = mod(y - 2 * c, NY)
    near_e, other_e = 1 - lax.rem(around, 2), lax.rem(around, 2)
    behind = jnp.logical_or(around == 0, around == 3)
    side = jnp.where(behind, 1, 0)
    onward, away = jnp.where(behind, yp, ym), jnp.where(behind, ym, yp)

    def amp_half(h):
        return pl.ds(pl.multiple_of(h * (GROUP // 2), GROUP // 2), GROUP // 2)

    def spread_amp(z0):
        block = ab.at[other_e, z0]
        send(block, block, ays.at[0, z0], ayr.at[0, z0], y1=yp)
        send(block, block, ays.at[1, z0], ayr.at[0, z0], y1=ym)

    def products(s, z0, x0, c0):
        for b in range(BLOCKS):
            q = x0 * (NC * BLOCKS) + c0 * BLOCKS + b
            a = jnp.concatenate([ab[0, z0, q], ab[1, z0, q]], axis=0)
            r = lax.dot_general(a, vb[z0, q], (((1,), (1,)), ((), ())), preferred_element_type=jnp.float32)
            w[pl.ds(s * GROUP + q, 2 * ROWS, stride=PITCH), :] = r[:, :SLOTS]
            tail = [r[m * 8 : m * 8 + 8, SLOTS:] for m in range(FOLD)]
            wt[pl.ds(s * GROUP + q, 8, stride=PITCH), :] = jnp.concatenate(tail, axis=1)

    def mix(src, dst, half):
        def some(i, carry):
            at = [pl.multiple_of((2 * i + h) * PITCH, 8) for h in range(2)]
            hi, lo = split(jnp.concatenate([src[pl.ds(a + half * SLOTS, SLOTS), :] for a in at], axis=1))
            pairs = near[:, half * TOTAL : (half + 1) * TOTAL]
            r = jnp.dot(pairs, jnp.concatenate([hi, lo], axis=0), preferred_element_type=jnp.float32)
            for h in range(2):
                to = pl.ds(at[h], TOTAL)
                part_sum = r[:, h * SLOTS : (h + 1) * SLOTS]
                dst[to, :] = dst[to, :] + part_sum if half else part_sum
            return carry

        lax.fori_loop(0, src.shape[0] // PITCH // 2, some, 0, unroll=True)

    def spread(z0):
        block = vb.at[z0, mine(x, c)]
        ha, hb = vb.at[z0, part(x, c, 0)], vb.at[z0, part(x, c, 1)]
        send(ha, ha, xs.at[0, z0], xr.at[0, z0], x1=xp)
        send(hb, hb, xs.at[1, z0], xr.at[1, z0], x1=xm)
        send(hb, hb, xs.at[4, z0], xr.at[4, z0], x1=xp)
        send(ha, ha, xs.at[5, z0], xr.at[5, z0], x1=xm)
        send(block, block, ss.at[0, z0], sr.at[0, z0], c1=mate)

    wait(vb.at[z, mine(x, c)], vzr.at[z])
    spread(z)

    def hand_first():
        for n in range(1, AHEAD + 1):
            hand_out(jnp.int32(n))

    @pl.when(jnp.logical_not(active))
    def _():
        hand_first()

    @pl.when(active)
    def _():
        for x0 in range(NX):
            for c0 in range(NC):
                wait(ab.at[edge, z, mine(x0, c0)], axr.at[x0, c0])
        block = ab.at[edge, z]
        send(block, block, azs.at[z], azr.at[z], z1=zp)
        send(block, block, azs.at[NZ], azr.at[z], z1=zm)
        spread_amp(z)
        hand_first()

    def step(s, carry):
        @pl.when(jnp.logical_and(jnp.logical_and(s >= 1, s < NZ), active))
        def _():
            z0 = source(s)
            block = ab.at[edge, z0]
            wait(block, azr.at[z0])

            @pl.when(s < NZ - 2)
            def _():
                send(block, block, azs.at[z0], azr.at[z0], z1=jnp.where(lax.rem(s, 2) == 1, zp, zm))

            spread_amp(z0)

        @pl.when(jnp.logical_and(s >= 1, s < NZ + 1))
        def _():
            z0 = source(s - 1)
            wait(ab.at[near_e, z0], ayr.at[0, z0])
            half = ab.at[near_e, z0, amp_half(side)]
            send(half, half, ayf.at[z0], ayr.at[1 + side, z0], y1=away)

        @pl.when(jnp.logical_and(s >= 1, s < NZ))
        def _():
            z0 = source(s)
            wait(vb.at[z0, mine(x, c)], vzr.at[z0])

            @pl.when(s < NZ - AHEAD)
            def _():
                hand_out(s + AHEAD)

            spread(z0)

        @pl.when(jnp.logical_and(s >= 1, s < NZ + 1))
        def _():
            z0 = source(s - 1)
            left, right = vb.at[z0, mine(xm, c)], vb.at[z0, mine(xp, c)]
            half = vb.at[z0, part(xm, c, 0)]
            wait(half, xr.at[0, z0])
            send(half, half, xs.at[2, z0], xr.at[2, z0], x1=xp)
            half = vb.at[z0, part(xp, c, 1)]
            wait(half, xr.at[1, z0])
            send(half, half, xs.at[3, z0], xr.at[3, z0], x1=xm)
            wait(vb.at[z0, part(xm, c, 1)], xr.at[4, z0])
            send(left, left, ss.at[1, z0], sr.at[1, z0], c1=mate)
            wait(vb.at[z0, part(xp, c, 0)], xr.at[5, z0])
            send(right, right, ss.at[2, z0], sr.at[2, z0], c1=mate)

        @pl.when(jnp.logical_and(s >= 2, s < NZ + 2))
        def _():
            z0 = source(s - 2)

            wait(vb.at[z0, part(xo, c, 0)], xr.at[2, z0])
            wait(vb.at[z0, part(xo, c, 1)], xr.at[3, z0])
            block = vb.at[z0, mine(xo, c)]
            send(block, block, ss.at[3, z0], sr.at[3, z0], c1=mate)

            @pl.when(jnp.logical_not(active))
            def _():
                for h in range(2):
                    wait(ab.at[other_e, z0, amp_half(h)], ayr.at[1 + h, z0])

            for x0 in (x, xm, xp):
                products(s - 2, z0, x0, c)
            wait(vb.at[z0, mine(x, mate)], sr.at[0, z0])
            products(s - 2, z0, x, mate)
            products(s - 2, z0, xo, c)
            for k, x0 in ((1, xm), (2, xp)):
                wait(vb.at[z0, mine(x0, mate)], sr.at[k, z0])
                products(s - 2, z0, x0, mate)

        @pl.when(s >= 3)
        def _():
            z0 = source(s - 3)
            wait(vb.at[z0, mine(xo, mate)], sr.at[3, z0])
            products(s - 3, z0, xo, mate)

        @pl.when(s == NZ - 1)
        def _():
            mix(w, u, 0)
            mix(wt, ut, 0)

        return carry

    lax.fori_loop(0, NZ + 3, step, 0)

    mix(w, u, 1)
    mix(wt, ut, 1)
    row = lax.broadcasted_iota(jnp.int32, (2 * ROWS, SLOTS), 0)
    lane = lax.broadcasted_iota(jnp.int32, (2 * ROWS, SLOTS), 1)
    own_fold = lax.div(row, 8) == lax.div(lane, DEPTH - SLOTS)

    def residuals(zt):
        def some(n, carry):
            for step_in in range(4):
                p = n * 4 + step_in
                full = u[pl.ds(zt * GROUP + p, 2 * ROWS, stride=PITCH), :]
                tail = jnp.concatenate([ut[pl.ds(zt * GROUP + p, 8, stride=PITCH), :]] * FOLD, axis=0)
                u2 = jnp.concatenate([full, jnp.where(own_fold, tail, 0.0)], axis=1)
                left = jnp.concatenate(split(u2), axis=0)
                right = jnp.concatenate([vb[zt, p, :SLOTS, :]] + [vb[zt, p, SLOTS:, :]] * FOLD, axis=0)
                r = jnp.dot(left, right, preferred_element_type=jnp.float32)
                r = r[: 2 * ROWS] + r[2 * ROWS :]
                o[0, zt, p] = r[:ROWS]
                o[1, zt, p] = r[ROWS:]
            return carry

        lax.fori_loop(0, GROUP // 4, some, 0, unroll=2)

    def y1(n, zt):
        @pl.when(jnp.logical_not(active))
        def _():
            for h, y1_ in enumerate((ym, yp)):
                half = o.at[other_e, zt, pl.ds(h * (FIRST // 2), FIRST // 2)]
                send(half, yhf.at[n], yhs.at[h, n], yhr.at[n], y1=y1_)

    def y2(n, zt):
        wait(yhf.at[n], yhr.at[n])
        at = pl.ds(side * (FIRST // 2), FIRST // 2)
        o[near_e, zt, at] = o[near_e, zt, at] + yhf[n]
        send(o.at[near_e, zt, pl.ds(0, FIRST)], yff.at[side, n], yfs.at[n], yfr.at[side, n], y1=onward)

    def y3(n, zt):
        @pl.when(active)
        def _():
            for k in range(2):
                wait(yff.at[k, n], yfr.at[k, n])
            at = pl.ds(0, FIRST)
            o[other_e, zt, at] = o[other_e, zt, at] + (yff[0, n] + yff[1, n])

    def gview(e):
        def view(zt, far, k):
            return o.at[e, zt, pl.ds(FIRST + k * (REST // 2), REST // 2)] if far else o.at[e, zt, pl.ds(FIRST, REST)]

        return view

    def fview(zt, far, k):
        return o.at[other_e, zt, pl.ds(k * (FIRST // 2), FIRST // 2)] if far else o.at[other_e, zt, pl.ds(0, FIRST)]

    def gland(e):
        def land(i, k):
            return gzb.at[e, k, i, pl.ds(0, REST // 2)] if G_HOPS[i][0] == 4 else gzb.at[e, k, i]

        return land

    def fland(i, k):
        return fzb.at[k, i, pl.ds(0, FIRST // 2)] if F_HOPS[i][0] == 4 else fzb.at[k, i]

    def ahead(k, d):
        return mod(z + d, NZ) if k == 0 else mod(z - d, NZ)

    def ztake(view, land, rsem, hops, k, dist):
        for i, (far, d) in enumerate(hops):
            if d == dist:
                wait(land(i, k), rsem.at[k, i])
                into = view(ahead(k, d), far == 4, k)
                into[...] = into[...] + land(i, k)[...]

    def zpass(view, land, ssem, rsem, hops, k, i):
        far, d = hops[i]
        ztake(view, land, rsem, hops, k, far)
        send(view(ahead(k, far), far == 4, k), land(i, k), ssem.at[k, i], rsem.at[k, i], z1=ahead(k, far - d))

    def deliver(src, zt, slot_to, ssem, groups, z1, y1, local):
        for i in groups:
            x1, c1 = i // NC, i % NC
            piece = src.at[zt, pl.ds(i * BLOCKS, BLOCKS)]
            dst, rsem = fin.at[x, slot_to], finr.at[x, slot_to]
            if local:

                @pl.when(x * NC + c == i)
                def _():
                    pltpu.make_async_copy(piece, dst, rsem).start()

                @pl.when(x * NC + c != i)
                def _():
                    send(piece, dst, ssem.at[i], rsem, z1=z1, x1=x1, c1=c1, y1=y1)
            else:
                send(piece, dst, ssem.at[i], rsem, z1=z1, x1=x1, c1=c1, y1=y1)

    f_groups, g_groups = range(FIRST // BLOCKS), range(FIRST // BLOCKS, NX * NC)

    def f_pass(k, i):
        @pl.when(active)
        def _():
            far, d = F_HOPS[i]
            if d:
                zpass(fview, fland, fzs, fzr, F_HOPS, k, i)
            else:
                ztake(fview, fland, fzr, F_HOPS, k, far)
                j = k * len(F_LAST) + F_LAST.index(i)
                deliver(o.at[other_e], ahead(k, far), 1 + j, ffs.at[j], f_groups, ahead(k, far), y, False)

    def last(groups, base):
        deliver(o.at[near_e], z, base + side, fns, groups, z, onward, False)

        @pl.when(active)
        def _():
            deliver(o.at[other_e], z, 0, fos, groups, z, y, True)

        @pl.when(jnp.logical_not(active))
        def _():
            deliver(o.at[other_e], z, base + 2, fos, groups, z, mod(y + 2, NY), False)

    def sent(n):
        z0 = mod(z + n, NZ)
        block, half = vb.at[z0, mine(x, c)], vb.at[z0, part(x, c, 0)]
        for k in range(6):
            wait(half, xs.at[k, z0])
        for k in range(4):
            wait(block, ss.at[k, z0])

        if n > 0:
            wait(block, vzs.at[z0])

        wait(ab.at[edge, z0, amp_half(0)], ayf.at[z0])

        @pl.when(active)
        def _():
            for k in range(2):
                wait(ab.at[edge, z0], ays.at[k, z0])

    def sent_first():
        piece = amp.at[:, pl.ds(0, ROWS), :]
        for d in range(1, NX):
            wait(piece, axs.at[d])

        @pl.when(c != home)
        def _():
            wait(piece, axs.at[0])


        @pl.when(active)
        def _():
            wait(ab.at[edge, z], azs.at[NZ])
            for d in (0, 1, -1, 2, -2, 3):
                wait(ab.at[edge, z], azs.at[mod(z - d, NZ)])

    chunk = [mod(z + d, NZ) for d in (4, 3, -3, 2, -2, 1, -1, 0)]

    def run(name, *a):
        if name == "R":
            residuals(chunk[a[0]])
            sent(a[0])
        elif name == "y1":
            y1(a[0], chunk[a[0]])
        elif name == "y2":
            y2(a[0], chunk[a[0]])
        elif name == "y3":
            y3(a[0], chunk[a[0]])
        elif name == "g":
            e, k, i = a
            zpass(gview(e), gland(e), gzs.at[e], gzr.at[e], G_HOPS, k, i)
        elif name == "gr":
            e, k = a
            ztake(gview(e), gland(e), gzr.at[e], G_HOPS, k, 0)
        elif name == "gfin":
            last(g_groups, 1)
        elif name == "f":
            f_pass(*a)
        elif name == "f7":
            last(f_groups, 1 + 2 * len(F_LAST))

    for name, *a in ORDER:
        run(name, *a)
    sent_first()

    for n in range(NZ - 1):

        @pl.when(jnp.logical_not(active))
        def _():
            wait(yhf.at[n], yhs.at[0, n])
            wait(yhf.at[n], yhs.at[1, n])

        wait(yff.at[0, n], yfs.at[n])
    for k in range(2):
        for i in range(len(G_HOPS)):
            for e in range(2):
                wait(gland(e)(i, k), gzs.at[e, k, i])
    piece = fin.at[0, 0]

    @pl.when(active)
    def _():
        for k in range(2):
            for i in range(len(F_HOPS)):
                if i not in F_LAST:
                    wait(fland(i, k), fzs.at[k, i])
        for j in range(2 * len(F_LAST)):
            for i in f_groups:
                wait(piece, ffs.at[j, i])

    for i in range(NX * NC):
        wait(piece, fns.at[i])

        @pl.when(jnp.logical_or(jnp.logical_not(active), x * NC + c != i))
        def _():
            wait(piece, fos.at[i])

    def collect(slots):
        for x0 in range(NX):
            for k in range(slots):
                wait(fin.at[x0, k], finr.at[x0, k])
            total = fin[x0, 0]
            for k in range(1, slots):
                total = total + fin[x0, k]
            out[:, x0 * ROWS : (x0 + 1) * ROWS, :] = total.astype(jnp.bfloat16)

    @pl.when(x * NC + c < FIRST // BLOCKS)
    def _():
        collect(4 + 2 * len(F_LAST))

    @pl.when(x * NC + c >= FIRST // BLOCKS)
    def _():
        collect(4)


def body(amplitudes, vectors, pair_count, tile_map):
    live = lax.broadcasted_iota(jnp.int32, (BLOCKS, 1, SLOTS), 2) < pair_count[:, None, None]
    f32, bf16 = jnp.float32, jnp.bfloat16
    dma = pltpu.SemaphoreType.DMA
    slots = 4 + 2 * len(F_LAST)
    out = pl.pallas_call(
        kernel,
        out_shape=jax.ShapeDtypeStruct(amplitudes.shape, bf16),
        in_specs=[
            pl.BlockSpec(memory_space=pl.ANY),
            pl.BlockSpec(memory_space=pl.ANY),
            pl.BlockSpec(memory_space=pltpu.SMEM),
            pl.BlockSpec(memory_space=pl.ANY),
        ],
        out_specs=pl.BlockSpec(memory_space=pltpu.VMEM),
        scratch_shapes=[
            pltpu.VMEM(amplitudes.shape, bf16),
            pltpu.VMEM(tile_map.shape[::-1], jnp.int32),
            pltpu.VMEM((TOTAL, 2 * TOTAL), bf16),
            pltpu.VMEM((NZ, GROUP, DEPTH, SLOTS), bf16),
            pltpu.VMEM((2, NZ, GROUP, ROWS, SLOTS), bf16),
            pltpu.VMEM(((2 * ROWS + 1) * PITCH, SLOTS), f32),
            pltpu.VMEM((9 * PITCH, SLOTS), f32),
            pltpu.VMEM(((2 * ROWS + 1) * PITCH, SLOTS), f32),
            pltpu.VMEM((9 * PITCH, SLOTS), f32),
            pltpu.VMEM((2, NZ, GROUP, ROWS, SLOTS), f32),
            pltpu.VMEM((2, 2, 4, REST, ROWS, SLOTS), f32),
            pltpu.VMEM((2, 4, FIRST, ROWS, SLOTS), f32),
            pltpu.VMEM((NZ - 1, FIRST // 2, ROWS, SLOTS), f32),
            pltpu.VMEM((2, NZ - 1, FIRST, ROWS, SLOTS), f32),
            pltpu.VMEM((NX, slots, BLOCKS, ROWS, SLOTS), f32),
            dma((NZ,)), dma((NZ,)),
            dma((6, NZ)), dma((6, NZ)),
            dma((4, NZ)), dma((4, NZ)),
            dma((NX,)), dma((NX, NC)),
            dma((NZ + 1,)), dma((NZ,)),
            dma((2, NZ)), dma((NZ,)), dma((3, NZ)),
            dma((2, 2, 4)), dma((2, 2, 4)),
            dma((2, 4)), dma((2, 4)),
            dma((2, NZ - 1)), dma((NZ - 1,)),
            dma((NZ - 1,)), dma((2, NZ - 1)),
            dma((2 * len(F_LAST), NX * NC)), dma((NX * NC,)), dma((NX * NC,)),
            dma((NX, slots)),
            dma((2,)),
        ],
        compiler_params=pltpu.CompilerParams(
            collective_id=0, has_side_effects=True, vmem_limit_bytes=60 * 2**20
        ),
        cost_estimate=pl.CostEstimate(flops=12 * 10**9, bytes_accessed=4 * 10**6, transcendentals=0),
    )(amplitudes, vectors, pair_count, tile_map.T)
    return jnp.where(live, out, jnp.zeros_like(out))


def solution(mesh):
    fine = Mesh(mesh.devices.reshape(NZ, NX, NC, NY), ("z", "x", "c", "y"))
    pair = ("z", "x", "c")
    return jax.shard_map(
        body,
        mesh=fine,
        in_specs=(P(pair, "y", None), P(pair, "y", None), P(pair), P()),
        out_specs=P(pair, "y", None),
        check_vma=False,
    )
```
